128 devices in a mesh: dp: 32 (over y_hi, x, z), seq: 4 (over y_lo, core).
Axes of the slice: x: 4, y: 4 (y_hi: 2, y_lo: 2; y = y_hi * 2 + y_lo), z: 4, core: 2. Of those that a mesh axis runs over, the one named last changes fastest.
Arguments:
- layer_in: bfloat16 [16384, 1024], P(('dp', 'seq')), may hold values from -6 to 6
- norm_one: bfloat16 [1024], P('dp'), may hold values from 0.099609375 to 1.8984375
- w_query: bfloat16 [1024, 1024], P('dp'), may hold values from -0.625 to 0.625
- key_weight: bfloat16 [1024, 512], P('dp'), may hold values from -0.625 to 0.625
- value_weight: bfloat16 [1024, 512], P('dp'), may hold values from -0.1875 to 0.1875
- w_output: bfloat16 [1024, 1024], P('dp'), may hold values from -4 to 4
- norm_two: bfloat16 [1024], P('dp'), may hold values from 0.099609375 to 1.8984375
- w_gate: bfloat16 [1024, 16, 512], P('dp'), may hold values from -0.1875 to 0.1875
- w_up: bfloat16 [1024, 16, 512], P('dp'), may hold values from -0.1875 to 0.1875
- w_down: bfloat16 [1024, 16, 512], P('dp'), may hold values from -1 to 1
- routes: int32 [16384, 8], P(('dp', 'seq')), may hold values from 0 to 15, all different within a row; in each aligned block of 128 rows (0 to 127, 128 to 255, ...) at most 72 rows name the same one
- route_gates: float32 [16384, 8], P(('dp', 'seq')), may hold values from 0.5 to 1.5
- cotangent: bfloat16 [16384, 1024], P(('dp', 'seq')), may hold values from -6 to 6
Outputs:
- layer_out: bfloat16 [16384, 1024], P(('dp', 'seq'))
- grad_input: bfloat16 [16384, 1024], P(('dp', 'seq'))
- grad_norm_one: float32 [1024], P('dp')
- grad_query_proj: float32 [1024, 1024], P('dp')
- grad_key_proj: float32 [1024, 512], P('dp')
- grad_value_proj: float32 [1024, 512], P('dp')
- grad_output_proj: float32 [1024, 1024], P('dp')
- grad_norm_two: float32 [1024], P('dp')
- grad_gate_proj: float32 [1024, 16, 512], P('dp')
- grad_up_proj: float32 [1024, 16, 512], P('dp')
- grad_down_proj: float32 [1024, 16, 512], P('dp')
- grad_gates: float32 [16384, 8], P(('dp', 'seq'))
The draws below stay inside these ranges and needn't reach their ends.
Inputs may be any that keep to these rules, and one draw needn't show every extreme that they name: `routes`: each row names 8 different experts. In the 128 rows of one device no expert is named by more than 72 rows, a bound that some block reaches of some device in every draw.
All inputs are finite; a program needn't handle non-finite values.
Results may differ from the reference program's by a relative error of at most 0.03.
Values may be sent and summed in bfloat16 or wider, within the bound.
A program may use at most 256 MiB of HBM per device.

```python
import math
import jax
import jax.numpy as jnp
import numpy as np
from jax import lax

MODEL_WIDTH = 1024
QUERY_HEADS = 16
KEY_VALUE_HEADS = 8
HEAD_SIZE = 64
FF = 512
TOP = 8
EXPERTS = 16
SEQ_LEN = 512
TOK_DEV = 128
TOKENS = 16384
CAP = 72
N_DP = 32
N_SEQ = 4


def block_levels(own_key, extent, shards, smallest, largest):
    level, own = 1.0, jax.random.fold_in(own_key, 6)
    for position, blocks in shards:
        draws = jnp.exp(jax.random.uniform(jax.random.fold_in(own, position), (blocks,), jnp.float32, smallest / len(shards), largest / len(shards)))
        level = level * jnp.repeat(draws, extent[position] // blocks).reshape([-1 if axis == position else 1 for axis in range(len(extent))])
    return level


def assign_block(stream_key, own, number, rows, number_of, top, reach, slope):
    ranking = jax.random.permutation(stream_key, number_of)
    packed, common = shares(number_of, rows * top, reach, slope, True), shares(number_of, rows * top, reach, slope, False)
    places = jnp.arange(number_of)

    def named(tallies, rotation):
        used = int((tallies > 0).sum())
        fixed = max(1, used // 4)
        shifted = fixed + (places - fixed + rotation * (used - fixed)) % max(1, number_of - fixed)
        return jnp.zeros((number_of,), jnp.int32).at[ranking[jnp.where(places < fixed, places, shifted)]].set(jnp.asarray(tallies, jnp.int32))

    tallies = jnp.where(number % 4 == 0, named(packed, number // 4), named(common, number - number // 4 - 1))
    mixed = jax.random.permutation(jax.random.fold_in(own, 3), number_of)
    donor, sink = mixed[0:number_of // 2 * 2:2], mixed[1:number_of // 2 * 2:2]
    room = jnp.minimum(tallies[donor] - 1, reach - tallies[sink]) // 2
    room = jnp.where((donor == ranking[0]) | (sink == ranking[0]) | (tallies[sink] == 0), 0, jnp.maximum(room, 0))
    shifted = jax.random.randint(jax.random.fold_in(own, 4), (number_of // 2,), 0, 1 << 20) % (room + 1)
    tallies = tallies.at[donor].add(-shifted).at[sink].add(shifted)
    labels = jnp.searchsorted(jnp.cumsum(tallies), jnp.arange(rows * top), side="right").astype(jnp.int32)
    table = labels.reshape(top, rows).T
    table = table[jax.random.permutation(jax.random.fold_in(own, 1), rows)]
    rotation = jax.random.randint(jax.random.fold_in(own, 2), (rows, 1), 0, top)
    return jnp.take_along_axis(table, (jnp.arange(top)[None, :] + rotation) % top, axis=1)


def shares(amount, total, most, slope, full):
    weights = [(1 << 20) // math.isqrt(rank ** slope) + 1 for rank in range(1, amount + 1)]
    largest = most if full else min(most, max(-(-total // amount), total * weights[0] // sum(weights)))
    least = 1 if total - largest >= amount - 1 else 0
    given, spare = [largest] + [least] * (amount - 1), total - largest - least * (amount - 1)
    while spare > 0:
        free = [i for i in range(1, amount) if given[i] < largest] or [i for i in range(1, amount) if given[i] < most]
        whole, left = sum([weights[i] for i in free]), spare
        for i in free:
            extra = min(most - given[i], max(1, left * weights[i] // whole), spare)
            given[i] = given[i] + extra
            spare = spare - extra
    return np.array(given)


def centred(own_key, extent, deviation, limit, split=(), kind=jnp.bfloat16):
    values = deviation * jax.random.normal(own_key, extent, jnp.float32)
    if split:
        values = values * block_levels(own_key, extent, split, -0.22, 0.18)
    return jnp.clip(values, -limit, limit).astype(kind)


def setup_inputs(seed: int = 0) -> dict:
    key_list = jax.random.split(jax.random.key(seed), 14)
    layer_in = centred(key_list[0], (TOKENS, MODEL_WIDTH), 1.0, 6.0, ((0, 128),))
    norm_one = jnp.clip(1.0 + 0.18 * jax.random.normal(key_list[1], (MODEL_WIDTH,), jnp.float32), 0.099609375, 1.8984375).astype(jnp.bfloat16)
    w_query = centred(key_list[2], (MODEL_WIDTH, QUERY_HEADS * HEAD_SIZE), (MODEL_WIDTH // 12) ** -0.5, 0.625, ((0, 32),))
    key_weight = centred(key_list[3], (MODEL_WIDTH, KEY_VALUE_HEADS * HEAD_SIZE), (MODEL_WIDTH // 12) ** -0.5, 0.625, ((0, 32),))
    value_weight = centred(key_list[4], (MODEL_WIDTH, KEY_VALUE_HEADS * HEAD_SIZE), MODEL_WIDTH ** -0.5, 0.1875, ((0, 32),))
    w_output = centred(key_list[5], (QUERY_HEADS * HEAD_SIZE, MODEL_WIDTH), 2 ** -0.5, 4.0, ((0, 32),))
    norm_two = jnp.clip(1.0 + 0.18 * jax.random.normal(key_list[6], (MODEL_WIDTH,), jnp.float32), 0.099609375, 1.8984375).astype(jnp.bfloat16)
    w_gate = centred(key_list[7], (MODEL_WIDTH, EXPERTS, FF), MODEL_WIDTH ** -0.5, 0.1875, ((0, 32),))
    w_up = centred(key_list[8], (MODEL_WIDTH, EXPERTS, FF), MODEL_WIDTH ** -0.5, 0.1875, ((0, 32),))
    w_down = centred(key_list[9], (MODEL_WIDTH, EXPERTS, FF), (FF // 12) ** -0.5, 1.0, ((0, 32),))
    routes_keys = jax.random.split(jax.random.fold_in(key_list[10], 1), TOKENS // TOK_DEV)
    routes_turns = jax.random.permutation(jax.random.fold_in(key_list[10], 3), TOKENS // TOK_DEV)
    routes = jax.vmap(lambda own, number: assign_block(jax.random.fold_in(key_list[10], 2), own, number, TOK_DEV, EXPERTS, TOP, CAP, 1))(routes_keys, routes_turns).reshape((TOKENS, TOP))
    route_gates = jnp.clip(0.5 + 1.0 * jax.random.uniform(key_list[11], (TOKENS, TOP), jnp.float32) ** block_levels(key_list[11], (TOKENS, TOP), ((0, 128),), -0.2, 0.2), 0.5, 1.5)
    cotangent = centred(key_list[12], (TOKENS, MODEL_WIDTH), 1.0, 6.0, ((0, 128),))
    return dict(layer_in=layer_in, norm_one=norm_one, w_query=w_query, key_weight=key_weight, value_weight=value_weight, w_output=w_output, norm_two=norm_two, w_gate=w_gate, w_up=w_up, w_down=w_down, routes=routes, route_gates=route_gates, cotangent=cotangent)


EPSILON = 1e-05
RESIDUAL = 0.22
ROPE_BASE = 10000.0
MASK_VALUE = -1e+30
HIGHEST_ACCURACY = lax.Precision.HIGHEST

@jax.custom_vjp
def lower_half(v):
    return lax.optimization_barrier(v.astype(jnp.bfloat16)).astype(jnp.float32)

@jax.custom_vjp
def lower_half_unturned(v):
    return v

def low_keep(v):
    return (lower_half(v), None)

def low_pass(kept, grad):
    return (grad,)

def back_keep(v):
    return (v, None)

def back_low(kept, grad):
    return (lower_half(grad),)
lower_half.defvjp(low_keep, low_pass)
lower_half_unturned.defvjp(back_keep, back_low)

def rms_norm(value_matrix, gain):
    factor = lax.rsqrt(lax.optimization_barrier(jnp.mean(value_matrix * value_matrix, axis=-1, keepdims=True)) + EPSILON)
    return value_matrix * factor * gain

def angles(start, count):
    freqs = ROPE_BASE ** (-jnp.arange(0, HEAD_SIZE, 2).astype(jnp.float32) / HEAD_SIZE)
    places = (start + jnp.arange(count)).astype(jnp.float32)
    turns = places[:, None] * freqs[None, :]
    turns = jnp.concatenate([turns, turns], axis=-1)
    return (jnp.cos(turns)[:, None, :], jnp.sin(turns)[:, None, :])

def apply_rotary(value_matrix, cosine_table, sine_table):
    half_dim = value_matrix.shape[-1] // 2
    turned = jnp.concatenate([-value_matrix[..., half_dim:], value_matrix[..., :half_dim]], axis=-1)
    return value_matrix * cosine_table + turned * sine_table

def slot_tables(routes_block):
    chosen = routes_block.reshape(-1)
    onehot = (chosen[:, None] == jnp.arange(EXPERTS, dtype=jnp.int32)[None, :]).astype(jnp.int32)
    ranks = lax.optimization_barrier(jnp.sum(onehot * (jnp.cumsum(onehot, axis=0) - 1), axis=1)).astype(jnp.int32)
    slots = chosen * CAP + ranks
    serial = jnp.arange(chosen.shape[0], dtype=jnp.int32)
    owners = jnp.zeros((EXPERTS * CAP,), jnp.int32).at[slots].set(serial // TOP)
    return (slots, owners)

def expert_block(normed_rows, routes_block, gate_block, w_gate, w_up, w_down):
    slots, owners = slot_tables(routes_block)
    rows = normed_rows[owners].reshape(EXPERTS, CAP, MODEL_WIDTH)
    gate_pre = lower_half_unturned(jnp.einsum('ecd,def->ecf', rows, w_gate, precision=HIGHEST_ACCURACY))
    up_pre = lower_half_unturned(jnp.einsum('ecd,def->ecf', rows, w_up, precision=HIGHEST_ACCURACY))
    active = lower_half(jax.nn.silu(gate_pre) * up_pre)
    returned = lower_half_unturned(jnp.einsum('ecf,def->ecd', active, w_down, precision=HIGHEST_ACCURACY)).reshape(EXPERTS * CAP, MODEL_WIDTH)
    picked = returned[slots].reshape(routes_block.shape[0], TOP, MODEL_WIDTH)
    return lax.optimization_barrier(jnp.sum(gate_block[:, :, None] * picked, axis=1))

def layer_fwd(inputs, gate_vals, routes_seq, params):
    norm_one, w_query, key_weight, value_weight, w_output, norm_two, w_gate, w_up, w_down = params
    sequence_length = inputs.shape[0]
    cosine_table, sine_table = angles(0, sequence_length)
    normed_input = lower_half(rms_norm(inputs, norm_one))
    query_matrix = lower_half_unturned(jnp.dot(normed_input, w_query, precision=HIGHEST_ACCURACY)).reshape(sequence_length, QUERY_HEADS, HEAD_SIZE)
    query_matrix = lower_half_unturned(lower_half(apply_rotary(query_matrix, cosine_table, sine_table)))
    key_matrix = lower_half_unturned(jnp.dot(normed_input, key_weight, precision=HIGHEST_ACCURACY)).reshape(sequence_length, KEY_VALUE_HEADS, HEAD_SIZE)
    key_matrix = lower_half_unturned(lower_half(apply_rotary(key_matrix, cosine_table, sine_table)))
    value_matrix = lower_half_unturned(lower_half(jnp.dot(normed_input, value_weight, precision=HIGHEST_ACCURACY))).reshape(sequence_length, KEY_VALUE_HEADS, HEAD_SIZE)
    grouped_heads = query_matrix.reshape(sequence_length, KEY_VALUE_HEADS, QUERY_HEADS // KEY_VALUE_HEADS, HEAD_SIZE)
    scores = jnp.einsum('qkgd,skd->kgqs', grouped_heads, key_matrix, precision=HIGHEST_ACCURACY) / HEAD_SIZE
    causal = jnp.arange(sequence_length)[:, None] >= jnp.arange(sequence_length)[None, :]
    scores = lower_half_unturned(jnp.where(causal, scores, MASK_VALUE))
    top_score = lax.optimization_barrier(jnp.max(scores, axis=-1, keepdims=True))
    exponent = jnp.exp(scores - top_score)
    probs = lower_half(exponent / lax.optimization_barrier(jnp.sum(exponent, axis=-1, keepdims=True)))
    attended = jnp.einsum('kgqs,skd->qkgd', probs, value_matrix, precision=HIGHEST_ACCURACY).reshape(sequence_length, QUERY_HEADS * HEAD_SIZE)
    attended = lower_half_unturned(lower_half(attended))
    branch = lower_half_unturned(jnp.dot(attended, w_output, precision=HIGHEST_ACCURACY))
    middle = inputs + RESIDUAL * branch
    normed_two = lower_half(rms_norm(middle, norm_two))
    mixed = []
    for part_index in range(N_SEQ):
        first = part_index * TOK_DEV
        mixed.append(expert_block(normed_two[first:first + TOK_DEV], routes_seq[first:first + TOK_DEV], gate_vals[first:first + TOK_DEV], w_gate, w_up, w_down))
    return middle + RESIDUAL * jnp.concatenate(mixed, axis=0)

def reference(layer_in, norm_one, w_query, key_weight, value_weight, w_output, norm_two, w_gate, w_up, w_down, routes, route_gates, cotangent):
    params = tuple((tensor.astype(jnp.float32) for tensor in (norm_one, w_query, key_weight, value_weight, w_output, norm_two, w_gate, w_up, w_down)))
    inputs = layer_in.astype(jnp.float32).reshape(N_DP, SEQ_LEN, MODEL_WIDTH)
    route_seqs = routes.reshape(N_DP, SEQ_LEN, TOP)
    gate_seqs = route_gates.astype(jnp.float32).reshape(N_DP, SEQ_LEN, TOP)
    cot_seqs = cotangent.astype(jnp.float32).reshape(N_DP, SEQ_LEN, MODEL_WIDTH)

    def per_sequence(running, items):
        seq_in, seq_routes, seq_gates, seq_cot = items

        def forward(values_in, gate_vals, weights):
            return layer_fwd(values_in, gate_vals, seq_routes, weights)
        result, pullback = jax.vjp(forward, seq_in, seq_gates, params)
        grad_in, grad_gate_vals, grad_params = pullback(seq_cot)
        running = tuple((before + gradient for before, gradient in zip(running, grad_params)))
        return (running, (result.astype(jnp.bfloat16), grad_in.astype(jnp.bfloat16), grad_gate_vals))
    zeros_init = tuple((jnp.zeros_like(tensor) for tensor in params))
    totals, (outputs, grad_inputs, grad_gate_all) = lax.scan(per_sequence, zeros_init, (inputs, route_seqs, gate_seqs, cot_seqs))
    return (outputs.reshape(TOKENS, MODEL_WIDTH), grad_inputs.reshape(TOKENS, MODEL_WIDTH), totals[0], totals[1], totals[2], totals[3], totals[4], totals[5], totals[6], totals[7], totals[8], grad_gate_all.reshape(TOKENS, TOP))
```

```python
import jax
import jax.numpy as jnp
from jax import lax
from jax.experimental import pallas as pl
from jax.experimental.pallas import tpu as pltpu
from jax.sharding import Mesh
from jax.sharding import PartitionSpec as P

MODEL_WIDTH = 1024
QUERY_HEADS = 16
KEY_VALUE_HEADS = 8
HEAD_SIZE = 64
TOP = 8
EXPERTS = 16
CAP = 72
SLOTS = EXPERTS * CAP
TOK = 128
SEQ_LEN = 512
FF = 512
EPSILON = 1e-05
RESIDUAL = 0.22
ROPE_BASE = 10000.0
MASK_VALUE = -1e30

BF16 = jnp.bfloat16
F32 = jnp.float32
AXES = ("yh", "x", "z", "seq")
BY_ID = pl.DeviceIdType.MESH


def place():
    return tuple(lax.axis_index(axis) for axis in AXES)


class Sender:
    def __init__(self, send, recv):
        self.send, self.recv, self.used, self.copies = send, recv, 0, []

    def start(self, source, target, device):
        copy = pltpu.make_async_remote_copy(
            src_ref=source,
            dst_ref=target,
            send_sem=self.send.at[self.used],
            recv_sem=self.recv.at[self.used],
            device_id=device,
            device_id_type=BY_ID,
        )
        copy.start()
        self.used += 1
        self.copies.append(copy)
        return copy

    def finish(self):
        for copy in self.copies:
            copy.wait_send()


def arrived(copies):
    for copy in copies:
        copy.wait_recv()


def greet(partners):
    barrier = pltpu.get_barrier_semaphore()
    for partner in partners:
        pl.semaphore_signal(barrier, inc=1, device_id=partner, device_id_type=BY_ID)
    pl.semaphore_wait(barrier, len(partners))


def remote_call(kernel, inputs, outputs, copies, local_copies, collective_id, name):
    return pl.pallas_call(
        kernel,
        out_shape=tuple(jax.ShapeDtypeStruct(shape, BF16) for shape in outputs),
        in_specs=[pl.BlockSpec(memory_space=pl.ANY)] * len(inputs),
        out_specs=tuple(pl.BlockSpec(memory_space=pl.ANY) for _ in outputs),
        scratch_shapes=[
            pltpu.SemaphoreType.DMA((copies,)),
            pltpu.SemaphoreType.DMA((copies,)),
            pltpu.SemaphoreType.DMA((local_copies,)),
        ],
        compiler_params=pltpu.CompilerParams(collective_id=collective_id, has_side_effects=True),
        name=name,
    )(*inputs)


def local_starts(pairs, sems):
    copies = []
    for index, (source, target) in enumerate(pairs):
        copy = pltpu.make_async_copy(source, target, sems.at[index])
        copy.start()
        copies.append(copy)
    return copies


def gather_kernel(
    heads, branch, tokens, experts, rows,
    heads_all, branch_all, tokens_all, experts_all, rows_all,
    send, recv, local,
):
    yh, x, z, seq = place()
    yl, core = seq // 2, seq % 2
    along_y = (1 - yh, x, z, seq)
    along_x = [(yh, (x + k) % 4, z, seq) for k in (1, 2, 3)]
    along_z = [(yh, x, (z + k) % 4, seq) for k in (1, 2, 3)]
    group = [
        (yh, x, (z + k // 4) % 4, (yl + (k // 2) % 2) % 2 * 2 + (core + k % 2) % 2)
        for k in range(1, 16)
    ]
    near = (yh, x, z, (1 - yl) * 2 + core)
    sibling = (yh, x, z, yl * 2 + 1 - core)
    expert = z * 4 + seq
    greet([along_y] + along_x + group)
    own = local_starts(
        [
            (heads, heads_all.at[yh, x, z]),
            (branch, branch_all.at[core, yh, x, z]),
            (tokens, tokens_all.at[yl, core]),
            (experts.at[z], experts_all.at[:, yh, x, z]),
            (rows.at[expert], rows_all.at[expert]),
        ],
        local,
    )
    sender = Sender(send, recv)
    first = [
        sender.start(heads, heads_all.at[yh, x, z], along_y),
        sender.start(branch, branch_all.at[core, yh, x, z], along_y),
    ]
    expert_first = [
        sender.start(experts.at[(z + k) % 4], experts_all.at[:, yh, x, z], along_z[k - 1])
        for k in (1, 2, 3)
    ]
    token_copies = [
        sender.start(tokens, tokens_all.at[yl, core], near),
        sender.start(tokens, tokens_all.at[yl, core], sibling),
    ]
    for copy in own:
        copy.wait()
    arrived(first)
    second = []
    for k in range(3):
        for source in (heads_all.at[:, x, z, 0], branch_all.at[core, :, x, z, 0]):
            second.append(sender.start(source, source, along_x[k]))
        for source in (heads_all.at[:, x, z, 1], branch_all.at[core, :, x, z, 1]):
            second.append(sender.start(source, source, along_z[k]))
    arrived(expert_first)
    mine = experts_all.at[:, yh, x]
    expert_second = [sender.start(mine, mine, along_y)]
    arrived(second)
    third = []
    for k in range(3):
        for source in (heads_all.at[:, :, z, 0], branch_all.at[core, :, :, z, 0]):
            third.append(sender.start(source, source, along_z[k]))
        for source in (heads_all.at[:, x, :, 1], branch_all.at[core, :, x, :, 1]):
            third.append(sender.start(source, source, along_x[k]))
    arrived(expert_second)
    mine = experts_all.at[:, :, x]
    expert_third = [sender.start(mine, mine, along_x[k]) for k in range(3)]
    row_copies = []
    for partner in group:
        other = partner[2] * 4 + partner[3]
        row_copies.append(sender.start(rows.at[other], rows_all.at[expert], partner))
    arrived(token_copies)
    far = tokens_all.at[1 - yl, core]
    last = [sender.start(far, far, sibling)]
    arrived(third)
    half = branch_all.at[core]
    last.append(sender.start(half, half, sibling))
    arrived(expert_third)
    arrived(row_copies)
    arrived(last)
    sender.finish()


def scatter_kernel(
    heads, branch, experts,
    heads_all, branch_all, experts_all,
    send, recv, local,
):
    yh, x, z, seq = place()
    dp = yh * 16 + x * 4 + z

    def branch_block(index):
        top = pl.multiple_of(index // 2 * 16, 16)
        left = pl.multiple_of(index % 2 * 512, 512)
        return branch.at[pl.ds(top, 16), pl.ds(left, 512)]

    others = [(dp + k) % 32 for k in range(1, 32)]
    partners = [(other // 16, other // 4 % 4, other % 4, seq) for other in others]
    greet(partners)
    own = local_starts(
        [
            (heads.at[dp], heads_all.at[dp]),
            (branch_block(dp), branch_all.at[dp]),
            (experts.at[:, dp], experts_all.at[dp]),
        ],
        local,
    )
    sender = Sender(send, recv)
    for other, partner in zip(others, partners):
        sender.start(experts.at[:, other], experts_all.at[dp], partner)
        sender.start(heads.at[other], heads_all.at[dp], partner)
        sender.start(branch_block(other), branch_all.at[dp], partner)
    for copy in own:
        copy.wait()
    arrived(sender.copies)
    sender.finish()


def share_kernel(
    heads, branch, experts,
    heads_all, branch_all, experts_all,
    send, recv, local, branch_sends, branch_recvs,
):
    yh, x, z, seq = place()
    yl, core = seq // 2, seq % 2
    dp = yh * 16 + x * 4 + z
    near = (yh, x, z, (1 - yl) * 2 + core)
    sibling = (yh, x, z, yl * 2 + 1 - core)
    owner = seq * 8 + dp // 4
    source_seq = dp // 8
    slot = dp % 4
    barrier = pltpu.get_barrier_semaphore()
    for partner in (near, sibling):
        pl.semaphore_signal(barrier, inc=1, device_id=partner, device_id_type=BY_ID)
    here = jnp.logical_and(owner == dp, True)
    for k in range(4):
        maker = dp % 8 * 4 + k
        foreign = jnp.logical_or(maker != dp, source_seq != seq)

        @pl.when(foreign)
        def _():
            pl.semaphore_signal(
                barrier,
                inc=1,
                device_id=(maker // 16, maker // 4 % 4, maker % 4, source_seq),
                device_id_type=BY_ID,
            )

    pl.semaphore_wait(barrier, 6 - here.astype(jnp.int32))
    own = local_starts(
        [(heads, heads_all.at[yl, core]), (experts, experts_all.at[yl, core])], local
    )
    sender = Sender(send, recv)
    first = []
    for partner in (near, sibling):
        first.append(sender.start(heads, heads_all.at[yl, core], partner))
        first.append(sender.start(experts, experts_all.at[yl, core], partner))
    place_of = branch_all.at[slot]

    def branch_copy(k):
        return pltpu.make_async_remote_copy(
            src_ref=branch,
            dst_ref=place_of,
            send_sem=branch_sends.at[k],
            recv_sem=branch_recvs.at[slot],
            device_id=(owner // 16, owner // 4 % 4, owner % 4, k),
            device_id_type=BY_ID,
        )

    for k in range(4):
        self_copy = jnp.logical_and(here, seq == k)

        @pl.when(jnp.logical_not(self_copy))
        def _():
            branch_copy(k).start()

        @pl.when(self_copy)
        def _():
            pltpu.make_async_copy(branch, place_of, branch_recvs.at[slot]).start()

    for copy in own:
        copy.wait()
    arrived(first[:2])
    last = []
    for buffer in (heads_all, experts_all):
        far = buffer.at[1 - yl, core]
        last.append(sender.start(far, far, sibling))
    arrived(first[2:])
    arrived(last)
    for k in range(4):
        pltpu.make_async_copy(branch, branch_all.at[k], branch_recvs.at[k]).wait()
        self_copy = jnp.logical_and(here, seq == k)

        @pl.when(jnp.logical_not(self_copy))
        def _():
            branch_copy(k).wait_send()

    sender.finish()


def angles(count, head_dim):
    freqs = ROPE_BASE ** (-jnp.arange(0, head_dim, 2).astype(F32) / head_dim)
    places = jnp.arange(count, dtype=jnp.int32).astype(F32)
    turns = places[:, None] * freqs[None, :]
    turns = jnp.concatenate([turns, turns], axis=-1)
    return (jnp.cos(turns)[:, None, :], jnp.sin(turns)[:, None, :])


def turned(values):
    half = values.shape[-1] // 2
    return jnp.concatenate([-values[..., half:], values[..., :half]], axis=-1)


def masked_scores(query_block, key_rows):
    scores = (
        jnp.einsum("qkgd,skd->kgqs", query_block, key_rows, preferred_element_type=F32)
        / query_block.shape[-1]
    )
    causal = jnp.arange(query_block.shape[0])[:, None] >= jnp.arange(key_rows.shape[0])[None, :]
    return jnp.where(causal, scores, MASK_VALUE)


def norm_back(grad_normed, values, factor, gain):
    scaled = grad_normed * gain
    mean_term = jnp.mean(scaled * values, axis=-1, keepdims=True)
    grad_values = factor * scaled - values * factor * factor * factor * mean_term
    grad_gain = jnp.sum(grad_normed * values * factor, axis=0)
    return (grad_values, grad_gain)


def slot_matrices(routes, route_gates):
    named = (routes[:, :, None] == jnp.arange(EXPERTS, dtype=jnp.int32)).astype(F32)
    uses = jnp.sum(named, axis=1)
    gates = jnp.sum(named * route_gates[:, :, None], axis=1)
    row = lax.broadcasted_iota(jnp.int32, (TOK, TOK), 0)
    column = lax.broadcasted_iota(jnp.int32, (TOK, TOK), 1)
    earlier = (row > column).astype(BF16)
    ranks = jnp.dot(earlier, uses.astype(BF16), preferred_element_type=F32)
    slot = jnp.arange(SLOTS, dtype=jnp.int32)
    spread = (jnp.arange(EXPERTS, dtype=jnp.int32)[:, None] == slot[None, :] // CAP).astype(F32)
    both = jnp.where(uses > 0.5, ranks, -1.0).astype(BF16)
    flat = jnp.dot(both, spread.astype(BF16), preferred_element_type=F32)
    hits = flat == (slot % CAP).astype(F32)[None, :]
    flat_gates = jnp.dot(gates, spread, precision=lax.Precision.HIGHEST)
    weights = jnp.where(hits, RESIDUAL * flat_gates, 0.0)
    return (named, spread, hits.astype(BF16), weights)


def shards(
    layer_in, norm_one, w_query, key_weight, value_weight, w_output, norm_two,
    w_gate, w_up, w_down, routes, route_gates, cotangent,
):
    seq = lax.axis_index("seq")
    core = seq % 2
    key_value_resident = KEY_VALUE_HEADS // 4
    group_width = QUERY_HEADS // KEY_VALUE_HEADS
    head_width = key_value_resident * group_width * HEAD_SIZE
    kv_width = key_value_resident * HEAD_SIZE

    gains = jnp.pad(jnp.stack([norm_one, norm_two], axis=1), ((0, 0), (0, 126)))
    heads_block = jnp.concatenate(
        [
            lax.dynamic_slice_in_dim(w_query, seq * head_width, head_width, 1),
            lax.dynamic_slice_in_dim(key_weight, seq * kv_width, kv_width, 1),
            lax.dynamic_slice_in_dim(value_weight, seq * kv_width, kv_width, 1),
            gains,
        ],
        axis=1,
    ).reshape(2, 16, 640)
    branch_block = lax.dynamic_slice_in_dim(w_output, core * 512, 512, 1).reshape(2, 16, 512)
    expert_block = jnp.stack(
        [
            lax.dynamic_index_in_dim(w.reshape(32, 4, 4, FF), seq, 2, keepdims=False)
            for w in (w_gate, w_up, w_down)
        ]
    ).transpose(2, 0, 1, 3)
    named, spread, hits, weights = slot_matrices(routes, route_gates)
    slot_weights = jnp.sum(weights, axis=0)
    grad_slots = (
        jnp.einsum("tj,td->jd", hits, cotangent, preferred_element_type=F32)
        * slot_weights[:, None]
    ).astype(BF16).reshape(EXPERTS, CAP, MODEL_WIDTH)

    heads_w, branch_w, tokens_all, expert_w, grad_returned = remote_call(
        gather_kernel,
        (heads_block, branch_block, layer_in, expert_block, grad_slots),
        (
            (2, 4, 4, 2, 16, 640),
            (2, 2, 4, 4, 2, 16, 512),
            (2, 2, TOK, MODEL_WIDTH),
            (3, 2, 4, 4, 32, FF),
            (EXPERTS, CAP, MODEL_WIDTH),
        ),
        52,
        5,
        1,
        "gather_all",
    )
    heads_w = heads_w.reshape(MODEL_WIDTH, 640)
    gain_first = heads_w[:, 512].astype(F32)
    gain_second = heads_w[:, 513].astype(F32)
    heads_w = heads_w[:, :512]
    branch_w = branch_w.reshape(2, MODEL_WIDTH, 512)
    expert_w = expert_w.reshape(3, MODEL_WIDTH, FF)
    grad_back = grad_returned.reshape(SLOTS, MODEL_WIDTH)

    sequence = tokens_all.reshape(SEQ_LEN, MODEL_WIDTH).astype(F32)
    factor_all = lax.rsqrt(jnp.mean(sequence * sequence, axis=-1, keepdims=True) + EPSILON)
    normed_all = (sequence * factor_all * gain_first).astype(BF16)
    cosine, sine = angles(SEQ_LEN, HEAD_SIZE)
    projected = jnp.dot(normed_all, heads_w, preferred_element_type=F32)
    query_pre = projected[:, :head_width].reshape(SEQ_LEN, -1, HEAD_SIZE)
    key_pre = projected[:, head_width : head_width + kv_width].reshape(SEQ_LEN, -1, HEAD_SIZE)
    query_all = (query_pre * cosine + turned(query_pre) * sine).astype(BF16)
    query_all = query_all.reshape(SEQ_LEN, key_value_resident, group_width, HEAD_SIZE)
    key_all = (key_pre * cosine + turned(key_pre) * sine).astype(BF16)
    value_all = projected[:, head_width + kv_width :].astype(BF16)
    value_all = value_all.reshape(SEQ_LEN, key_value_resident, HEAD_SIZE)
    scores = masked_scores(query_all, key_all)
    top_score = jnp.max(scores, axis=-1, keepdims=True)
    exponent = jnp.exp(scores - top_score)
    total_mass = jnp.sum(exponent, axis=-1, keepdims=True)
    probs = (exponent / total_mass).astype(BF16)
    log_sums = top_score + jnp.log(total_mass)
    attended = jnp.einsum("kgqs,skd->qkgd", probs, value_all, preferred_element_type=F32)
    attended = attended.reshape(SEQ_LEN, head_width).astype(BF16)
    attended_tok = lax.all_to_all(attended, "seq", split_axis=0, concat_axis=1, tiled=True)

    inputs = layer_in.astype(F32)
    branch = jnp.concatenate(
        [jnp.dot(attended_tok, branch_w[k], preferred_element_type=F32) for k in range(2)], axis=1
    )
    middle = inputs + RESIDUAL * branch
    factor_two = lax.rsqrt(jnp.mean(middle * middle, axis=-1, keepdims=True) + EPSILON)
    normed_two = (middle * factor_two * gain_second).astype(BF16)
    slot_rows = jnp.einsum("tj,td->jd", hits, normed_two, preferred_element_type=F32).astype(BF16)
    expert_rows = lax.all_to_all(
        slot_rows.reshape(EXPERTS, CAP, MODEL_WIDTH), ("z", "seq"), 0, 0, tiled=True
    ).reshape(SLOTS, MODEL_WIDTH)

    gate_pre = jnp.dot(expert_rows, expert_w[0], preferred_element_type=F32)
    up_pre = jnp.dot(expert_rows, expert_w[1], preferred_element_type=F32)
    sigmoid_gate = jax.nn.sigmoid(gate_pre)
    active = (gate_pre * sigmoid_gate * up_pre).astype(BF16)
    returned = jnp.einsum("cf,df->cd", active, expert_w[2], preferred_element_type=F32)
    grad_active = jnp.dot(grad_back, expert_w[2], preferred_element_type=F32)
    grad_gate = (
        grad_active * up_pre * sigmoid_gate * (1.0 + gate_pre * (1.0 - sigmoid_gate))
    ).astype(BF16)
    grad_up = (grad_active * gate_pre * sigmoid_gate).astype(BF16)
    grad_rows = (
        jnp.einsum("cf,df->cd", grad_gate, expert_w[0], preferred_element_type=F32)
        + jnp.einsum("cf,df->cd", grad_up, expert_w[1], preferred_element_type=F32)
    ).astype(BF16)
    grad_rows = lax.all_to_all(
        grad_rows.reshape(EXPERTS, CAP, MODEL_WIDTH), ("z", "seq"), 0, 0, tiled=True
    ).reshape(SLOTS, MODEL_WIDTH)
    returned = lax.all_to_all(
        returned.astype(BF16).reshape(EXPERTS, CAP, MODEL_WIDTH), ("z", "seq"), 0, 0, tiled=True
    ).reshape(SLOTS, MODEL_WIDTH)
    expert_grads = jnp.stack(
        [
            jnp.einsum("cd,cf->df", expert_rows, grad_gate, preferred_element_type=F32).astype(BF16),
            jnp.einsum("cd,cf->df", expert_rows, grad_up, preferred_element_type=F32).astype(BF16),
            jnp.einsum("cd,cf->df", grad_back, active, preferred_element_type=F32).astype(BF16),
        ]
    ).reshape(3, 32, 32, FF)

    grad_out = cotangent.astype(F32)
    layer_out = (
        middle + jnp.dot(weights.astype(BF16), returned, preferred_element_type=F32)
    ).astype(BF16)
    pair_dots = jnp.einsum("td,jd->tj", cotangent, returned, preferred_element_type=F32)
    expert_dots = jnp.einsum(
        "tj,ej->te", pair_dots * hits.astype(F32), spread, precision=lax.Precision.HIGHEST
    )
    grad_gates = RESIDUAL * jnp.sum(named * expert_dots[:, None, :], axis=-1)
    grad_normed_two = jnp.dot(hits, grad_rows, preferred_element_type=F32)
    grad_middle_norm, gain_two_term = norm_back(grad_normed_two, middle, factor_two, gain_second)
    grad_middle = grad_out + grad_middle_norm
    grad_branch = (RESIDUAL * grad_middle).astype(BF16)
    grad_branch_all = lax.all_gather(grad_branch, "seq", axis=0, tiled=True)
    branch_rows = lax.dynamic_slice_in_dim(branch_w, seq * head_width, head_width, 1)
    output_term = jnp.einsum(
        "th,td->hd", attended, grad_branch_all, preferred_element_type=F32
    ).astype(BF16)
    grad_heads = (
        jnp.einsum("td,hd->th", grad_branch_all[:, :512], branch_rows[0], preferred_element_type=F32)
        + jnp.einsum(
            "td,hd->th", grad_branch_all[:, 512:], branch_rows[1], preferred_element_type=F32
        )
    ).astype(BF16)

    scores = masked_scores(query_all, key_all)
    probs = jnp.exp(scores - log_sums)
    grad_block = grad_heads.reshape(SEQ_LEN, key_value_resident, group_width, HEAD_SIZE)
    grad_probs = jnp.einsum("qkgd,skd->kgqs", grad_block, value_all, preferred_element_type=F32)
    grad_value = jnp.einsum(
        "kgqs,qkgd->skd", probs.astype(BF16), grad_block, preferred_element_type=F32
    )
    inner = jnp.sum(probs * grad_probs, axis=-1, keepdims=True)
    grad_scores = (probs * (grad_probs - inner)).astype(BF16)
    grad_query = (
        jnp.einsum("kgqs,skd->qkgd", grad_scores, key_all, preferred_element_type=F32) / HEAD_SIZE
    ).reshape(SEQ_LEN, -1, HEAD_SIZE)
    grad_key = (
        jnp.einsum("kgqs,qkgd->skd", grad_scores, query_all, preferred_element_type=F32) / HEAD_SIZE
    )
    grad_query = grad_query.astype(BF16).astype(F32)
    grad_key = grad_key.astype(BF16).astype(F32)
    grad_projected = jnp.concatenate(
        [
            (grad_query * cosine - turned(grad_query) * sine).reshape(SEQ_LEN, -1).astype(BF16),
            (grad_key * cosine - turned(grad_key) * sine).reshape(SEQ_LEN, -1).astype(BF16),
            grad_value.reshape(SEQ_LEN, -1).astype(BF16),
        ],
        axis=1,
    )
    heads_term = jnp.einsum(
        "td,tf->df", normed_all, grad_projected, preferred_element_type=F32
    ).astype(BF16)
    grad_normed_parts = jnp.einsum(
        "tf,df->td", grad_projected, heads_w, preferred_element_type=F32
    ).astype(BF16)
    grad_normed_parts = lax.all_to_all(
        grad_normed_parts.reshape(4, TOK, MODEL_WIDTH), "seq", 0, 0, tiled=True
    )
    grad_normed = jnp.sum(grad_normed_parts.astype(F32), axis=0)
    factor_one = lax.rsqrt(jnp.mean(inputs * inputs, axis=-1, keepdims=True) + EPSILON)
    grad_input_norm, gain_one_term = norm_back(grad_normed, inputs, factor_one, gain_first)
    grad_input = (grad_middle + grad_input_norm).astype(BF16)

    gain_terms = jnp.pad(
        jnp.stack([gain_one_term, gain_two_term], axis=1).astype(BF16), ((0, 0), (0, 126))
    )
    heads_term = jnp.concatenate([heads_term, gain_terms], axis=1).reshape(32, 32, 640)
    heads_parts, branch_parts, expert_parts = remote_call(
        scatter_kernel,
        (heads_term, output_term, expert_grads),
        ((32, 32, 640), (32, 16, 512), (32, 3, 32, FF)),
        93,
        3,
        2,
        "scatter_all",
    )
    heads_sum = jnp.sum(heads_parts.astype(F32), axis=0).astype(BF16)
    branch_sum = jnp.sum(branch_parts.astype(F32), axis=0).astype(BF16)
    expert_sum = jnp.sum(expert_parts.astype(F32).reshape(8, 4, 3, 32, FF), axis=0).astype(BF16)
    heads_four, branch_four, expert_four = pl.pallas_call(
        share_kernel,
        out_shape=(
            jax.ShapeDtypeStruct((2, 2, 32, 640), BF16),
            jax.ShapeDtypeStruct((4, 16, 512), BF16),
            jax.ShapeDtypeStruct((2, 2, 4, 3, 32, FF), BF16),
        ),
        in_specs=[pl.BlockSpec(memory_space=pl.ANY)] * 3,
        out_specs=(pl.BlockSpec(memory_space=pl.ANY),) * 3,
        scratch_shapes=[
            pltpu.SemaphoreType.DMA((6,)),
            pltpu.SemaphoreType.DMA((6,)),
            pltpu.SemaphoreType.DMA((2,)),
            pltpu.SemaphoreType.DMA((4,)),
            pltpu.SemaphoreType.DMA((4,)),
        ],
        compiler_params=pltpu.CompilerParams(collective_id=3, has_side_effects=True),
        name="share_all",
    )(heads_sum, branch_sum, expert_sum)
    heads_four = heads_four.reshape(4, 32, 640).astype(F32)
    grad_query_proj = heads_four[:, :, :head_width].transpose(1, 0, 2).reshape(32, -1)
    grad_key_proj = heads_four[:, :, 256:384].transpose(1, 0, 2).reshape(32, -1)
    grad_value_proj = heads_four[:, :, 384:512].transpose(1, 0, 2).reshape(32, -1)
    gain_sums = jnp.sum(heads_four[:, :, 512:514], axis=0)
    grad_output_proj = (
        branch_four.reshape(2, 2, 16, 512).transpose(0, 2, 1, 3).reshape(32, MODEL_WIDTH).astype(F32)
    )
    expert_four = expert_four.reshape(4, 4, 3, 32, FF).transpose(2, 3, 1, 0, 4)
    expert_four = expert_four.reshape(3, 32, EXPERTS, FF).astype(F32)
    return (
        layer_out,
        grad_input,
        gain_sums[:, 0],
        grad_query_proj,
        grad_key_proj,
        grad_value_proj,
        grad_output_proj,
        gain_sums[:, 1],
        expert_four[0],
        expert_four[1],
        expert_four[2],
        grad_gates,
    )


def solution(mesh):
    dp = ("yh", "x", "z")
    cut = Mesh(mesh.devices.reshape(2, 4, 4, 4), AXES)
    tokens, rows, gain, experts = P(AXES, None), P(dp, None), P(dp), P(dp, None, None)
    return jax.shard_map(
        shards,
        mesh=cut,
        in_specs=(
            tokens, gain, rows, rows, rows, rows, gain, experts, experts, experts,
            tokens, tokens, tokens,
        ),
        out_specs=(
            tokens, tokens, gain, rows, rows, rows, rows, gain, experts, experts, experts, tokens,
        ),
        check_vma=False,
    )
```

```python
import jax
import jax.numpy as jnp
from jax import lax
from jax.experimental import pallas as pl
from jax.experimental.pallas import tpu as pltpu
from jax.sharding import Mesh
from jax.sharding import PartitionSpec as P

MODEL_WIDTH = 1024
QUERY_HEADS = 16
KEY_VALUE_HEADS = 8
HEAD_SIZE = 64
TOP = 8
EXPERTS = 16
CAP = 72
SLOTS = EXPERTS * CAP
TOK = 128
SEQ_LEN = 512
FF = 512
EPSILON = 1e-05
RESIDUAL = 0.22
ROPE_BASE = 10000.0
MASK_VALUE = -1e30

BF16 = jnp.bfloat16
F32 = jnp.float32
AXES = ("yh", "x", "z", "seq")
BY_ID = pl.DeviceIdType.MESH


def place():
    return tuple(lax.axis_index(axis) for axis in AXES)


class Sender:
    def __init__(self, send, recv):
        self.send, self.recv, self.used, self.copies = send, recv, 0, []

    def start(self, source, target, device):
        copy = pltpu.make_async_remote_copy(
            src_ref=source,
            dst_ref=target,
            send_sem=self.send.at[self.used],
            recv_sem=self.recv.at[self.used],
            device_id=device,
            device_id_type=BY_ID,
        )
        copy.start()
        self.used += 1
        self.copies.append(copy)
        return copy

    def finish(self):
        for copy in self.copies:
            copy.wait_send()


def arrived(copies):
    for copy in copies:
        copy.wait_recv()


def greet(partners):
    barrier = pltpu.get_barrier_semaphore()
    for partner in partners:
        pl.semaphore_signal(barrier, inc=1, device_id=partner, device_id_type=BY_ID)
    pl.semaphore_wait(barrier, len(partners))


def remote_call(kernel, inputs, outputs, copies, local_copies, collective_id, name):
    return pl.pallas_call(
        kernel,
        out_shape=tuple(jax.ShapeDtypeStruct(shape, BF16) for shape in outputs),
        in_specs=[pl.BlockSpec(memory_space=pl.ANY)] * len(inputs),
        out_specs=tuple(pl.BlockSpec(memory_space=pl.ANY) for _ in outputs),
        scratch_shapes=[
            pltpu.SemaphoreType.DMA((copies,)),
            pltpu.SemaphoreType.DMA((copies,)),
            pltpu.SemaphoreType.DMA((local_copies,)),
        ],
        compiler_params=pltpu.CompilerParams(collective_id=collective_id, has_side_effects=True),
        name=name,
    )(*inputs)


def local_starts(pairs, sems):
    copies = []
    for index, (source, target) in enumerate(pairs):
        copy = pltpu.make_async_copy(source, target, sems.at[index])
        copy.start()
        copies.append(copy)
    return copies


def group_of(x, z, seq, yh):
    yl, core = seq // 2, seq % 2
    return [
        (yh, x, (z + k // 4) % 4, (yl + (k // 2) % 2) % 2 * 2 + (core + k % 2) % 2)
        for k in range(1, 16)
    ]


def gather_kernel(
    heads, branch, tokens, experts, rows,
    heads_all, branch_all, tokens_all, gate_all, rest_all, rows_all,
    send, recv, local,
):
    yh, x, z, seq = place()
    yl, core = seq // 2, seq % 2
    along_y = (1 - yh, x, z, seq)
    along_x = [(yh, (x + k) % 4, z, seq) for k in (1, 2, 3)]
    along_z = [(yh, x, (z + k) % 4, seq) for k in (1, 2, 3)]
    near = (yh, x, z, (1 - yl) * 2 + core)
    sibling = (yh, x, z, yl * 2 + 1 - core)
    group = group_of(x, z, seq, yh)
    expert = z * 4 + seq
    greet([along_y] + along_x + group)
    sender = Sender(send, recv)
    first = [
        sender.start(heads, heads_all.at[yh, x, z], along_y),
        sender.start(branch, branch_all.at[core, yh, x, z], along_y),
    ]
    expert_first = []
    for partner in along_z:
        block = experts.at[partner[2]]
        expert_first.append(sender.start(block.at[0], gate_all.at[yh, x, z], partner))
        expert_first.append(
            sender.start(block.at[pl.ds(1, 2)], rest_all.at[:, yh, z], partner)
        )
    token_copies = [
        sender.start(tokens, tokens_all.at[yl, core], near),
        sender.start(tokens, tokens_all.at[yl, core], sibling),
    ]
    own = local_starts(
        [
            (heads, heads_all.at[yh, x, z]),
            (branch, branch_all.at[core, yh, x, z]),
            (experts.at[z, 0], gate_all.at[yh, x, z]),
            (experts.at[z, pl.ds(1, 2)], rest_all.at[:, yh, z]),
            (tokens, tokens_all.at[yl, core]),
            (rows.at[expert], rows_all.at[expert]),
        ],
        local,
    )
    for copy in own[:2]:
        copy.wait()
    arrived(first)
    second = []
    for partner in along_z:
        for source in (heads_all.at[:, x, z], branch_all.at[core, :, x, z]):
            second.append(sender.start(source, source, partner))
    for copy in own[2:4]:
        copy.wait()
    arrived(expert_first)
    mine, rest = gate_all.at[yh, x], rest_all.at[:, yh]
    expert_second = [
        sender.start(mine, mine, along_y),
        sender.start(rest, rest, along_y),
    ]
    arrived(second)
    third = []
    for partner in along_x:
        for source in (heads_all.at[:, x], branch_all.at[core, :, x]):
            third.append(sender.start(source, source, partner))
    row_copies = []
    for partner in group:
        other = partner[2] * 4 + partner[3]
        row_copies.append(sender.start(rows.at[other], rows_all.at[expert], partner))
    arrived(expert_second)
    mine = gate_all.at[:, x]
    expert_third = [sender.start(mine, mine, partner) for partner in along_x]
    arrived(token_copies)
    far = tokens_all.at[1 - yl, core]
    last = [sender.start(far, far, sibling)]
    arrived(third)
    half = branch_all.at[core]
    last.append(sender.start(half, half, sibling))
    for copy in own[4:]:
        copy.wait()
    arrived(expert_third)
    arrived(row_copies)
    arrived(last)
    sender.finish()


def dispatch_kernel(rows, rest, rows_all, rest_all, send, recv, local):
    yh, x, z, seq = place()
    along_x = [(yh, (x + k) % 4, z, seq) for k in (1, 2, 3)]
    group = group_of(x, z, seq, yh)
    expert = z * 4 + seq
    greet(along_x + group)
    sender = Sender(send, recv)
    for partner in group:
        other = partner[2] * 4 + partner[3]
        sender.start(rows.at[other], rows_all.at[expert], partner)
    for partner in along_x:
        sender.start(rest, rest_all.at[:, :, x], partner)
    own = local_starts(
        [(rows.at[expert], rows_all.at[expert]), (rest, rest_all.at[:, :, x])], local
    )
    for copy in own:
        copy.wait()
    arrived(sender.copies)
    sender.finish()


def trade_kernel(blocks, blocks_all, send, recv, local):
    yh, x, z, seq = place()
    partners = [(yh, x, z, (seq + k) % 4) for k in (1, 2, 3)]
    greet(partners)
    own = local_starts([(blocks.at[seq], blocks_all.at[seq])], local)
    sender = Sender(send, recv)
    for partner in partners:
        sender.start(blocks.at[partner[3]], blocks_all.at[seq], partner)
    own[0].wait()
    arrived(sender.copies)
    sender.finish()


def spread_kernel(block, blocks_all, send, recv, local):
    yh, x, z, seq = place()
    yl, core = seq // 2, seq % 2
    near = (yh, x, z, (1 - yl) * 2 + core)
    sibling = (yh, x, z, yl * 2 + 1 - core)
    greet([near, sibling])
    sender = Sender(send, recv)
    first = [
        sender.start(block, blocks_all.at[yl, core], near),
        sender.start(block, blocks_all.at[yl, core], sibling),
    ]
    own = local_starts([(block, blocks_all.at[yl, core])], local)
    arrived(first[:1])
    far = blocks_all.at[1 - yl, core]
    last = sender.start(far, far, sibling)
    arrived(first[1:])
    own[0].wait()
    arrived([last])
    sender.finish()


def gather_sums(parts):
    total = parts[0].astype(F32)
    for part in parts[1:]:
        total = total + part.astype(F32)
    return total


def trade_sum_kernel(parts, total, arriving, paired, outgoing, incoming, send, recv):
    yh, x, z, seq = place()
    yl, core = seq // 2, seq % 2
    near = (yh, x, z, (1 - yl) * 2 + core)
    sibling = (yh, x, z, yl * 2 + 1 - core)
    greet([near, sibling])
    sender = Sender(send, recv)
    first = [
        sender.start(parts.at[1 - yl, 1 - core], arriving.at[0], sibling),
        sender.start(parts.at[yl, 1 - core], arriving.at[1], sibling),
    ]
    arrived(first[:1])
    outgoing[...] = gather_sums([parts[1 - yl, core], arriving[0]]).astype(BF16)
    last = sender.start(outgoing, incoming, near)
    arrived(first[1:])
    paired[...] = gather_sums([parts[yl, core], arriving[1]])
    arrived([last])
    total[...] = paired[...] + incoming[...].astype(F32)
    sender.finish()


def finish_kernel(
    heads, branch, experts,
    heads_four, branch_four, experts_four,
    heads_x, branch_x, heads_out, branch_out,
    heads_plane, branch_plane, experts_plane,
    heads_sum, branch_sum, experts_sum,
    send, recv, local, branch_sends, branch_recvs,
):
    yh, x, z, seq = place()
    yl, core = seq // 2, seq % 2
    dp = yh * 16 + x * 4 + z
    near = (yh, x, z, (1 - yl) * 2 + core)
    sibling = (yh, x, z, yl * 2 + 1 - core)
    along_x = [(yh, (x + k) % 4, z, seq) for k in (1, 2, 3)]
    plane = [((yh + k // 4) % 2, x, (z + k % 4) % 4, seq) for k in range(1, 8)]
    owner = seq * 8 + dp // 4
    source_seq = dp // 8
    slot = dp % 4
    here = owner == dp
    barrier = pltpu.get_barrier_semaphore()
    for partner in [near, sibling] + along_x + plane:
        pl.semaphore_signal(barrier, inc=1, device_id=partner, device_id_type=BY_ID)
    for k in range(4):
        maker = dp % 8 * 4 + k
        foreign = jnp.logical_or(maker != dp, source_seq != seq)

        @pl.when(foreign)
        def _():
            pl.semaphore_signal(
                barrier,
                inc=1,
                device_id=(maker // 16, maker // 4 % 4, maker % 4, source_seq),
                device_id_type=BY_ID,
            )

    pl.semaphore_wait(barrier, 16 - here.astype(jnp.int32))
    sender = Sender(send, recv)
    first = []
    for k, partner in enumerate(along_x):
        first.append(sender.start(heads.at[:, partner[1]], heads_x.at[k], partner))
        first.append(sender.start(branch.at[:, partner[1]], branch_x.at[k], partner))
    across = []
    for k, partner in enumerate(plane):
        across.append(
            sender.start(experts.at[partner[0], partner[2]], experts_plane.at[yh, z], partner)
        )
    arrived(first)
    for y in range(2):
        for j in range(4):
            heads_out[y, j] = gather_sums(
                [heads[y, x, j]] + [heads_x[k, y, j] for k in range(3)]
            ).astype(BF16)
        total = gather_sums([branch[y, x]] + [branch_x[k, y] for k in range(3)]).astype(BF16)
        for j in range(4):
            branch_out[y, j] = total[j // 2 * 16 : j // 2 * 16 + 16, j % 2 * 512 : j % 2 * 512 + 512]
    second = []
    for k, partner in enumerate(plane):
        second.append(sender.start(heads_out.at[partner[0], partner[2]], heads_plane.at[k], partner))
        second.append(
            sender.start(branch_out.at[partner[0], partner[2]], branch_plane.at[k], partner)
        )
    arrived(across)
    for j in range(4):
        @pl.when(z == j)
        def _():
            experts_sum[j] = gather_sums([experts[yh, j], experts_plane[1 - yh, j]]).astype(BF16)

        @pl.when(z != j)
        def _():
            experts_sum[j] = gather_sums([experts_plane[0, j], experts_plane[1, j]]).astype(BF16)

    third = []
    for partner in (near, sibling):
        third.append(sender.start(experts_sum, experts_four.at[yl, core], partner))
    own = local_starts([(experts_sum, experts_four.at[yl, core])], local)
    arrived(second)
    heads_sum[...] = gather_sums([heads_out[yh, z]] + [heads_plane[k] for k in range(7)]).astype(BF16)
    branch_sum[...] = gather_sums(
        [branch_out[yh, z]] + [branch_plane[k] for k in range(7)]
    ).astype(BF16)
    fourth = []
    for partner in (near, sibling):
        fourth.append(sender.start(heads_sum, heads_four.at[yl, core], partner))
    place_of = branch_four.at[slot]

    def branch_copy(k):
        return pltpu.make_async_remote_copy(
            src_ref=branch_sum,
            dst_ref=place_of,
            send_sem=branch_sends.at[k],
            recv_sem=branch_recvs.at[slot],
            device_id=(owner // 16, owner // 4 % 4, owner % 4, k),
            device_id_type=BY_ID,
        )

    for k in range(4):
        self_copy = jnp.logical_and(here, seq == k)

        @pl.when(jnp.logical_not(self_copy))
        def _():
            branch_copy(k).start()

        @pl.when(self_copy)
        def _():
            pltpu.make_async_copy(branch_sum, place_of, branch_recvs.at[slot]).start()

    own_heads = pltpu.make_async_copy(heads_sum, heads_four.at[yl, core], local.at[1])
    own_heads.start()
    arrived(third[:1])
    far = experts_four.at[1 - yl, core]
    last = [sender.start(far, far, sibling)]
    arrived(fourth[:1])
    far = heads_four.at[1 - yl, core]
    last.append(sender.start(far, far, sibling))
    arrived(third[1:])
    arrived(fourth[1:])
    own[0].wait()
    own_heads.wait()
    arrived(last)
    for k in range(4):
        pltpu.make_async_copy(branch_sum, branch_four.at[k], branch_recvs.at[k]).wait()
        self_copy = jnp.logical_and(here, seq == k)

        @pl.when(jnp.logical_not(self_copy))
        def _():
            branch_copy(k).wait_send()

    sender.finish()


def unpack_kernel(heads, branch, experts, query, key, value, output, gate, up, down):
    for s in range(4):
        block = heads[s // 2, s % 2].astype(F32)
        query[:, s * 256 : s * 256 + 256] = block[:, :256]
        key[:, s * 128 : s * 128 + 128] = block[:, 256:384]
        value[:, s * 128 : s * 128 + 128] = block[:, 384:512]
        rows, columns = s // 2 * 16, s % 2 * 512
        output[rows : rows + 16, columns : columns + 512] = branch[s].astype(F32)
        for j in range(4):
            block = experts[s // 2, s % 2, j].astype(F32)
            for index, result in enumerate((gate, up, down)):
                result[:, j * 4 + s, :] = block[:, index * 512 : index * 512 + 512]


def expert_kernel(
    rows, back, gate_w, up_w, down_w, grad_rows, returned, active, grad_gate, grad_up
):
    gate_pre = jnp.dot(rows[...], gate_w[...], preferred_element_type=F32)
    up_pre = jnp.dot(rows[...], up_w[...], preferred_element_type=F32)
    grad_active = jnp.dot(back[...], down_w[...], preferred_element_type=F32)
    sigmoid_gate = jax.nn.sigmoid(gate_pre)
    silu = gate_pre * sigmoid_gate
    act = (silu * up_pre).astype(BF16)
    slope = sigmoid_gate * (1.0 + gate_pre * (1.0 - sigmoid_gate))
    by_gate = (grad_active * up_pre * slope).astype(BF16)
    by_up = (grad_active * silu).astype(BF16)
    active[...] = act
    grad_gate[...] = by_gate
    grad_up[...] = by_up
    turned_dims = (((1,), (1,)), ((), ()))
    grad_rows[...] = (
        lax.dot_general(by_gate, gate_w[...], turned_dims, preferred_element_type=F32)
        + lax.dot_general(by_up, up_w[...], turned_dims, preferred_element_type=F32)
    ).astype(BF16)
    returned[...] = lax.dot_general(
        act, down_w[...], turned_dims, preferred_element_type=F32
    ).astype(BF16)


def expert_grad_kernel(rows, back, active, grad_gate, grad_up, result):
    first_dims = (((0,), (0,)), ((), ()))
    for index, (left, right) in enumerate(((rows, grad_gate), (rows, grad_up), (back, active))):
        total = lax.dot_general(left[...], right[...], first_dims, preferred_element_type=F32)
        result[:, 0, :, index * 512 : index * 512 + 512] = total.astype(BF16).reshape(4, TOK, 512)


def angles(count, head_dim):
    freqs = ROPE_BASE ** (-jnp.arange(0, head_dim, 2).astype(F32) / head_dim)
    places = jnp.arange(count, dtype=jnp.int32).astype(F32)
    turns = places[:, None] * freqs[None, :]
    turns = jnp.concatenate([turns, turns], axis=-1)
    return (jnp.cos(turns)[:, None, :], jnp.sin(turns)[:, None, :])


def turned(values):
    half = values.shape[-1] // 2
    return jnp.concatenate([-values[..., half:], values[..., :half]], axis=-1)


def masked_scores(query_block, key_rows):
    scores = (
        jnp.einsum("qkgd,skd->kgqs", query_block, key_rows, preferred_element_type=F32)
        / query_block.shape[-1]
    )
    causal = jnp.arange(query_block.shape[0])[:, None] >= jnp.arange(key_rows.shape[0])[None, :]
    return jnp.where(causal, scores, MASK_VALUE)


def norm_back(grad_normed, values, factor, gain):
    scaled = grad_normed * gain
    mean_term = jnp.mean(scaled * values, axis=-1, keepdims=True)
    grad_values = factor * scaled - values * factor * factor * factor * mean_term
    grad_gain = jnp.sum(grad_normed * values * factor, axis=0)
    return (grad_values, grad_gain)


def slot_matrices(routes, route_gates):
    named = (routes[:, :, None] == jnp.arange(EXPERTS, dtype=jnp.int32)).astype(F32)
    uses = jnp.sum(named, axis=1)
    gates = jnp.sum(named * route_gates[:, :, None], axis=1)
    row = lax.broadcasted_iota(jnp.int32, (TOK, TOK), 0)
    column = lax.broadcasted_iota(jnp.int32, (TOK, TOK), 1)
    earlier = (row > column).astype(BF16)
    ranks = jnp.dot(earlier, uses.astype(BF16), preferred_element_type=F32)
    slot = jnp.arange(SLOTS, dtype=jnp.int32)
    spread = (jnp.arange(EXPERTS, dtype=jnp.int32)[:, None] == slot[None, :] // CAP).astype(F32)
    both = jnp.where(uses > 0.5, ranks, -1.0).astype(BF16)
    flat = jnp.dot(both, spread.astype(BF16), preferred_element_type=F32)
    hits = flat == (slot % CAP).astype(F32)[None, :]
    flat_gates = jnp.dot(gates, spread, precision=lax.Precision.HIGHEST)
    weights = jnp.where(hits, RESIDUAL * flat_gates, 0.0)
    return (named, spread, hits.astype(BF16), weights)


def to_group(rows):
    blocks = rows.reshape(EXPERTS, CAP, MODEL_WIDTH)
    return lax.all_to_all(blocks, ("z", "seq"), 0, 0, tiled=True).reshape(SLOTS, MODEL_WIDTH)


def shards(
    layer_in, norm_one, w_query, key_weight, value_weight, w_output, norm_two,
    w_gate, w_up, w_down, routes, route_gates, cotangent,
):
    seq = lax.axis_index("seq")
    core = seq % 2
    key_value_resident = KEY_VALUE_HEADS // 4
    group_width = QUERY_HEADS // KEY_VALUE_HEADS
    head_width = key_value_resident * group_width * HEAD_SIZE
    kv_width = key_value_resident * HEAD_SIZE

    gains = jnp.pad(jnp.stack([norm_one, norm_two], axis=1), ((0, 0), (0, 126)))
    heads_block = jnp.concatenate(
        [
            lax.dynamic_slice_in_dim(w_query, seq * head_width, head_width, 1),
            lax.dynamic_slice_in_dim(key_weight, seq * kv_width, kv_width, 1),
            lax.dynamic_slice_in_dim(value_weight, seq * kv_width, kv_width, 1),
            gains,
        ],
        axis=1,
    )
    branch_block = lax.dynamic_slice_in_dim(w_output, core * 512, 512, 1)
    expert_block = jnp.stack(
        [
            lax.dynamic_index_in_dim(w.reshape(32, 4, 4, FF), seq, 2, keepdims=False)
            for w in (w_gate, w_up, w_down)
        ]
    ).transpose(2, 0, 1, 3)
    named, spread, hits, weights = slot_matrices(routes, route_gates)
    slot_weights = jnp.sum(weights, axis=0)
    grad_slots = (
        jnp.einsum("tj,td->jd", hits, cotangent, preferred_element_type=F32)
        * slot_weights[:, None]
    ).astype(BF16).reshape(EXPERTS, CAP, MODEL_WIDTH)

    heads_w, branch_w, tokens_all, gate_w, rest_w, grad_back = remote_call(
        gather_kernel,
        (heads_block, branch_block, layer_in, expert_block, grad_slots),
        (
            (2, 4, 4, 32, 640),
            (2, 2, 4, 4, 32, 512),
            (2, 2, TOK, MODEL_WIDTH),
            (2, 4, 4, 32, FF),
            (2, 2, 4, 32, FF),
            (EXPERTS, CAP, MODEL_WIDTH),
        ),
        48,
        6,
        1,
        "gather_all",
    )
    heads_w = heads_w.reshape(MODEL_WIDTH, 640)
    gain_first = heads_w[:, 512].astype(F32)
    gain_second = heads_w[:, 513].astype(F32)
    heads_w = heads_w[:, :512]
    branch_w = branch_w.reshape(2, MODEL_WIDTH, 512)
    gate_w = gate_w.reshape(MODEL_WIDTH, FF)
    grad_back = grad_back.reshape(SLOTS, MODEL_WIDTH)

    sequence = tokens_all.reshape(SEQ_LEN, MODEL_WIDTH).astype(F32)
    factor_all = lax.rsqrt(jnp.mean(sequence * sequence, axis=-1, keepdims=True) + EPSILON)
    normed_all = (sequence * factor_all * gain_first).astype(BF16)
    cosine, sine = angles(SEQ_LEN, HEAD_SIZE)
    projected = jnp.dot(normed_all, heads_w, preferred_element_type=F32)
    query_pre = projected[:, :head_width].reshape(SEQ_LEN, -1, HEAD_SIZE)
    key_pre = projected[:, head_width : head_width + kv_width].reshape(SEQ_LEN, -1, HEAD_SIZE)
    query_all = (query_pre * cosine + turned(query_pre) * sine).astype(BF16)
    query_all = query_all.reshape(SEQ_LEN, key_value_resident, group_width, HEAD_SIZE)
    key_all = (key_pre * cosine + turned(key_pre) * sine).astype(BF16)
    value_all = projected[:, head_width + kv_width :].astype(BF16)
    value_all = value_all.reshape(SEQ_LEN, key_value_resident, HEAD_SIZE)
    scores = masked_scores(query_all, key_all)
    top_score = jnp.max(scores, axis=-1, keepdims=True)
    exponent = jnp.exp(scores - top_score)
    total_mass = jnp.sum(exponent, axis=-1, keepdims=True)
    probs = (exponent / total_mass).astype(BF16)
    log_sums = top_score + jnp.log(total_mass)
    attended = jnp.einsum("kgqs,skd->qkgd", probs, value_all, preferred_element_type=F32)
    attended = attended.reshape(SEQ_LEN, head_width).astype(BF16)
    (attended_tok,) = remote_call(
        trade_kernel, (attended.reshape(4, TOK, head_width),), ((4, TOK, head_width),), 3, 1, 4, "trade_heads"
    )
    attended_tok = attended_tok.transpose(1, 0, 2).reshape(TOK, MODEL_WIDTH)

    inputs = layer_in.astype(F32)
    branch = jnp.concatenate(
        [jnp.dot(attended_tok, branch_w[k], preferred_element_type=F32) for k in range(2)], axis=1
    )
    middle = inputs + RESIDUAL * branch
    factor_two = lax.rsqrt(jnp.mean(middle * middle, axis=-1, keepdims=True) + EPSILON)
    normed_two = (middle * factor_two * gain_second).astype(BF16)
    slot_rows = jnp.einsum("tj,td->jd", hits, normed_two, preferred_element_type=F32).astype(BF16)
    expert_rows, rest_w = remote_call(
        dispatch_kernel,
        (slot_rows.reshape(EXPERTS, CAP, MODEL_WIDTH), rest_w),
        ((EXPERTS, CAP, MODEL_WIDTH), (2, 2, 4, 4, 32, FF)),
        18,
        2,
        7,
        "dispatch_rows",
    )
    expert_rows = expert_rows.reshape(SLOTS, MODEL_WIDTH)
    up_w = rest_w[0].reshape(MODEL_WIDTH, FF)
    down_w = rest_w[1].reshape(MODEL_WIDTH, FF)

    step = SLOTS // 3
    wide = pl.BlockSpec((step, MODEL_WIDTH), lambda i: (i, 0))
    narrow = pl.BlockSpec((step, FF), lambda i: (i, 0))
    weight = pl.BlockSpec((MODEL_WIDTH, FF), lambda i: (0, 0))
    grad_rows, returned, active, grad_gate, grad_up = pl.pallas_call(
        expert_kernel,
        grid=(3,),
        out_shape=(jax.ShapeDtypeStruct((SLOTS, MODEL_WIDTH), BF16),) * 2
        + (jax.ShapeDtypeStruct((SLOTS, FF), BF16),) * 3,
        in_specs=[wide, wide, weight, weight, weight],
        out_specs=(wide, wide, narrow, narrow, narrow),
        compiler_params=pltpu.CompilerParams(vmem_limit_bytes=48 * 2**20),
        name="expert_rows",
    )(expert_rows, grad_back, gate_w, up_w, down_w)
    grad_rows = to_group(grad_rows)
    half = pl.BlockSpec((SLOTS, 512), lambda i: (0, i))
    whole = pl.BlockSpec((SLOTS, FF), lambda i: (0, 0))
    expert_grads = pl.pallas_call(
        expert_grad_kernel,
        grid=(2,),
        out_shape=jax.ShapeDtypeStruct((4, 2, TOK, 3 * FF), BF16),
        in_specs=[half, half, whole, whole, whole],
        out_specs=pl.BlockSpec((4, 1, TOK, 3 * FF), lambda i: (0, i, 0, 0)),
        compiler_params=pltpu.CompilerParams(vmem_limit_bytes=48 * 2**20),
        name="expert_grads",
    )(expert_rows, grad_back, active, grad_gate, grad_up)
    x_place = lax.axis_index("x")
    x_parts = [lax.dynamic_index_in_dim(expert_grads, x_place, 0, keepdims=False)]
    for k in (1, 2, 3):
        block = lax.dynamic_index_in_dim(expert_grads, (x_place + k) % 4, 0, keepdims=False)
        x_parts.append(lax.ppermute(block, "x", [(i, (i + k) % 4) for i in range(4)]))

    grad_out = cotangent.astype(F32)
    grad_normed_two = jnp.dot(hits, grad_rows, preferred_element_type=F32)
    grad_middle_norm, gain_two_term = norm_back(grad_normed_two, middle, factor_two, gain_second)
    grad_middle = grad_out + grad_middle_norm
    grad_branch = (RESIDUAL * grad_middle).astype(BF16)
    (grad_branch_all,) = remote_call(
        spread_kernel, (grad_branch,), ((2, 2, TOK, MODEL_WIDTH),), 3, 1, 5, "spread_branch"
    )
    returned, grad_branch_all = lax.optimization_barrier((returned, grad_branch_all))
    returned = to_group(returned)
    grad_branch_all = grad_branch_all.reshape(SEQ_LEN, MODEL_WIDTH)
    branch_rows = lax.dynamic_slice_in_dim(branch_w, seq * head_width, head_width, 1)
    output_term = jnp.einsum(
        "th,td->hd", attended, grad_branch_all, preferred_element_type=F32
    ).astype(BF16)
    grad_heads = (
        jnp.einsum("td,hd->th", grad_branch_all[:, :512], branch_rows[0], preferred_element_type=F32)
        + jnp.einsum(
            "td,hd->th", grad_branch_all[:, 512:], branch_rows[1], preferred_element_type=F32
        )
    ).astype(BF16)

    scores = masked_scores(query_all, key_all)
    probs = jnp.exp(scores - log_sums)
    grad_block = grad_heads.reshape(SEQ_LEN, key_value_resident, group_width, HEAD_SIZE)
    grad_probs = jnp.einsum("qkgd,skd->kgqs", grad_block, value_all, preferred_element_type=F32)
    grad_value = jnp.einsum(
        "kgqs,qkgd->skd", probs.astype(BF16), grad_block, preferred_element_type=F32
    )
    inner = jnp.sum(probs * grad_probs, axis=-1, keepdims=True)
    grad_scores = (probs * (grad_probs - inner)).astype(BF16)
    grad_query = (
        jnp.einsum("kgqs,skd->qkgd", grad_scores, key_all, preferred_element_type=F32) / HEAD_SIZE
    ).reshape(SEQ_LEN, -1, HEAD_SIZE)
    grad_key = (
        jnp.einsum("kgqs,qkgd->skd", grad_scores, query_all, preferred_element_type=F32) / HEAD_SIZE
    )
    grad_query = grad_query.astype(BF16).astype(F32)
    grad_key = grad_key.astype(BF16).astype(F32)
    grad_projected = jnp.concatenate(
        [
            (grad_query * cosine - turned(grad_query) * sine).reshape(SEQ_LEN, -1).astype(BF16),
            (grad_key * cosine - turned(grad_key) * sine).reshape(SEQ_LEN, -1).astype(BF16),
            grad_value.reshape(SEQ_LEN, -1).astype(BF16),
        ],
        axis=1,
    )
    heads_term = jnp.einsum(
        "td,tf->df", normed_all, grad_projected, preferred_element_type=F32
    ).astype(BF16)
    grad_normed_parts = jnp.einsum(
        "tf,df->td", grad_projected, heads_w, preferred_element_type=F32
    ).astype(BF16)
    block = (TOK, MODEL_WIDTH)
    grad_normed = pl.pallas_call(
        trade_sum_kernel,
        out_shape=jax.ShapeDtypeStruct(block, F32),
        in_specs=[pl.BlockSpec(memory_space=pltpu.VMEM)],
        out_specs=pl.BlockSpec(memory_space=pltpu.VMEM),
        scratch_shapes=[
            pltpu.VMEM((2,) + block, BF16),
            pltpu.VMEM(block, F32),
            pltpu.VMEM(block, BF16),
            pltpu.VMEM(block, BF16),
            pltpu.SemaphoreType.DMA((3,)),
            pltpu.SemaphoreType.DMA((3,)),
        ],
        compiler_params=pltpu.CompilerParams(
            collective_id=6, has_side_effects=True, vmem_limit_bytes=16 * 2**20
        ),
        name="trade_normed",
    )(grad_normed_parts.reshape(2, 2, TOK, MODEL_WIDTH))
    x_parts, heads_term, grad_normed, returned = lax.optimization_barrier(
        (x_parts, heads_term, grad_normed, returned)
    )
    expert_grads = (
        x_parts[0].astype(F32) + x_parts[1].astype(F32)
        + x_parts[2].astype(F32) + x_parts[3].astype(F32)
    ).astype(BF16)
    factor_one = lax.rsqrt(jnp.mean(inputs * inputs, axis=-1, keepdims=True) + EPSILON)
    grad_input_norm, gain_one_term = norm_back(grad_normed, inputs, factor_one, gain_first)
    grad_input = (grad_middle + grad_input_norm).astype(BF16)

    gain_terms = jnp.pad(
        jnp.stack([gain_one_term, gain_two_term], axis=1).astype(BF16), ((0, 0), (0, 126))
    )
    heads_term = jnp.concatenate([heads_term, gain_terms], axis=1).reshape(32, 32, 640)
    any_place, vmem = pl.BlockSpec(memory_space=pl.ANY), pl.BlockSpec(memory_space=pltpu.VMEM)
    heads_four, branch_four, expert_four = pl.pallas_call(
        finish_kernel,
        out_shape=(
            jax.ShapeDtypeStruct((2, 2, 32, 640), BF16),
            jax.ShapeDtypeStruct((4, 16, 512), BF16),
            jax.ShapeDtypeStruct((2, 2, 4, 32, 3 * FF), BF16),
        ),
        in_specs=[vmem] * 3,
        out_specs=(any_place,) * 3,
        scratch_shapes=[
            pltpu.VMEM((3, 2, 4, 32, 640), BF16),
            pltpu.VMEM((3, 2, 32, MODEL_WIDTH), BF16),
            pltpu.VMEM((2, 4, 32, 640), BF16),
            pltpu.VMEM((2, 4, 16, 512), BF16),
            pltpu.VMEM((7, 32, 640), BF16),
            pltpu.VMEM((7, 16, 512), BF16),
            pltpu.VMEM((2, 4, 32, 3 * FF), BF16),
            pltpu.VMEM((32, 640), BF16),
            pltpu.VMEM((16, 512), BF16),
            pltpu.VMEM((4, 32, 3 * FF), BF16),
            pltpu.SemaphoreType.DMA((33,)),
            pltpu.SemaphoreType.DMA((33,)),
            pltpu.SemaphoreType.DMA((2,)),
            pltpu.SemaphoreType.DMA((4,)),
            pltpu.SemaphoreType.DMA((4,)),
        ],
        compiler_params=pltpu.CompilerParams(
            collective_id=2, has_side_effects=True, vmem_limit_bytes=32 * 2**20
        ),
        name="finish",
    )(
        heads_term.reshape(2, 4, 4, 32, 640),
        output_term.reshape(2, 4, 32, MODEL_WIDTH),
        expert_grads.reshape(2, 4, 32, 3 * FF),
    )
    layer_out = (
        middle + jnp.dot(weights.astype(BF16), returned, preferred_element_type=F32)
    ).astype(BF16)
    pair_dots = jnp.einsum("td,jd->tj", cotangent, returned, preferred_element_type=F32)
    expert_dots = jnp.einsum(
        "tj,ej->te", pair_dots * hits.astype(F32), spread, precision=lax.Precision.HIGHEST
    )
    grad_gates = RESIDUAL * jnp.sum(named * expert_dots[:, None, :], axis=-1)
    gain_sums = jnp.sum(heads_four[:, :, :, 512:514].astype(F32), axis=(0, 1))
    projections = pl.pallas_call(
        unpack_kernel,
        out_shape=tuple(
            jax.ShapeDtypeStruct(shape, F32)
            for shape in ((32, 1024), (32, 512), (32, 512), (32, 1024)) + ((32, EXPERTS, FF),) * 3
        ),
        in_specs=[vmem] * 3,
        out_specs=(vmem,) * 7,
        compiler_params=pltpu.CompilerParams(vmem_limit_bytes=16 * 2**20),
        name="unpack",
    )(heads_four, branch_four, expert_four)
    experts_out = projections[4:]
    return (
        layer_out,
        grad_input,
        gain_sums[:, 0],
        projections[0],
        projections[1],
        projections[2],
        projections[3],
        gain_sums[:, 1],
        experts_out[0],
        experts_out[1],
        experts_out[2],
        grad_gates,
    )


def solution(mesh):
    dp = ("yh", "x", "z")
    cut = Mesh(mesh.devices.reshape(2, 4, 4, 4), AXES)
    tokens, rows, gain, experts = P(AXES, None), P(dp, None), P(dp), P(dp, None, None)
    return jax.shard_map(
        shards,
        mesh=cut,
        in_specs=(
            tokens, gain, rows, rows, rows, rows, gain, experts, experts, experts,
            tokens, tokens, tokens,
        ),
        out_specs=(
            tokens, tokens, gain, rows, rows, rows, rows, gain, experts, experts, experts, tokens,
        ),
        check_vma=False,
    )
```

```python
import jax
import jax.numpy as jnp
import numpy as np
from jax import lax
from jax.experimental import pallas as pl
from jax.experimental.pallas import tpu as pltpu
from jax.sharding import Mesh
from jax.sharding import PartitionSpec as P

MODEL_WIDTH = 1024
QUERY_HEADS = 16
KEY_VALUE_HEADS = 8
HEAD_SIZE = 64
TOP = 8
EXPERTS = 16
CAP = 72
SLOTS = EXPERTS * CAP
TOK = 128
SEQ_LEN = 512
FF = 512
EPSILON = 1e-05
RESIDUAL = 0.22
ROPE_BASE = 10000.0
MASK_VALUE = -1e30

PLACES = np.arange(SEQ_LEN, dtype=np.float32)
FREQUENCIES = (ROPE_BASE ** (-np.arange(0, HEAD_SIZE, 2) / HEAD_SIZE)).astype(np.float32)
TURNS = PLACES[:, None] * np.tile(FREQUENCIES, 4)[None, :]
COSINE = np.cos(TURNS).astype(np.float32)
SINE = np.where(np.arange(TOK) % HEAD_SIZE < 32, -np.sin(TURNS), np.sin(TURNS)).astype(np.float32)

BF16 = jnp.bfloat16
F32 = jnp.float32
AXES = ("yh", "x", "z", "seq")
BY_ID = pl.DeviceIdType.MESH


def place():
    return tuple(lax.axis_index(axis) for axis in AXES)


class Sender:
    def __init__(self, send, recv):
        self.send, self.recv, self.used, self.copies = send, recv, 0, []

    def start(self, source, target, device):
        copy = pltpu.make_async_remote_copy(
            src_ref=source,
            dst_ref=target,
            send_sem=self.send.at[self.used],
            recv_sem=self.recv.at[self.used],
            device_id=device,
            device_id_type=BY_ID,
        )
        copy.start()
        self.used += 1
        self.copies.append(copy)
        return copy

    def finish(self):
        for copy in self.copies:
            copy.wait_send()


def arrived(copies):
    for copy in copies:
        copy.wait_recv()


def greet(partners):
    barrier = pltpu.get_barrier_semaphore()
    for partner in partners:
        pl.semaphore_signal(barrier, inc=1, device_id=partner, device_id_type=BY_ID)
    pl.semaphore_wait(barrier, len(partners))


def remote_call(kernel, inputs, outputs, copies, local_copies, collective_id, name):
    return pl.pallas_call(
        kernel,
        out_shape=tuple(
            shape if isinstance(shape, jax.ShapeDtypeStruct) else jax.ShapeDtypeStruct(shape, BF16)
            for shape in outputs
        ),
        in_specs=[pl.BlockSpec(memory_space=pltpu.HBM)] * len(inputs),
        out_specs=tuple(pl.BlockSpec(memory_space=pltpu.HBM) for _ in outputs),
        scratch_shapes=[
            pltpu.SemaphoreType.DMA((copies,)),
            pltpu.SemaphoreType.DMA((copies,)),
            pltpu.SemaphoreType.DMA((local_copies,)),
        ],
        compiler_params=pltpu.CompilerParams(collective_id=collective_id, has_side_effects=True),
        name=name,
    )(*inputs)


def local_starts(pairs, sems):
    copies = []
    for index, (source, target) in enumerate(pairs):
        copy = pltpu.make_async_copy(source, target, sems.at[index])
        copy.start()
        copies.append(copy)
    return copies


def group_of(x, z, seq, yh):
    yl, core = seq // 2, seq % 2
    return [
        (yh, x, (z + k // 4) % 4, (yl + (k // 2) % 2) % 2 * 2 + (core + k % 2) % 2)
        for k in range(1, 16)
    ]


class Blocks:
    def __init__(self, sender, block, blocks_all):
        yh, x, z, seq = place()
        self.yl, self.core = seq // 2, seq % 2
        self.sender, self.z, self.blocks = sender, z, blocks_all
        self.near = (yh, x, z, (1 - self.yl) * 2 + self.core)
        self.sibling = (yh, x, z, self.yl * 2 + 1 - self.core)
        self.along_z = [(yh, x, (z + k) % 4, seq) for k in (1, 2, 3)]
        own = blocks_all.at[z, self.yl, self.core]
        self.to_near = sender.start(block, own, self.near)
        self.to_z = [sender.start(block, own, partner) for partner in self.along_z]
        self.to_sibling = [sender.start(block, own, self.sibling)]

    def again(self, ref, partner):
        return self.sender.start(ref, ref, partner)

    def forward(self):
        arrived([self.to_near])
        beside = self.blocks.at[self.z, 1 - self.yl, self.core]
        self.passed = [self.again(beside.at[pl.ds(0, 64)], partner) for partner in self.along_z]
        self.to_sibling.append(self.again(beside, self.sibling))
        for k, copy in enumerate(self.to_z):
            arrived([copy])
            block = self.blocks.at[(self.z + 3 - k) % 4, self.yl, self.core]
            self.passed.append(self.again(block.at[pl.ds(64, 64)], self.near))
            self.to_sibling.append(self.again(block, self.sibling))

    def finish(self):
        for k in range(3):
            arrived([self.passed[k], self.passed[k + 3]])
            block = self.blocks.at[(self.z + 3 - k) % 4, 1 - self.yl, self.core]
            self.to_sibling.append(self.again(block, self.sibling))
        arrived(self.to_sibling)


def gather_kernel(
    heads, branch, tokens, experts, rows, gates,
    heads_all, branch_all, tokens_all, experts_all, rows_all, gates_all,
    send, recv, local,
):
    yh, x, z, seq = place()
    yl, core = seq // 2, seq % 2
    along_y = (1 - yh, x, z, seq)
    along_x = [(yh, (x + k) % 4, z, seq) for k in (1, 2, 3)]
    along_z = [(yh, x, (z + k) % 4, seq) for k in (1, 2, 3)]
    near = (yh, x, z, (1 - yl) * 2 + core)
    sibling = (yh, x, z, yl * 2 + 1 - core)
    group = [
        (yh, x, (z + k // 4) % 4, (yl + (k // 2) % 2) % 2 * 2 + (core + k % 2) % 2)
        for k in range(1, 16)
    ]
    expert = z * 4 + seq
    greet([along_y] + along_x + group)
    sender = Sender(send, recv)
    first = [
        sender.start(heads, heads_all.at[yh, x, z], along_y),
        sender.start(branch, branch_all.at[core, yh, x, z], along_y),
    ]
    expert_first = [
        sender.start(experts.at[partner[2]], experts_all.at[:, yh, z], partner)
        for partner in along_z
    ]
    token_copies = [
        sender.start(tokens, tokens_all.at[yl, core], near),
        sender.start(tokens, tokens_all.at[yl, core], sibling),
    ]
    own = local_starts(
        [
            (heads, heads_all.at[yh, x, z]),
            (branch, branch_all.at[core, yh, x, z]),
            (experts.at[z], experts_all.at[:, yh, z]),
            (tokens, tokens_all.at[yl, core]),
            (rows, rows_all.at[z, yl, core]),
            (gates.at[expert], gates_all.at[expert]),
        ],
        local,
    )
    for copy in own[:2]:
        copy.wait()
    arrived(first)
    second = []
    for partner in along_z:
        for source in (heads_all.at[:, x, z], branch_all.at[core, :, x, z]):
            second.append(sender.start(source, source, partner))
    own[2].wait()
    arrived(expert_first)
    mine = experts_all.at[:, yh]
    expert_second = [sender.start(mine, mine, along_y)]
    arrived(second)
    third = []
    for partner in along_x:
        for source in (heads_all.at[:, x], branch_all.at[core, :, x]):
            third.append(sender.start(source, source, partner))
    blocks = Blocks(sender, rows, rows_all)
    gate_copies = [
        sender.start(gates.at[partner[2] * 4 + partner[3]], gates_all.at[expert], partner)
        for partner in group
    ]
    arrived(token_copies)
    far = tokens_all.at[1 - yl, core]
    last = [sender.start(far, far, sibling)]
    blocks.forward()
    for copy in own[3:]:
        copy.wait()
    blocks.finish()
    arrived(third)
    half = branch_all.at[core]
    last.append(sender.start(half, half, sibling))
    arrived(expert_second)
    arrived(gate_copies)
    arrived(last)
    sender.finish()


def by_rows(left, right):
    return lax.dot_general(left, right, (((0,), (0,)), ((), ())), preferred_element_type=F32)


def by_columns(left, right):
    return lax.dot_general(left, right, (((1,), (1,)), ((), ())), preferred_element_type=F32)


def half_turn(values):
    lane = lax.broadcasted_iota(jnp.int32, values.shape, 1)
    return jnp.where(lane % 64 < 32, pltpu.roll(values, 96, 1), pltpu.roll(values, 32, 1))


def causal_scores(query, key):
    row = lax.broadcasted_iota(jnp.int32, (SEQ_LEN, SEQ_LEN), 0)
    column = lax.broadcasted_iota(jnp.int32, (SEQ_LEN, SEQ_LEN), 1)
    return jnp.where(row >= column, by_columns(query, key) * (1.0 / HEAD_SIZE), MASK_VALUE)


def forward_kernel(
    tokens_in, heads_in, branch_in, cosine_in, sine_in, gates_in, out_in,
    normed_out, query_out, key_out, value_out, attended_out, sums_out, middle_out, picks_out,
    back_out, rows_all, gains,
    tokens, heads_w, branch_here, cosine, sine, gates, out_here,
    normed, query, key, value, attended, sums, middle, picks, back,
    traded, rows, send, recv, fetch, keep,
):
    yh, x, z, seq = place()
    yl, core = seq // 2, seq % 2
    along_z = [(yh, x, (z + k) % 4, seq) for k in (1, 2, 3)]
    beside = [(yh, x, z, (seq + k) % 4) for k in (1, 2, 3)]
    fetched = local_starts(
        [
            (heads_in, heads_w), (tokens_in, tokens), (cosine_in, cosine), (sine_in, sine),
            (branch_in, branch_here), (gates_in, gates), (out_in, out_here),
        ],
        fetch,
    )
    greet(along_z + beside)
    for copy in fetched[:4]:
        copy.wait()
    gains[...] = heads_w[:, 512:640].astype(F32).T[0:8]
    sequence = tokens[...].reshape(SEQ_LEN, MODEL_WIDTH).astype(F32)
    factor = lax.rsqrt(jnp.mean(sequence * sequence, axis=-1, keepdims=True) + EPSILON)
    normed[...] = (sequence * factor * gains[0:1]).astype(BF16)
    projected = jnp.dot(normed[...], heads_w[:, 0:512], preferred_element_type=F32)
    for k in range(2):
        part = projected[:, k * 128 : k * 128 + 128]
        query[:, k * 128 : k * 128 + 128] = (
            part * cosine[...] + half_turn(part) * sine[...]
        ).astype(BF16)
    part = projected[:, 256:384]
    key[...] = (part * cosine[...] + half_turn(part) * sine[...]).astype(BF16)
    value[...] = projected[:, 384:512].astype(BF16)
    lane = lax.broadcasted_iota(jnp.int32, (SEQ_LEN, TOK), 1)
    all_sums = jnp.zeros((SEQ_LEN, TOK), F32)
    for k in range(2):
        results = []
        key_head, value_head = key[:, k * 64 : k * 64 + 64], value[:, k * 64 : k * 64 + 64]
        for g in range(2):
            head = k * 2 + g
            scores = causal_scores(query[:, head * 64 : head * 64 + 64], key_head)
            top = jnp.max(scores, axis=-1, keepdims=True)
            exponent = jnp.exp(scores - top)
            total = jnp.sum(exponent, axis=-1, keepdims=True)
            probs = (exponent / total).astype(BF16)
            all_sums = jnp.where(lane == head, top + jnp.log(total), all_sums)
            results.append(jnp.dot(probs, value_head, preferred_element_type=F32))
        attended[:, k * 128 : k * 128 + 128] = jnp.concatenate(results, axis=1).astype(BF16)
    sums[...] = all_sums

    sender = Sender(send, recv)
    trades = []
    for partner in beside:
        start = pl.multiple_of(partner[3] * TOK, TOK)
        trades.append(sender.start(attended.at[pl.ds(start, TOK)], traded.at[seq], partner))
    traded[seq] = attended[pl.ds(pl.multiple_of(seq * TOK, TOK), TOK), :]
    kept = local_starts(
        [
            (normed, normed_out), (query, query_out), (key, key_out), (value, value_out),
            (attended, attended_out), (sums, sums_out),
        ],
        keep,
    )
    fetched[4].wait()
    arrived(trades)
    here = jnp.concatenate([traded[k] for k in range(4)], axis=1)
    branch = jnp.concatenate(
        [jnp.dot(here, branch_here[k], preferred_element_type=F32) for k in range(2)], axis=1
    )
    mid = tokens[seq].astype(F32) + RESIDUAL * branch
    middle[...] = mid
    factor = lax.rsqrt(jnp.mean(mid * mid, axis=-1, keepdims=True) + EPSILON)
    rows[...] = (mid * factor * gains[1:2]).astype(BF16)

    blocks = Blocks(sender, rows, rows_all)
    for index, (source, target) in enumerate(
        ((rows, rows_all.at[z, yl, core]), (middle, middle_out))
    ):
        kept.append(pltpu.make_async_copy(source, target, keep.at[6 + index]))
        kept[-1].start()
    for copy in fetched[5:]:
        copy.wait()
    row = lax.broadcasted_iota(jnp.int32, (TOK, TOK), 0)
    column = lax.broadcasted_iota(jnp.int32, (TOK, TOK), 1)
    earlier = jnp.where(row < column, 1.0, 0.0).astype(BF16)
    slot = lax.broadcasted_iota(jnp.int32, (CAP, TOK), 0).astype(F32)

    def two(index, carry):
        parts = []
        for j in range(2):
            gate = gates[index * 2 + j]
            named = jnp.where(gate > 0.0, 1.0, 0.0)
            ranks = jnp.dot(named.astype(BF16), earlier, preferred_element_type=F32)
            place_in = jnp.where(named > 0.5, ranks, -1.0)[0:1]
            hit = jnp.where(slot == place_in, 1.0, 0.0)
            pick = hit.astype(BF16)
            picks[index * 2 + j] = pick
            weight = jnp.sum(hit * gate[0:1], axis=1, keepdims=True)
            chosen = jnp.dot(pick, out_here[index * 2 + j], preferred_element_type=F32)
            parts.append(chosen * (RESIDUAL * weight))
        start = pl.multiple_of(index * (2 * CAP), 2 * CAP)
        back[pl.ds(start, 2 * CAP), :] = jnp.concatenate(parts, axis=0).astype(BF16)
        return carry

    lax.fori_loop(0, 4, two, 0)
    blocks.forward()
    lax.fori_loop(4, 8, two, 0)
    for index, (source, target) in enumerate(((picks, picks_out), (back, back_out))):
        kept.append(pltpu.make_async_copy(source, target, keep.at[8 + index]))
        kept[-1].start()
    blocks.finish()
    for copy in kept:
        copy.wait()
    sender.finish()


def backward_kernel(
    block, returned, branch_w,
    attended_in, query_in, key_in, value_in, sums_in, normed_in, heads_in, cosine_in, sine_in,
    grad_normed, heads_term, branch_total, returned_all,
    attended, query, key, value, sums, normed, heads_w, cosine, sine,
    branch_here, blocks_all, output_term, parts,
    arriving, paired, outgoing, incoming, branch_z, branch_out, branch_plane, send, recv, local,
):
    yh, x, z, seq = place()
    yl, core = seq // 2, seq % 2
    expert = z * 4 + seq
    near = (yh, x, z, (1 - yl) * 2 + core)
    sibling = (yh, x, z, yl * 2 + 1 - core)
    along_z = [(yh, x, (z + k) % 4, seq) for k in (1, 2, 3)]
    plane = [((yh + k // 4) % 2, (x + k % 4) % 4, z, seq) for k in range(1, 8)]
    group = [
        (yh, x, (z + k // 4) % 4, (yl + (k // 2) % 2) % 2 * 2 + (core + k % 2) % 2)
        for k in range(1, 16)
    ]
    rows = pl.ds(pl.multiple_of(seq * 256, 256), 256)
    fetched = local_starts(
        [
            (branch_w.at[:, rows], branch_here),
            (attended_in, attended), (query_in, query), (key_in, key), (value_in, value),
            (sums_in, sums), (normed_in, normed), (heads_in, heads_w),
            (cosine_in, cosine), (sine_in, sine),
            (returned.at[0, expert], returned_all.at[expert]),
        ],
        local,
    )
    greet(group + plane)
    sender = Sender(send, recv)
    first = [
        sender.start(block, blocks_all.at[yl, core], near),
        sender.start(block, blocks_all.at[yl, core], sibling),
    ]
    blocks_all[yl, core] = block[...]
    arrived(first[:1])
    far = blocks_all.at[1 - yl, core]
    last = sender.start(far, far, sibling)
    row_copies = [
        sender.start(returned.at[0, partner[2] * 4 + partner[3]], returned_all.at[expert], partner)
        for partner in group
    ]
    for copy in fetched[:10]:
        copy.wait()
    arrived(first[1:])
    arrived([last])
    branch_all = blocks_all[...].reshape(SEQ_LEN, MODEL_WIDTH)
    output_term[...] = by_rows(attended[...], branch_all).astype(BF16).reshape(8, 2, 16, MODEL_WIDTH)

    def branch_block(place_z):
        left = pl.multiple_of(place_z % 2 * 512, 512)
        return output_term.at[:, place_z // 2, :, pl.ds(left, 512)]

    around = [
        sender.start(branch_block(partner[2]), branch_z.at[k], partner)
        for k, partner in enumerate(along_z)
    ]
    grad_heads = (
        by_columns(branch_all[:, :512], branch_here[0])
        + by_columns(branch_all[:, 512:], branch_here[1])
    ).astype(BF16)
    lane = lax.broadcasted_iota(jnp.int32, (SEQ_LEN, TOK), 1)
    grad_queries, grad_keys, grad_values = [], [], []
    for k in range(2):
        key_head, value_head = key[:, k * 64 : k * 64 + 64], value[:, k * 64 : k * 64 + 64]
        grad_key, grad_value = 0.0, 0.0
        for g in range(2):
            head = k * 2 + g
            query_head = query[:, head * 64 : head * 64 + 64]
            grad_head = grad_heads[:, head * 64 : head * 64 + 64]
            log_sum = jnp.sum(jnp.where(lane == head, sums[...], 0.0), axis=-1, keepdims=True)
            probs = jnp.exp(causal_scores(query_head, key_head) - log_sum)
            grad_probs = by_columns(grad_head, value_head)
            inner = jnp.sum(probs * grad_probs, axis=-1, keepdims=True)
            grad_scores = (probs * (grad_probs - inner)).astype(BF16)
            grad_value += by_rows(probs.astype(BF16), grad_head)
            grad_key += by_rows(grad_scores, query_head)
            grad_queries.append(
                jnp.dot(grad_scores, key_head, preferred_element_type=F32) * (1.0 / HEAD_SIZE)
            )
        grad_keys.append(grad_key * (1.0 / HEAD_SIZE))
        grad_values.append(grad_value)

    def unturn(pair):
        values = jnp.concatenate(pair, axis=1).astype(BF16).astype(F32)
        return (values * cosine[...] - half_turn(values) * sine[...]).astype(BF16)

    projected = jnp.concatenate(
        [
            unturn(grad_queries[:2]),
            unturn(grad_queries[2:]),
            unturn(grad_keys),
            jnp.concatenate(grad_values, axis=1).astype(BF16),
        ],
        axis=1,
    )
    parts[...] = by_columns(projected, heads_w[:, 0:512]).astype(BF16).reshape(2, 2, TOK, MODEL_WIDTH)
    second = [
        sender.start(parts.at[1 - yl, 1 - core], arriving.at[0], sibling),
        sender.start(parts.at[yl, 1 - core], arriving.at[1], sibling),
    ]
    arrived(around)
    mine = branch_block(z)[...]
    branch_out[...] = gather_sums([mine] + [branch_z[k] for k in range(3)]).astype(BF16)
    across = [
        sender.start(branch_out.at[partner[0] * 4 + partner[1]], branch_plane.at[k], partner)
        for k, partner in enumerate(plane)
    ]
    arrived(second[:1])
    outgoing[...] = gather_sums([parts[1 - yl, core], arriving[0]]).astype(BF16)
    third = sender.start(outgoing, incoming, near)
    heads_term[...] = by_rows(normed[...], projected).astype(BF16)
    arrived(second[1:])
    paired[...] = gather_sums([parts[yl, core], arriving[1]])
    arrived(across)
    branch_total[...] = gather_sums(
        [branch_out[yh * 4 + x]] + [branch_plane[k] for k in range(7)]
    ).astype(BF16)
    arrived([third])
    grad_normed[...] = paired[...] + incoming[...].astype(F32)
    fetched[10].wait()
    arrived(row_copies)
    sender.finish()


def gather_sums(parts):
    total = parts[0].astype(F32)
    for part in parts[1:]:
        total = total + part.astype(F32)
    return total


def finish_kernel(
    heads, branch_sum, experts, rows,
    heads_four, branch_four, experts_four, rows_all,
    upper_in, lower_in, upper_out, lower_out, upper_plane, lower_plane, experts_plane,
    heads_sum, experts_sum,
    send, recv, local, branch_sends, branch_recvs,
):
    yh, x, z, seq = place()
    yl, core = seq // 2, seq % 2
    dp = yh * 16 + x * 4 + z
    near = (yh, x, z, (1 - yl) * 2 + core)
    sibling = (yh, x, z, yl * 2 + 1 - core)
    along_x = [(yh, (x + k) % 4, z, seq) for k in (1, 2, 3)]
    along_z = [(yh, x, (z + k) % 4, seq) for k in (1, 2, 3)]
    plane = [((yh + k // 4) % 2, x, (z + k % 4) % 4, seq) for k in range(1, 8)]
    group = [
        (yh, x, (z + k // 4) % 4, (yl + (k // 2) % 2) % 2 * 2 + (core + k % 2) % 2)
        for k in range(1, 16)
    ]
    expert = z * 4 + seq
    other_plane = [((yh + k // 4) % 2, (x + k % 4) % 4, z, seq) for k in range(1, 8)]
    owner = seq * 8 + dp // 4
    source_seq = dp // 8
    slot = dp % 4
    here = owner == dp
    barrier = pltpu.get_barrier_semaphore()
    for partner in group + along_x + plane[3:] + other_plane[4:]:
        pl.semaphore_signal(barrier, inc=1, device_id=partner, device_id_type=BY_ID)
    for k in range(4):
        maker = dp % 8 * 4 + k
        foreign = jnp.logical_or(maker != dp, source_seq != seq)

        @pl.when(foreign)
        def _():
            pl.semaphore_signal(
                barrier,
                inc=1,
                device_id=(maker // 16, maker // 4 % 4, maker % 4, source_seq),
                device_id_type=BY_ID,
            )

    pl.semaphore_wait(barrier, 29 - here.astype(jnp.int32))
    sender = Sender(send, recv)
    upper, lower = pl.ds(0, 16), pl.ds(16, 16)
    first = []
    for k in range(3):
        partner = along_x[k]
        first.append(sender.start(heads.at[:, partner[1], :, upper], upper_in.at[k], partner))
        partner = along_z[k]
        first.append(sender.start(heads.at[:, :, partner[2], lower], lower_in.at[k], partner))
    place_of = branch_four.at[slot]

    def branch_copy(k):
        return pltpu.make_async_remote_copy(
            src_ref=branch_sum,
            dst_ref=place_of,
            send_sem=branch_sends.at[k],
            recv_sem=branch_recvs.at[slot],
            device_id=(owner // 16, owner // 4 % 4, owner % 4, k),
            device_id_type=BY_ID,
        )

    for k in range(4):
        self_copy = jnp.logical_and(here, seq == k)

        @pl.when(jnp.logical_not(self_copy))
        def _():
            branch_copy(k).start()

        @pl.when(self_copy)
        def _():
            pltpu.make_async_copy(branch_sum, place_of, branch_recvs.at[slot]).start()

    across = [
        sender.start(experts.at[partner[0], partner[2]], experts_plane.at[yh, z], partner)
        for partner in plane
    ]
    row_copies = [
        sender.start(rows.at[1, partner[2] * 4 + partner[3]], rows_all.at[expert], partner)
        for partner in group
    ]
    own_rows = pltpu.make_async_copy(rows.at[1, expert], rows_all.at[expert], local.at[2])
    own_rows.start()
    arrived(first)
    for y in range(2):
        for j in range(4):
            upper_out[y, j] = gather_sums(
                [heads[y, x, j, 0:16]] + [upper_in[k, y, j] for k in range(3)]
            ).astype(BF16)
            lower_out[y, j] = gather_sums(
                [heads[y, j, z, 16:32]] + [lower_in[k, y, j] for k in range(3)]
            ).astype(BF16)
    second = []
    for k in range(7):
        partner = plane[k]
        second.append(sender.start(upper_out.at[partner[0], partner[2]], upper_plane.at[k], partner))
        partner = other_plane[k]
        second.append(sender.start(lower_out.at[partner[0], partner[1]], lower_plane.at[k], partner))
    arrived(across)
    for j in range(4):
        @pl.when(z == j)
        def _():
            experts_sum[j] = gather_sums([experts[yh, j], experts_plane[1 - yh, j]]).astype(BF16)

        @pl.when(z != j)
        def _():
            experts_sum[j] = gather_sums([experts_plane[0, j], experts_plane[1, j]]).astype(BF16)

    third = []
    for partner in (near, sibling):
        third.append(sender.start(experts_sum, experts_four.at[yl, core], partner))
    own = local_starts([(experts_sum, experts_four.at[yl, core])], local)
    arrived(second)
    heads_sum[0:16] = gather_sums(
        [upper_out[yh, z]] + [upper_plane[k] for k in range(7)]
    ).astype(BF16)
    heads_sum[16:32] = gather_sums(
        [lower_out[yh, x]] + [lower_plane[k] for k in range(7)]
    ).astype(BF16)
    fourth = []
    for partner in (near, sibling):
        fourth.append(sender.start(heads_sum, heads_four.at[yl, core], partner))
    own_heads = pltpu.make_async_copy(heads_sum, heads_four.at[yl, core], local.at[1])
    own_heads.start()
    arrived(third[:1])
    far = experts_four.at[1 - yl, core]
    last = [sender.start(far, far, sibling)]
    arrived(fourth[:1])
    far = heads_four.at[1 - yl, core]
    last.append(sender.start(far, far, sibling))
    arrived(third[1:])
    arrived(fourth[1:])
    own[0].wait()
    own_heads.wait()
    own_rows.wait()
    arrived(row_copies)
    arrived(last)
    for k in range(4):
        pltpu.make_async_copy(branch_sum, branch_four.at[k], branch_recvs.at[k]).wait()
        self_copy = jnp.logical_and(here, seq == k)

        @pl.when(jnp.logical_not(self_copy))
        def _():
            branch_copy(k).wait_send()

    sender.finish()


def unpack_kernel(heads, branch, experts, query, key, value, output, gate, up, down):
    for s in range(4):
        block = heads[s // 2, s % 2].astype(F32)
        query[:, s * 256 : s * 256 + 256] = block[:, :256]
        key[:, s * 128 : s * 128 + 128] = block[:, 256:384]
        value[:, s * 128 : s * 128 + 128] = block[:, 384:512]
        rows, columns = s // 2 * 16, s % 2 * 512
        output[rows : rows + 16, columns : columns + 512] = branch[s].astype(F32)
        for j in range(4):
            block = experts[s // 2, s % 2, j].astype(F32)
            for index, result in enumerate((gate, up, down)):
                result[:, j * 4 + s, :] = block[:, index * 512 : index * 512 + 512]


def expert_kernel(
    rows_all, picks_in, back_in, own_w, first_w, second_w, third_w,
    grad_rows, returned_out, expert_grads_out,
    picks, back, returned, expert_grads,
    rows_here, weights, outgoing, chosen, active, by_gate, by_up, send, recv, local,
):
    yh, x, z, seq = place()
    expert = z * 4 + seq
    turns = (2, 1, 3, 0)
    offsets = [(turn, k) for turn in turns for k in range(4) if turn + k > 0]
    partners = [(yh, x, (z + turn) % 4, (seq + k) % 4) for turn, k in offsets]
    fetches = local_starts(
        [
            (part, weights.at[:, :, (x + 4 - k) % 4])
            for k, part in enumerate((own_w, first_w, second_w, third_w))
        ]
        + [(rows_all.at[(z + turn) % 4], rows_here.at[turn]) for turn in turns]
        + [(picks_in, picks), (back_in, back)],
        local,
    )
    greet(partners)
    sender = Sender(send, recv)
    for copy in fetches[:4] + fetches[8:]:
        copy.wait()
    gate_w, up_w, down_w = (weights[k].reshape(MODEL_WIDTH, FF) for k in range(3))
    for index, turn in enumerate(turns):
        fetches[4 + index].wait()
        first = (z + turn) % 4 * 4
        rows = jnp.concatenate(
            [
                jnp.dot(picks[first + j], rows_here[turn, j], preferred_element_type=F32)
                for j in range(4)
            ],
            axis=0,
        ).astype(BF16)
        span = pl.ds(index * 288, 288)
        chosen[span, :] = rows
        gate_pre = jnp.dot(rows, gate_w, preferred_element_type=F32)
        up_pre = jnp.dot(rows, up_w, preferred_element_type=F32)
        back_rows = back[pl.ds(pl.multiple_of(first * CAP, 288), 288), :]
        grad_active = jnp.dot(back_rows, down_w, preferred_element_type=F32)
        sigmoid_gate = jax.nn.sigmoid(gate_pre)
        silu = gate_pre * sigmoid_gate
        slope = sigmoid_gate * (1.0 + gate_pre * (1.0 - sigmoid_gate))
        grad_gate = (grad_active * up_pre * slope).astype(BF16)
        grad_up = (grad_active * silu).astype(BF16)
        by_gate[span, :] = grad_gate
        by_up[span, :] = grad_up
        active[span, :] = (silu * up_pre).astype(BF16)
        result = by_columns(grad_gate, gate_w) + by_columns(grad_up, up_w)
        for j in range(4):
            outgoing[first + j] = result[j * CAP : j * CAP + CAP].astype(BF16)
        for partner, offset in zip(partners, offsets):
            if offset[0] == turn:
                block = partner[2] * 4 + partner[3]
                sender.start(outgoing.at[block], grad_rows.at[expert], partner)
    kept = [pltpu.make_async_copy(outgoing.at[expert], grad_rows.at[expert], local.at[10])]
    kept[0].start()
    for index, turn in enumerate(turns):
        first = (z + turn) % 4 * 4
        result = by_columns(active[pl.ds(index * 288, 288), :], down_w)
        for j in range(4):
            piece = result[j * CAP : j * CAP + CAP].astype(BF16)
            returned[0, first + j], returned[1, first + j] = piece[:, :512], piece[:, 512:]
    kept.append(pltpu.make_async_copy(returned, returned_out, local.at[11]))
    kept[-1].start()
    for part in range(2):
        columns = pl.ds(part * 512, 512)
        for index, right in enumerate((by_gate, by_up)):
            total = by_rows(chosen[:, columns], right[...]).astype(BF16)
            expert_grads[:, part, :, index * 512 : index * 512 + 512] = total.reshape(4, TOK, 512)
        total = 0.0
        for index, turn in enumerate(turns):
            start = pl.multiple_of((z + turn) % 4 * 288, 288)
            total += by_rows(
                back[pl.ds(start, 288), columns], active[pl.ds(index * 288, 288), :]
            )
        expert_grads[:, part, :, 1024:1536] = total.astype(BF16).reshape(4, TOK, 512)
    kept.append(pltpu.make_async_copy(expert_grads, expert_grads_out, local.at[12]))
    kept[-1].start()
    for copy in kept:
        copy.wait()
    arrived(sender.copies)
    sender.finish()


def norm_back(grad_normed, values, factor, gain):
    scaled = grad_normed * gain
    mean_term = jnp.mean(scaled * values, axis=-1, keepdims=True)
    grad_values = factor * scaled - values * factor * factor * factor * mean_term
    grad_gain = jnp.sum(grad_normed * values * factor, axis=0)
    return (grad_values, grad_gain)


def slot_matrices(routes, route_gates):
    named = (routes[:, :, None] == jnp.arange(EXPERTS, dtype=jnp.int32)).astype(F32)
    uses = jnp.sum(named, axis=1)
    gates = jnp.sum(named * route_gates[:, :, None], axis=1)
    row = lax.broadcasted_iota(jnp.int32, (TOK, TOK), 0)
    column = lax.broadcasted_iota(jnp.int32, (TOK, TOK), 1)
    earlier = (row > column).astype(BF16)
    ranks = jnp.dot(earlier, uses.astype(BF16), preferred_element_type=F32)
    slot = jnp.arange(SLOTS, dtype=jnp.int32)
    spread = (jnp.arange(EXPERTS, dtype=jnp.int32)[:, None] == slot[None, :] // CAP).astype(F32)
    both = jnp.where(uses > 0.5, ranks, -1.0).astype(BF16)
    flat = jnp.dot(both, spread.astype(BF16), preferred_element_type=F32)
    hits = flat == (slot % CAP).astype(F32)[None, :]
    flat_gates = jnp.dot(gates, spread, precision=lax.Precision.HIGHEST)
    weights = jnp.where(hits, RESIDUAL * flat_gates, 0.0)
    return (named, spread, hits.astype(BF16), weights)


def shards(
    layer_in, norm_one, w_query, key_weight, value_weight, w_output, norm_two,
    w_gate, w_up, w_down, routes, route_gates, cotangent,
):
    seq = lax.axis_index("seq")
    core = seq % 2
    key_value_resident = KEY_VALUE_HEADS // 4
    group_width = QUERY_HEADS // KEY_VALUE_HEADS
    head_width = key_value_resident * group_width * HEAD_SIZE
    kv_width = key_value_resident * HEAD_SIZE

    gains = jnp.pad(jnp.stack([norm_one, norm_two], axis=1), ((0, 0), (0, 126)))
    heads_block = jnp.concatenate(
        [
            lax.dynamic_slice_in_dim(w_query, seq * head_width, head_width, 1),
            lax.dynamic_slice_in_dim(key_weight, seq * kv_width, kv_width, 1),
            lax.dynamic_slice_in_dim(value_weight, seq * kv_width, kv_width, 1),
            gains,
        ],
        axis=1,
    )
    branch_block = lax.dynamic_slice_in_dim(w_output, core * 512, 512, 1)
    expert_block = jnp.stack(
        [
            lax.dynamic_index_in_dim(w.reshape(32, 4, 4, FF), seq, 2, keepdims=False)
            for w in (w_gate, w_up, w_down)
        ]
    ).transpose(2, 0, 1, 3)
    named = (routes[:, :, None] == jnp.arange(EXPERTS, dtype=jnp.int32)).astype(F32)
    gates_sent = jnp.sum(named * route_gates[:, :, None], axis=1).T
    gates_sent = jnp.broadcast_to(gates_sent[:, None, :], (EXPERTS, 8, TOK))

    heads_w, branch_w, tokens_all, weights_here, out_rows, gates_all = remote_call(
        gather_kernel,
        (heads_block, branch_block, layer_in, expert_block, cotangent, gates_sent),
        (
            (2, 4, 4, 32, 640),
            (2, 2, 4, 4, 32, 512),
            (2, 2, TOK, MODEL_WIDTH),
            (3, 2, 4, 32, FF),
            (4, 2, 2, TOK, MODEL_WIDTH),
            jax.ShapeDtypeStruct((EXPERTS, 8, TOK), F32),
        ),
        55,
        6,
        1,
        "gather_all",
    )
    heads_w = heads_w.reshape(MODEL_WIDTH, 640)
    branch_w = branch_w.reshape(2, MODEL_WIDTH, 512)
    weights_here = weights_here.reshape(3, 2, TOK, FF)
    expert_w = [weights_here]
    for k in (1, 2, 3):
        expert_w.append(lax.ppermute(weights_here, "x", [(i, (i + k) % 4) for i in range(4)]))

    cosine, sine = jnp.asarray(COSINE), jnp.asarray(SINE)
    hbm, vmem = pl.BlockSpec(memory_space=pltpu.HBM), pl.BlockSpec(memory_space=pltpu.VMEM)
    block = (TOK, MODEL_WIDTH)

    def arrays(*entries):
        return tuple(jax.ShapeDtypeStruct(shape, kind) for shape, kind in entries)

    def buffers(*entries):
        return [pltpu.VMEM(shape, kind) for shape, kind in entries]

    kept_arrays = (
        ((SEQ_LEN, MODEL_WIDTH), BF16),
        ((SEQ_LEN, head_width), BF16),
        ((SEQ_LEN, kv_width), BF16),
        ((SEQ_LEN, kv_width), BF16),
        ((SEQ_LEN, head_width), BF16),
        ((SEQ_LEN, TOK), F32),
        (block, F32),
        ((EXPERTS, CAP, TOK), BF16),
        ((SLOTS, MODEL_WIDTH), BF16),
    )
    table = ((SEQ_LEN, TOK), F32)
    heads_array = ((MODEL_WIDTH, 640), BF16)
    (
        normed_all, query_all, key_all, value_all, attended, sums, middle, picks, grad_back,
        rows_all, gains,
    ) = pl.pallas_call(
        forward_kernel,
        out_shape=arrays(*kept_arrays, ((4, 2, 2) + block, BF16), ((8, MODEL_WIDTH), F32)),
        in_specs=[hbm] * 7,
        out_specs=(hbm,) * 10 + (vmem,),
        scratch_shapes=buffers(
            ((4,) + block, BF16),
            heads_array,
            ((2, MODEL_WIDTH, 512), BF16),
            table,
            table,
            ((EXPERTS, 8, TOK), F32),
            ((EXPERTS,) + block, BF16),
            *kept_arrays,
            ((4, TOK, head_width), BF16),
            (block, BF16),
        )
        + [
            pltpu.SemaphoreType.DMA((21,)),
            pltpu.SemaphoreType.DMA((21,)),
            pltpu.SemaphoreType.DMA((7,)),
            pltpu.SemaphoreType.DMA((10,)),
        ],
        compiler_params=pltpu.CompilerParams(
            collective_id=7, has_side_effects=True, vmem_limit_bytes=60 * 2**20
        ),
        name="forward",
    )(
        tokens_all.reshape((4,) + block),
        heads_w,
        branch_w,
        cosine,
        sine,
        gates_all,
        out_rows.reshape((EXPERTS,) + block),
    )
    gain_first, gain_second = gains[0], gains[1]
    inputs = layer_in.astype(F32)
    factor_two = lax.rsqrt(jnp.mean(middle * middle, axis=-1, keepdims=True) + EPSILON)

    returned_array = ((2, EXPERTS, CAP, 512), BF16)
    grads_array = ((4, 2, TOK, 3 * FF), BF16)
    grad_rows, returned, expert_grads = pl.pallas_call(
        expert_kernel,
        out_shape=arrays(((EXPERTS, CAP, MODEL_WIDTH), BF16), returned_array, grads_array),
        in_specs=[hbm] * 7,
        out_specs=(hbm,) * 3,
        scratch_shapes=buffers(
            ((EXPERTS, CAP, TOK), BF16), ((SLOTS, MODEL_WIDTH), BF16), returned_array, grads_array
        )
        + [
            pltpu.VMEM((4, 4) + block, BF16),
            pltpu.VMEM((3, 2, 4, TOK, FF), BF16),
            pltpu.VMEM((EXPERTS, CAP, MODEL_WIDTH), BF16),
            pltpu.VMEM((SLOTS, MODEL_WIDTH), BF16),
            pltpu.VMEM((SLOTS, FF), BF16),
            pltpu.VMEM((SLOTS, FF), BF16),
            pltpu.VMEM((SLOTS, FF), BF16),
            pltpu.SemaphoreType.DMA((15,)),
            pltpu.SemaphoreType.DMA((15,)),
            pltpu.SemaphoreType.DMA((13,)),
        ],
        compiler_params=pltpu.CompilerParams(
            collective_id=5, has_side_effects=True, vmem_limit_bytes=60 * 2**20
        ),
        name="experts",
    )(rows_all.reshape((4, 4) + block), picks, grad_back, *expert_w)
    grad_rows = grad_rows.reshape(SLOTS, MODEL_WIDTH)
    late_routes, late_gates, grad_rows = lax.optimization_barrier((routes, route_gates, grad_rows))
    named, spread, hits, weights = slot_matrices(late_routes, late_gates)
    x_place = lax.axis_index("x")
    x_parts = [lax.dynamic_index_in_dim(expert_grads, x_place, 0, keepdims=False)]
    for k in (1, 2, 3):
        piece = lax.dynamic_index_in_dim(expert_grads, (x_place + k) % 4, 0, keepdims=False)
        x_parts.append(lax.ppermute(piece, "x", [(i, (i + k) % 4) for i in range(4)]))

    grad_out = cotangent.astype(F32)
    grad_normed_two = jnp.dot(hits, grad_rows, preferred_element_type=F32)
    grad_middle_norm, gain_two_term = norm_back(grad_normed_two, middle, factor_two, gain_second)
    grad_middle = grad_out + grad_middle_norm
    grad_branch = (RESIDUAL * grad_middle).astype(BF16)
    grad_normed, heads_term, branch_total, returned_left = pl.pallas_call(
        backward_kernel,
        out_shape=arrays(
            (block, F32),
            ((MODEL_WIDTH, 512), BF16),
            ((16, 512), BF16),
            ((EXPERTS, CAP, 512), BF16),
        ),
        in_specs=[vmem] + [hbm] * 11,
        out_specs=(vmem, vmem, vmem, hbm),
        scratch_shapes=buffers(
            ((SEQ_LEN, head_width), BF16),
            ((SEQ_LEN, head_width), BF16),
            ((SEQ_LEN, kv_width), BF16),
            ((SEQ_LEN, kv_width), BF16),
            table,
            ((SEQ_LEN, MODEL_WIDTH), BF16),
            heads_array,
            table,
            table,
        )
        + [
            pltpu.VMEM((2, 256, 512), BF16),
            pltpu.VMEM((2, 2) + block, BF16),
            pltpu.VMEM((8, 2, 16, MODEL_WIDTH), BF16),
            pltpu.VMEM((2, 2) + block, BF16),
            pltpu.VMEM((2,) + block, BF16),
            pltpu.VMEM(block, F32),
            pltpu.VMEM(block, BF16),
            pltpu.VMEM(block, BF16),
            pltpu.VMEM((3, 8, 16, 512), BF16),
            pltpu.VMEM((8, 16, 512), BF16),
            pltpu.VMEM((7, 16, 512), BF16),
            pltpu.SemaphoreType.DMA((31,)),
            pltpu.SemaphoreType.DMA((31,)),
            pltpu.SemaphoreType.DMA((11,)),
        ],
        compiler_params=pltpu.CompilerParams(
            collective_id=6, has_side_effects=True, vmem_limit_bytes=60 * 2**20
        ),
        name="backward",
    )(
        grad_branch,
        returned,
        branch_w,
        attended,
        query_all,
        key_all,
        value_all,
        sums,
        normed_all,
        heads_w,
        cosine,
        sine,
    )
    x_parts, heads_term, grad_normed = lax.optimization_barrier((x_parts, heads_term, grad_normed))
    expert_grads = (
        x_parts[0].astype(F32) + x_parts[1].astype(F32)
        + x_parts[2].astype(F32) + x_parts[3].astype(F32)
    ).astype(BF16)
    factor_one = lax.rsqrt(jnp.mean(inputs * inputs, axis=-1, keepdims=True) + EPSILON)
    grad_input_norm, gain_one_term = norm_back(grad_normed, inputs, factor_one, gain_first)
    grad_input = (grad_middle + grad_input_norm).astype(BF16)

    gain_terms = jnp.pad(
        jnp.stack([gain_one_term, gain_two_term], axis=1).astype(BF16), ((0, 0), (0, 126))
    )
    heads_term = jnp.concatenate([heads_term, gain_terms], axis=1).reshape(32, 32, 640)
    heads_four, branch_four, expert_four, returned_right = pl.pallas_call(
        finish_kernel,
        out_shape=(
            jax.ShapeDtypeStruct((2, 2, 32, 640), BF16),
            jax.ShapeDtypeStruct((4, 16, 512), BF16),
            jax.ShapeDtypeStruct((2, 2, 4, 32, 3 * FF), BF16),
            jax.ShapeDtypeStruct((EXPERTS, CAP, 512), BF16),
        ),
        in_specs=[vmem] * 3 + [hbm],
        out_specs=(hbm,) * 4,
        scratch_shapes=[
            pltpu.VMEM((3, 2, 4, 16, 640), BF16),
            pltpu.VMEM((3, 2, 4, 16, 640), BF16),
            pltpu.VMEM((2, 4, 16, 640), BF16),
            pltpu.VMEM((2, 4, 16, 640), BF16),
            pltpu.VMEM((7, 16, 640), BF16),
            pltpu.VMEM((7, 16, 640), BF16),
            pltpu.VMEM((2, 4, 32, 3 * FF), BF16),
            pltpu.VMEM((32, 640), BF16),
            pltpu.VMEM((4, 32, 3 * FF), BF16),
            pltpu.SemaphoreType.DMA((48,)),
            pltpu.SemaphoreType.DMA((48,)),
            pltpu.SemaphoreType.DMA((3,)),
            pltpu.SemaphoreType.DMA((4,)),
            pltpu.SemaphoreType.DMA((4,)),
        ],
        compiler_params=pltpu.CompilerParams(
            collective_id=2, has_side_effects=True, vmem_limit_bytes=60 * 2**20
        ),
        name="finish",
    )(
        heads_term.reshape(2, 4, 4, 32, 640),
        branch_total,
        expert_grads.reshape(2, 4, 32, 3 * FF),
        returned,
    )
    halves = [half.reshape(SLOTS, 512) for half in (returned_left, returned_right)]
    mixed = [
        jnp.dot(weights.astype(BF16), half, preferred_element_type=F32) for half in halves
    ]
    layer_out = (middle + jnp.concatenate(mixed, axis=1)).astype(BF16)
    pair_dots = sum(
        jnp.einsum("td,jd->tj", cotangent[:, k * 512 : k * 512 + 512], half, preferred_element_type=F32)
        for k, half in enumerate(halves)
    )
    expert_dots = jnp.einsum(
        "tj,ej->te", pair_dots * hits.astype(F32), spread, precision=lax.Precision.HIGHEST
    )
    grad_gates = RESIDUAL * jnp.sum(named * expert_dots[:, None, :], axis=-1)
    gain_sums = jnp.sum(heads_four[:, :, :, 512:514].astype(F32), axis=(0, 1))
    projections = pl.pallas_call(
        unpack_kernel,
        out_shape=tuple(
            jax.ShapeDtypeStruct(shape, F32)
            for shape in ((32, 1024), (32, 512), (32, 512), (32, 1024)) + ((32, EXPERTS, FF),) * 3
        ),
        in_specs=[vmem] * 3,
        out_specs=(vmem,) * 7,
        compiler_params=pltpu.CompilerParams(vmem_limit_bytes=16 * 2**20),
        name="unpack",
    )(heads_four, branch_four, expert_four)
    experts_out = projections[4:]
    return (
        layer_out,
        grad_input,
        gain_sums[:, 0],
        projections[0],
        projections[1],
        projections[2],
        projections[3],
        gain_sums[:, 1],
        experts_out[0],
        experts_out[1],
        experts_out[2],
        grad_gates,
    )


def solution(mesh):
    dp = ("yh", "x", "z")
    cut = Mesh(mesh.devices.reshape(2, 4, 4, 4), AXES)
    tokens, rows, gain, experts = P(AXES, None), P(dp, None), P(dp), P(dp, None, None)
    return jax.shard_map(
        shards,
        mesh=cut,
        in_specs=(
            tokens, gain, rows, rows, rows, rows, gain, experts, experts, experts,
            tokens, tokens, tokens,
        ),
        out_specs=(
            tokens, tokens, gain, rows, rows, rows, rows, gain, experts, experts, experts, tokens,
        ),
        check_vma=False,
    )
```

```python
import jax
import jax.numpy as jnp
import numpy as np
from jax import lax
from jax.experimental import pallas as pl
from jax.experimental.pallas import tpu as pltpu
from jax.sharding import Mesh
from jax.sharding import PartitionSpec as P

MODEL_WIDTH = 1024
QUERY_HEADS = 16
KEY_VALUE_HEADS = 8
HEAD_SIZE = 64
TOP = 8
EXPERTS = 16
CAP = 72
SLOTS = EXPERTS * CAP
TOK = 128
SEQ_LEN = 512
FF = 512
EPSILON = 1e-05
RESIDUAL = 0.22
ROPE_BASE = 10000.0
MASK_VALUE = -1e30

PLACES = np.arange(SEQ_LEN, dtype=np.float32)
FREQUENCIES = (ROPE_BASE ** (-np.arange(0, HEAD_SIZE, 2) / HEAD_SIZE)).astype(np.float32)
TURNS = PLACES[:, None] * np.tile(FREQUENCIES, 4)[None, :]
COSINE = np.cos(TURNS).astype(np.float32)
SINE = np.where(np.arange(TOK) % HEAD_SIZE < 32, -np.sin(TURNS), np.sin(TURNS)).astype(np.float32)

BF16 = jnp.bfloat16
F32 = jnp.float32
AXES = ("yh", "x", "z", "seq")
BY_ID = pl.DeviceIdType.MESH


def place():
    return tuple(lax.axis_index(axis) for axis in AXES)


class Sender:
    def __init__(self, send, recv):
        self.send, self.recv, self.used, self.copies = send, recv, 0, []

    def start(self, source, target, device):
        copy = pltpu.make_async_remote_copy(
            src_ref=source,
            dst_ref=target,
            send_sem=self.send.at[self.used],
            recv_sem=self.recv.at[self.used],
            device_id=device,
            device_id_type=BY_ID,
        )
        copy.start()
        self.used += 1
        self.copies.append(copy)
        return copy

    def finish(self):
        for copy in self.copies:
            copy.wait_send()


def arrived(copies):
    for copy in copies:
        copy.wait_recv()


def greet(partners):
    barrier = pltpu.get_barrier_semaphore()
    for partner in partners:
        pl.semaphore_signal(barrier, inc=1, device_id=partner, device_id_type=BY_ID)
    pl.semaphore_wait(barrier, len(partners))


def remote_call(kernel, inputs, outputs, scratch, copies, local_copies, collective_id, name):
    return pl.pallas_call(
        kernel,
        out_shape=tuple(
            shape if isinstance(shape, jax.ShapeDtypeStruct) else jax.ShapeDtypeStruct(shape, BF16)
            for shape in outputs
        ),
        in_specs=[pl.BlockSpec(memory_space=pltpu.HBM)] * len(inputs),
        out_specs=tuple(pl.BlockSpec(memory_space=pltpu.HBM) for _ in outputs),
        scratch_shapes=scratch
        + [
            pltpu.SemaphoreType.DMA((copies,)),
            pltpu.SemaphoreType.DMA((copies,)),
            pltpu.SemaphoreType.DMA((local_copies,)),
        ],
        compiler_params=pltpu.CompilerParams(collective_id=collective_id, has_side_effects=True),
        name=name,
    )(*inputs)


def local_starts(pairs, sems):
    copies = []
    for index, (source, target) in enumerate(pairs):
        copy = pltpu.make_async_copy(source, target, sems.at[index])
        copy.start()
        copies.append(copy)
    return copies


def group_of(x, z, seq, yh):
    yl, core = seq // 2, seq % 2
    return [
        (yh, x, (z + k // 4) % 4, (yl + (k // 2) % 2) % 2 * 2 + (core + k % 2) % 2)
        for k in range(1, 16)
    ]


class Blocks:
    def __init__(self, sender, block, blocks_all):
        yh, x, z, seq = place()
        self.yl, self.core = seq // 2, seq % 2
        self.sender, self.z, self.blocks = sender, z, blocks_all
        self.near = (yh, x, z, (1 - self.yl) * 2 + self.core)
        self.sibling = (yh, x, z, self.yl * 2 + 1 - self.core)
        self.along_z = [(yh, x, (z + k) % 4, seq) for k in (1, 2, 3)]
        own = blocks_all.at[z, self.yl, self.core]
        self.to_near = sender.start(block, own, self.near)
        self.to_z = [sender.start(block, own, partner) for partner in self.along_z]
        self.to_sibling = [sender.start(block, own, self.sibling)]

    def again(self, ref, partner):
        return self.sender.start(ref, ref, partner)

    def forward(self):
        arrived([self.to_near])
        beside = self.blocks.at[self.z, 1 - self.yl, self.core]
        self.passed = [self.again(beside.at[pl.ds(0, 64)], partner) for partner in self.along_z]
        self.to_sibling.append(self.again(beside, self.sibling))
        for k, copy in enumerate(self.to_z):
            arrived([copy])
            block = self.blocks.at[(self.z + 3 - k) % 4, self.yl, self.core]
            self.passed.append(self.again(block.at[pl.ds(64, 64)], self.near))
            self.to_sibling.append(self.again(block, self.sibling))

    def finish(self):
        for k in range(3):
            arrived([self.passed[k], self.passed[k + 3]])
            block = self.blocks.at[(self.z + 3 - k) % 4, 1 - self.yl, self.core]
            self.to_sibling.append(self.again(block, self.sibling))
        arrived(self.to_sibling)


def gather_kernel(
    w_query, key_weight, value_weight, w_output, gains, tokens, w_gate, w_up, w_down, gates,
    heads_all, branch_all, tokens_all, experts_all, gates_all,
    heads, weights, experts, send, recv, local,
):
    yh, x, z, seq = place()
    yl, core = seq // 2, seq % 2
    along_y = (1 - yh, x, z, seq)
    along_x = [(yh, (x + k) % 4, z, seq) for k in (1, 2, 3)]
    along_z = [(yh, x, (z + k) % 4, seq) for k in (1, 2, 3)]
    near = (yh, x, z, (1 - yl) * 2 + core)
    sibling = (yh, x, z, yl * 2 + 1 - core)
    group = [
        (yh, x, (z + k // 4) % 4, (yl + (k // 2) % 2) % 2 * 2 + (core + k % 2) % 2)
        for k in range(1, 16)
    ]
    expert = z * 4 + seq
    wide = pl.ds(pl.multiple_of(seq * 256, 256), 256)
    narrow = pl.ds(pl.multiple_of(seq * 128, 128), 128)
    branch = w_output.at[:, pl.ds(pl.multiple_of(core * 512, 512), 512)]
    built = local_starts(
        [
            (w_query.at[:, wide], heads.at[:, pl.ds(0, 256)]),
            (key_weight.at[:, narrow], heads.at[:, pl.ds(256, 128)]),
            (value_weight.at[:, narrow], heads.at[:, pl.ds(384, 128)]),
            (gains, heads.at[:, pl.ds(512, 128)]),
            (w_gate, weights.at[0]),
            (w_up, weights.at[1]),
            (w_down, weights.at[2]),
        ],
        local,
    )
    greet([along_y] + along_x + group)
    sender = Sender(send, recv)
    for copy in built[:4]:
        copy.wait()
    first = [
        sender.start(heads, heads_all.at[yh, x, z], along_y),
        sender.start(branch, branch_all.at[core, yh, x, z], along_y),
    ]
    token_copies = [
        sender.start(tokens, tokens_all.at[yl, core], near),
        sender.start(tokens, tokens_all.at[yl, core], sibling),
    ]
    own = []
    for source, target in (
        (heads, heads_all.at[yh, x, z]),
        (branch, branch_all.at[core, yh, x, z]),
        (tokens, tokens_all.at[yl, core]),
        (gates.at[expert], gates_all.at[expert]),
    ):
        own.append(pltpu.make_async_copy(source, target, local.at[7 + len(own)]))
        own[-1].start()
    for copy in built[4:]:
        copy.wait()
    row = lax.broadcasted_iota(jnp.int32, (TOK, 512), 0)
    column = lax.broadcasted_iota(jnp.int32, (TOK, 512), 1)
    same = jnp.logical_and(column // 16 == row % 32, column % 16 == row // 32 * 4 + seq)
    picker = jnp.where(same, 1.0, 0.0).astype(BF16)
    for k in range(3):
        picked = jnp.dot(picker, weights[k], preferred_element_type=F32).astype(BF16)
        experts[:, k] = picked.reshape(4, 32, FF)
    expert_first = [
        sender.start(experts.at[partner[2]], experts_all.at[:, yh, z], partner)
        for partner in along_z
    ]
    own.append(pltpu.make_async_copy(experts.at[z], experts_all.at[:, yh, z], local.at[11]))
    own[-1].start()
    for copy in own[:2]:
        copy.wait()
    arrived(first)
    second = []
    for k in range(3):
        source = heads_all.at[:, x, z]
        second.append(sender.start(source, source, along_z[k]))
        source = branch_all.at[core, :, x, z]
        second.append(sender.start(source, source, along_x[k]))
    own[4].wait()
    arrived(expert_first)
    mine = experts_all.at[:, yh]
    expert_second = [sender.start(mine, mine, along_y)]
    arrived(second)
    third = []
    for k in range(3):
        source = heads_all.at[:, x]
        third.append(sender.start(source, source, along_x[k]))
        source = branch_all.at[core, :, :, z]
        third.append(sender.start(source, source, along_z[k]))
    gate_copies = [
        sender.start(gates.at[partner[2] * 4 + partner[3]], gates_all.at[expert], partner)
        for partner in group
    ]
    arrived(token_copies)
    far = tokens_all.at[1 - yl, core]
    last = [sender.start(far, far, sibling)]
    for copy in own[2:4]:
        copy.wait()
    arrived(third)
    half = branch_all.at[core]
    last.append(sender.start(half, half, sibling))
    arrived(expert_second)
    arrived(gate_copies)
    arrived(last)
    sender.finish()


def by_rows(left, right):
    return lax.dot_general(left, right, (((0,), (0,)), ((), ())), preferred_element_type=F32)


def by_columns(left, right):
    return lax.dot_general(left, right, (((1,), (1,)), ((), ())), preferred_element_type=F32)


def half_turn(values):
    lane = lax.broadcasted_iota(jnp.int32, values.shape, 1)
    return jnp.where(lane % 64 < 32, pltpu.roll(values, 96, 1), pltpu.roll(values, 32, 1))


def causal_scores(query, key):
    row = lax.broadcasted_iota(jnp.int32, (SEQ_LEN, SEQ_LEN), 0)
    column = lax.broadcasted_iota(jnp.int32, (SEQ_LEN, SEQ_LEN), 1)
    return jnp.where(row >= column, by_columns(query, key) * (1.0 / HEAD_SIZE), MASK_VALUE)


def forward_kernel(
    tokens_in, heads_in, branch_in, cosine_in, sine_in, gates_in, out_in, weights_in, own_gates,
    normed_out, query_out, key_out, value_out, attended_out, sums_out, middle_out, picks_out,
    back_out, hits_out, shares_out, rows_all, weights_all, gains,
    tokens, heads_w, branch_here, cosine, sine, gates, out_here,
    normed, query, key, value, attended, sums, middle, picks, back, hits, shares,
    traded, rows, send, recv, fetch, keep,
):
    yh, x, z, seq = place()
    yl, core = seq // 2, seq % 2
    along_z = [(yh, x, (z + k) % 4, seq) for k in (1, 2, 3)]
    beside = [(yh, x, z, (seq + k) % 4) for k in (1, 2, 3)]
    fetched = local_starts(
        [
            (heads_in, heads_w), (tokens_in, tokens), (cosine_in, cosine), (sine_in, sine),
            (branch_in, branch_here), (gates_in, gates), (out_in, out_here.at[z, yl, core]),
        ],
        fetch,
    )
    along_x = [(yh, (x + k) % 4, z, seq) for k in (1, 2, 3)]
    greet(along_z + beside + along_x)
    sender = Sender(send, recv)
    out_blocks = Blocks(sender, out_in, out_here)
    weights = [
        sender.start(weights_in, weights_all.at[:, :, x], partner) for partner in along_x
    ]
    for copy in fetched[:4]:
        copy.wait()
    gains[...] = heads_w[:, 512:640].astype(F32).T[0:8]
    sequence = tokens[...].reshape(SEQ_LEN, MODEL_WIDTH).astype(F32)
    factor = lax.rsqrt(jnp.mean(sequence * sequence, axis=-1, keepdims=True) + EPSILON)
    normed[...] = (sequence * factor * gains[0:1]).astype(BF16)
    projected = jnp.dot(normed[...], heads_w[:, 0:512], preferred_element_type=F32)
    for k in range(2):
        part = projected[:, k * 128 : k * 128 + 128]
        query[:, k * 128 : k * 128 + 128] = (
            part * cosine[...] + half_turn(part) * sine[...]
        ).astype(BF16)
    part = projected[:, 256:384]
    key[...] = (part * cosine[...] + half_turn(part) * sine[...]).astype(BF16)
    value[...] = projected[:, 384:512].astype(BF16)
    lane = lax.broadcasted_iota(jnp.int32, (SEQ_LEN, TOK), 1)
    all_sums = jnp.zeros((SEQ_LEN, TOK), F32)
    for k in range(2):
        results = []
        key_head, value_head = key[:, k * 64 : k * 64 + 64], value[:, k * 64 : k * 64 + 64]
        for g in range(2):
            head = k * 2 + g
            scores = causal_scores(query[:, head * 64 : head * 64 + 64], key_head)
            top = jnp.max(scores, axis=-1, keepdims=True)
            exponent = jnp.exp(scores - top)
            total = jnp.sum(exponent, axis=-1, keepdims=True)
            probs = (exponent / total).astype(BF16)
            all_sums = jnp.where(lane == head, top + jnp.log(total), all_sums)
            results.append(jnp.dot(probs, value_head, preferred_element_type=F32))
        attended[:, k * 128 : k * 128 + 128] = jnp.concatenate(results, axis=1).astype(BF16)
    sums[...] = all_sums

    trades = []
    for partner in beside:
        start = pl.multiple_of(partner[3] * TOK, TOK)
        trades.append(sender.start(attended.at[pl.ds(start, TOK)], traded.at[seq], partner))
    traded[seq] = attended[pl.ds(pl.multiple_of(seq * TOK, TOK), TOK), :]
    out_blocks.forward()
    kept = local_starts(
        [
            (normed, normed_out), (query, query_out), (key, key_out), (value, value_out),
            (attended, attended_out), (sums, sums_out),
        ],
        keep,
    )
    fetched[4].wait()
    arrived(trades)
    here = jnp.concatenate([traded[k] for k in range(4)], axis=1)
    branch = jnp.concatenate(
        [jnp.dot(here, branch_here[k], preferred_element_type=F32) for k in range(2)], axis=1
    )
    mid = tokens[seq].astype(F32) + RESIDUAL * branch
    middle[...] = mid
    factor = lax.rsqrt(jnp.mean(mid * mid, axis=-1, keepdims=True) + EPSILON)
    rows[...] = (mid * factor * gains[1:2]).astype(BF16)

    blocks = Blocks(sender, rows, rows_all)
    for index, (source, target) in enumerate(
        ((rows, rows_all.at[z, yl, core]), (middle, middle_out))
    ):
        kept.append(pltpu.make_async_copy(source, target, keep.at[6 + index]))
        kept[-1].start()
    for copy in fetched[5:]:
        copy.wait()
    out_blocks.finish()
    row = lax.broadcasted_iota(jnp.int32, (TOK, TOK), 0)
    column = lax.broadcasted_iota(jnp.int32, (TOK, TOK), 1)
    earlier = jnp.where(row < column, 1.0, 0.0).astype(BF16)
    slot = lax.broadcasted_iota(jnp.int32, (CAP, TOK), 0).astype(F32)

    def two(index, carry):
        parts = []
        for j in range(2):
            gate = gates[index * 2 + j]
            named = jnp.where(gate > 0.0, 1.0, 0.0)
            ranks = jnp.dot(named.astype(BF16), earlier, preferred_element_type=F32)
            place_in = jnp.where(named > 0.5, ranks, -1.0)[0:1]
            hit = jnp.where(slot == place_in, 1.0, 0.0)
            pick = hit.astype(BF16)
            picks[index * 2 + j] = pick
            weight = jnp.sum(hit * gate[0:1], axis=1, keepdims=True)
            chosen = jnp.dot(
                pick, out_here[index // 2, index % 2, j], preferred_element_type=F32
            )
            parts.append(chosen * (RESIDUAL * weight))
        start = pl.multiple_of(index * (2 * CAP), 2 * CAP)
        back[pl.ds(start, 2 * CAP), :] = jnp.concatenate(parts, axis=0).astype(BF16)
        return carry

    lax.fori_loop(0, 4, two, 0)
    blocks.forward()
    lax.fori_loop(4, 8, two, 0)
    gate = own_gates[:, 0, :]
    named = jnp.where(gate > 0.0, 1.0, 0.0)
    ranks = jnp.dot(named.astype(BF16), earlier, preferred_element_type=F32)
    places = jnp.where(named > 0.5, ranks, -1.0).T
    gate_columns = gate.T * RESIDUAL
    lane = lax.broadcasted_iota(jnp.int32, (TOK, CAP), 1).astype(F32)
    for e in range(EXPERTS):
        hit = jnp.where(lane == places[:, e : e + 1], 1.0, 0.0)
        hits[e] = hit.astype(BF16)
        shares[e] = (hit * gate_columns[:, e : e + 1]).astype(BF16)
    for index, (source, target) in enumerate(
        ((picks, picks_out), (back, back_out), (hits, hits_out), (shares, shares_out))
    ):
        kept.append(pltpu.make_async_copy(source, target, keep.at[8 + index]))
        kept[-1].start()
    blocks.finish()
    for copy in kept:
        copy.wait()
    arrived(weights)
    sender.finish()


def backward_kernel(
    returned, branch_w,
    attended_in, query_in, key_in, value_in, sums_in, normed_in, heads_in, cosine_in, sine_in,
    experts_in, gate_in, rows_in, hits_in, shares_in, middle_in, out_in, tokens_in, gain_rows,
    layer_out, grad_input, pair_dots, heads_four, branch_four, experts_four,
    attended, query, key, value, sums, normed, heads_w, cosine, sine,
    gate_x, rows, hits, shares, middle, out_tokens, own_tokens, returned_all, block, grad_middle,
    experts_own, experts_x, branch_here, blocks_all, output_term, parts,
    arriving, paired, outgoing, incoming, branch_z, branch_out, branch_plane,
    heads, upper_in, lower_in, upper_out, lower_out, upper_plane, lower_plane,
    gains, gains_in, gains_out, gains_plane,
    experts, experts_plane, heads_sum, branch_sum, experts_sum,
    send, recv, local, branch_sends, branch_recvs,
):
    yh, x, z, seq = place()
    yl, core = seq // 2, seq % 2
    dp = yh * 16 + x * 4 + z
    expert = z * 4 + seq
    near = (yh, x, z, (1 - yl) * 2 + core)
    sibling = (yh, x, z, yl * 2 + 1 - core)
    along_x = [(yh, (x + k) % 4, z, seq) for k in (1, 2, 3)]
    along_z = [(yh, x, (z + k) % 4, seq) for k in (1, 2, 3)]
    plane = [((yh + k // 4) % 2, (x + k % 4) % 4, z, seq) for k in range(1, 8)]
    plane_z = [((yh + k // 4) % 2, x, (z + k % 4) % 4, seq) for k in range(1, 8)]
    group = [
        (yh, x, (z + k // 4) % 4, (yl + (k // 2) % 2) % 2 * 2 + (core + k % 2) % 2)
        for k in range(1, 16)
    ]
    owner = seq * 8 + dp // 4
    source_seq = dp // 8
    slot = dp % 4
    here = owner == dp
    span = pl.ds(pl.multiple_of(seq * 256, 256), 256)
    fetched = local_starts(
        [
            (rows_in, rows), (hits_in, hits), (middle_in, middle), (out_in, out_tokens),
            (branch_w.at[:, span], branch_here),
            (attended_in, attended), (query_in, query), (key_in, key), (value_in, value),
            (sums_in, sums), (normed_in, normed), (heads_in, heads_w),
            (cosine_in, cosine), (sine_in, sine),
            (returned.at[expert], returned_all.at[expert]),
            (experts_in.at[:, x], experts_own), (gate_in, gate_x), (shares_in, shares),
            (tokens_in, own_tokens),
        ],
        local,
    )
    barrier = pltpu.get_barrier_semaphore()
    for partner in group + plane + plane_z[4:]:
        pl.semaphore_signal(barrier, inc=1, device_id=partner, device_id_type=BY_ID)
    for k in range(4):
        maker = dp % 8 * 4 + k
        foreign = jnp.logical_or(maker != dp, source_seq != seq)

        @pl.when(foreign)
        def _():
            pl.semaphore_signal(
                barrier,
                inc=1,
                device_id=(maker // 16, maker // 4 % 4, maker % 4, source_seq),
                device_id_type=BY_ID,
            )

    pl.semaphore_wait(barrier, 29 - here.astype(jnp.int32))
    sender = Sender(send, recv)
    circling = [
        sender.start(experts_in.at[pl.ds(1, 2), partner[1]], experts_x.at[k], partner)
        for k, partner in enumerate(along_x)
    ]
    for copy in fetched[:4]:
        copy.wait()
    grad_normed_two = jnp.zeros((TOK, MODEL_WIDTH), F32)
    for e in range(EXPERTS):
        grad_normed_two += jnp.dot(hits[e], rows[e], preferred_element_type=F32)
    gain_first, gain_second = gain_rows[0:1], gain_rows[1:2]
    mid = middle[...]
    factor = lax.rsqrt(jnp.mean(mid * mid, axis=-1, keepdims=True) + EPSILON)
    gain_two = jnp.sum(grad_normed_two * mid * factor, axis=0, keepdims=True)
    scaled = grad_normed_two * gain_second
    mean_term = jnp.mean(scaled * mid, axis=-1, keepdims=True)
    grad_middle[...] = (
        out_tokens[...].astype(F32) + factor * scaled - mid * factor * factor * factor * mean_term
    )
    block[...] = (RESIDUAL * grad_middle[...]).astype(BF16)
    first = [
        sender.start(block, blocks_all.at[yl, core], near),
        sender.start(block, blocks_all.at[yl, core], sibling),
    ]
    blocks_all[yl, core] = block[...]
    arrived(first[:1])
    far = blocks_all.at[1 - yl, core]
    last = sender.start(far, far, sibling)
    row_copies = [
        sender.start(returned.at[partner[2] * 4 + partner[3]], returned_all.at[expert], partner)
        for partner in group
    ]
    for copy in fetched[4:14]:
        copy.wait()
    arrived(first[1:])
    arrived([last])
    branch_all = blocks_all[...].reshape(SEQ_LEN, MODEL_WIDTH)
    output_term[...] = by_rows(attended[...], branch_all).astype(BF16).reshape(8, 2, 16, MODEL_WIDTH)

    def branch_block(place_z):
        left = pl.multiple_of(place_z % 2 * 512, 512)
        return output_term.at[:, place_z // 2, :, pl.ds(left, 512)]

    around = [
        sender.start(branch_block(partner[2]), branch_z.at[k], partner)
        for k, partner in enumerate(along_z)
    ]
    grad_heads = (
        by_columns(branch_all[:, :512], branch_here[0])
        + by_columns(branch_all[:, 512:], branch_here[1])
    ).astype(BF16)
    lane = lax.broadcasted_iota(jnp.int32, (SEQ_LEN, TOK), 1)
    grad_queries, grad_keys, grad_values = [], [], []
    for k in range(2):
        key_head, value_head = key[:, k * 64 : k * 64 + 64], value[:, k * 64 : k * 64 + 64]
        grad_key, grad_value = 0.0, 0.0
        for g in range(2):
            head = k * 2 + g
            query_head = query[:, head * 64 : head * 64 + 64]
            grad_head = grad_heads[:, head * 64 : head * 64 + 64]
            log_sum = jnp.sum(jnp.where(lane == head, sums[...], 0.0), axis=-1, keepdims=True)
            probs = jnp.exp(causal_scores(query_head, key_head) - log_sum)
            grad_probs = by_columns(grad_head, value_head)
            inner = jnp.sum(probs * grad_probs, axis=-1, keepdims=True)
            grad_scores = (probs * (grad_probs - inner)).astype(BF16)
            grad_value += by_rows(probs.astype(BF16), grad_head)
            grad_key += by_rows(grad_scores, query_head)
            grad_queries.append(
                jnp.dot(grad_scores, key_head, preferred_element_type=F32) * (1.0 / HEAD_SIZE)
            )
        grad_keys.append(grad_key * (1.0 / HEAD_SIZE))
        grad_values.append(grad_value)

    def unturn(pair):
        values = jnp.concatenate(pair, axis=1).astype(BF16).astype(F32)
        return (values * cosine[...] - half_turn(values) * sine[...]).astype(BF16)

    projected = jnp.concatenate(
        [
            unturn(grad_queries[:2]),
            unturn(grad_queries[2:]),
            unturn(grad_keys),
            jnp.concatenate(grad_values, axis=1).astype(BF16),
        ],
        axis=1,
    )
    parts[...] = by_columns(projected, heads_w[:, 0:512]).astype(BF16).reshape(2, 2, TOK, MODEL_WIDTH)
    second = [
        sender.start(parts.at[1 - yl, 1 - core], arriving.at[0], sibling),
        sender.start(parts.at[yl, 1 - core], arriving.at[1], sibling),
    ]
    arrived(second[:1])
    outgoing[...] = gather_sums([parts[1 - yl, core], arriving[0]]).astype(BF16)
    third = sender.start(outgoing, incoming, near)
    term = by_rows(normed[...], projected).astype(BF16)
    heads[...] = term.reshape(2, 4, 4, 32, 512)
    upper, lower = pl.ds(0, 16), pl.ds(16, 16)
    heads_first = []
    for k in range(3):
        partner = along_x[k]
        source = heads.at[:, partner[1], :, upper]
        heads_first.append(sender.start(source, upper_in.at[k], partner))
        partner = along_z[k]
        source = heads.at[:, :, partner[2], lower]
        heads_first.append(sender.start(source, lower_in.at[k], partner))
    arrived(around)
    mine = branch_block(z)[...]
    branch_out[...] = gather_sums([mine] + [branch_z[k] for k in range(3)]).astype(BF16)
    across = [
        sender.start(branch_out.at[partner[0] * 4 + partner[1]], branch_plane.at[k], partner)
        for k, partner in enumerate(plane)
    ]
    arrived(second[1:])
    paired[...] = gather_sums([parts[yl, core], arriving[1]])
    arrived([third])
    total = paired[...] + incoming[...].astype(F32)
    fetched[18].wait()
    values = own_tokens[...].astype(F32)
    factor = lax.rsqrt(jnp.mean(values * values, axis=-1, keepdims=True) + EPSILON)
    gain_one = jnp.sum(total * values * factor, axis=0, keepdims=True)
    scaled = total * gain_first
    mean_term = jnp.mean(scaled * values, axis=-1, keepdims=True)
    grad_input[...] = (
        grad_middle[...] + factor * scaled - values * factor * factor * factor * mean_term
    ).astype(BF16)
    gain_terms = jnp.concatenate(
        [gain_one, gain_two, jnp.zeros((TOK - 2, MODEL_WIDTH), F32)], axis=0
    )
    gains[...] = gain_terms.T.astype(BF16).reshape(2, 4, 4, 32, TOK)
    gains_first = [
        sender.start(gains.at[:, partner[1]], gains_in.at[k], partner)
        for k, partner in enumerate(along_x)
    ]
    arrived(heads_first)
    for y in range(2):
        for j in range(4):
            upper_out[y, j] = gather_sums(
                [heads[y, x, j, 0:16]] + [upper_in[k, y, j] for k in range(3)]
            ).astype(BF16)
            lower_out[y, j] = gather_sums(
                [heads[y, j, z, 16:32]] + [lower_in[k, y, j] for k in range(3)]
            ).astype(BF16)
    heads_second = []
    for k in range(7):
        partner = plane_z[k]
        source = upper_out.at[partner[0], partner[2]]
        heads_second.append(sender.start(source, upper_plane.at[k], partner))
        partner = plane[k]
        source = lower_out.at[partner[0], partner[1]]
        heads_second.append(sender.start(source, lower_plane.at[k], partner))
    arrived(gains_first)
    for y in range(2):
        for j in range(4):
            gains_out[y, j] = gather_sums(
                [gains[y, x, j]] + [gains_in[k, y, j] for k in range(3)]
            ).astype(BF16)
    gains_second = [
        sender.start(gains_out.at[partner[0], partner[2]], gains_plane.at[k], partner)
        for k, partner in enumerate(plane_z)
    ]
    arrived(across)
    branch_sum[...] = gather_sums(
        [branch_out[yh * 4 + x]] + [branch_plane[k] for k in range(7)]
    ).astype(BF16)
    place_of = branch_four.at[slot]

    def branch_copy(k):
        return pltpu.make_async_remote_copy(
            src_ref=branch_sum,
            dst_ref=place_of,
            send_sem=branch_sends.at[k],
            recv_sem=branch_recvs.at[slot],
            device_id=(owner // 16, owner // 4 % 4, owner % 4, k),
            device_id_type=BY_ID,
        )

    for k in range(4):
        self_copy = jnp.logical_and(here, seq == k)

        @pl.when(jnp.logical_not(self_copy))
        def _():
            branch_copy(k).start()

        @pl.when(self_copy)
        def _():
            pltpu.make_async_copy(branch_sum, place_of, branch_recvs.at[slot]).start()

    for copy in fetched[15:17]:
        copy.wait()
    arrived(circling)
    for y in range(2):
        for k in range(3):
            if k == 0:
                pieces = [gate_x[j, y] for j in range(3)]
            else:
                pieces = [experts_x[j, k - 1, y] for j in range(3)]
            total = gather_sums([experts_own[k, y]] + pieces).astype(BF16)
            experts[y, :, :, k * 512 : k * 512 + 512] = total.reshape(4, 32, FF)
    experts_second = [
        sender.start(experts.at[partner[0], partner[2]], experts_plane.at[yh, z], partner)
        for partner in plane_z
    ]
    arrived(heads_second)
    heads_sum[0:16, 0:512] = gather_sums(
        [upper_out[yh, z]] + [upper_plane[k] for k in range(7)]
    ).astype(BF16)
    heads_sum[16:32, 0:512] = gather_sums(
        [lower_out[yh, x]] + [lower_plane[k] for k in range(7)]
    ).astype(BF16)
    arrived(gains_second)
    heads_sum[:, 512:640] = gather_sums(
        [gains_out[yh, z]] + [gains_plane[k] for k in range(7)]
    ).astype(BF16)
    heads_shared = [
        sender.start(heads_sum, heads_four.at[yl, core], partner) for partner in (near, sibling)
    ]
    kept = [pltpu.make_async_copy(heads_sum, heads_four.at[yl, core], local.at[19])]
    kept[0].start()
    fetched[14].wait()
    fetched[17].wait()
    arrived(row_copies)
    mixed = middle[...]
    dots = jnp.zeros((TOK, TOK), F32)
    lane = lax.broadcasted_iota(jnp.int32, (TOK, TOK), 1)
    for e in range(EXPERTS):
        mixed += jnp.dot(shares[e], returned_all[e], preferred_element_type=F32)
        found = by_columns(out_tokens[...], returned_all[e]) * hits[e].astype(F32)
        dots = jnp.where(lane == e, jnp.sum(found, axis=-1, keepdims=True), dots)
    layer_out[...] = mixed.astype(BF16)
    pair_dots[...] = dots * RESIDUAL
    arrived(experts_second)
    for j in range(4):

        @pl.when(z == j)
        def _():
            experts_sum[j] = gather_sums([experts[yh, j], experts_plane[1 - yh, j]]).astype(BF16)

        @pl.when(z != j)
        def _():
            experts_sum[j] = gather_sums([experts_plane[0, j], experts_plane[1, j]]).astype(BF16)

    experts_shared = [
        sender.start(experts_sum, experts_four.at[yl, core], partner) for partner in (near, sibling)
    ]
    kept.append(pltpu.make_async_copy(experts_sum, experts_four.at[yl, core], local.at[20]))
    kept[-1].start()
    arrived(heads_shared[:1])
    far = heads_four.at[1 - yl, core]
    ending = [sender.start(far, far, sibling)]
    arrived(experts_shared[:1])
    far = experts_four.at[1 - yl, core]
    ending.append(sender.start(far, far, sibling))
    arrived(heads_shared[1:])
    arrived(experts_shared[1:])
    for copy in kept:
        copy.wait()
    arrived(ending)
    for k in range(4):
        pltpu.make_async_copy(branch_sum, branch_four.at[k], branch_recvs.at[k]).wait()
        self_copy = jnp.logical_and(here, seq == k)

        @pl.when(jnp.logical_not(self_copy))
        def _():
            branch_copy(k).wait_send()

    sender.finish()


def gather_sums(parts):
    total = parts[0].astype(F32)
    for part in parts[1:]:
        total = total + part.astype(F32)
    return total


def unpack_kernel(heads, branch, experts, query, key, value, output, gate, up, down):
    for s in range(4):
        block = heads[s // 2, s % 2].astype(F32)
        query[:, s * 256 : s * 256 + 256] = block[:, :256]
        key[:, s * 128 : s * 128 + 128] = block[:, 256:384]
        value[:, s * 128 : s * 128 + 128] = block[:, 384:512]
        rows, columns = s // 2 * 16, s % 2 * 512
        output[rows : rows + 16, columns : columns + 512] = branch[s].astype(F32)
        for j in range(4):
            block = experts[s // 2, s % 2, j].astype(F32)
            for index, result in enumerate((gate, up, down)):
                result[:, j * 4 + s, :] = block[:, index * 512 : index * 512 + 512]


def expert_kernel(
    rows_all, picks_in, back_in, own_w, weights_all,
    grad_rows, returned_out, expert_grads_out, gate_x,
    picks, back, returned, expert_grads,
    rows_here, weights, outgoing, chosen, active, by_gate, by_up, send, recv, local,
):
    yh, x, z, seq = place()
    expert = z * 4 + seq
    turns = (2, 1, 3, 0)
    offsets = [(turn, k) for turn in turns for k in range(4) if turn + k > 0]
    partners = [(yh, x, (z + turn) % 4, (seq + k) % 4) for turn, k in offsets]
    fetches = local_starts(
        [
            (weights_all.at[:, :, (x + k) % 4], weights.at[:, :, (x + k) % 4])
            for k in (1, 2, 3)
        ]
        + [(own_w, weights.at[:, :, x])]
        + [(rows_all.at[(z + turn) % 4], rows_here.at[turn]) for turn in turns]
        + [(picks_in, picks), (back_in, back)],
        local,
    )
    along_x = [(yh, (x + k) % 4, z, seq) for k in (1, 2, 3)]
    greet(partners + along_x)
    sender = Sender(send, recv)
    for copy in fetches[:4] + fetches[8:]:
        copy.wait()
    gate_w, up_w, down_w = (weights[k].reshape(MODEL_WIDTH, FF) for k in range(3))
    for index, turn in enumerate(turns):
        fetches[4 + index].wait()
        first = (z + turn) % 4 * 4
        rows = jnp.concatenate(
            [
                jnp.dot(picks[first + j], rows_here[turn, j], preferred_element_type=F32)
                for j in range(4)
            ],
            axis=0,
        ).astype(BF16)
        span = pl.ds(index * 288, 288)
        chosen[span, :] = rows
        gate_pre = jnp.dot(rows, gate_w, preferred_element_type=F32)
        up_pre = jnp.dot(rows, up_w, preferred_element_type=F32)
        back_rows = back[pl.ds(pl.multiple_of(first * CAP, 288), 288), :]
        grad_active = jnp.dot(back_rows, down_w, preferred_element_type=F32)
        sigmoid_gate = jax.nn.sigmoid(gate_pre)
        silu = gate_pre * sigmoid_gate
        slope = sigmoid_gate * (1.0 + gate_pre * (1.0 - sigmoid_gate))
        grad_gate = (grad_active * up_pre * slope).astype(BF16)
        grad_up = (grad_active * silu).astype(BF16)
        by_gate[span, :] = grad_gate
        by_up[span, :] = grad_up
        active[span, :] = (silu * up_pre).astype(BF16)
        result = by_columns(grad_gate, gate_w) + by_columns(grad_up, up_w)
        for j in range(4):
            outgoing[first + j] = result[j * CAP : j * CAP + CAP].astype(BF16)
        for partner, offset in zip(partners, offsets):
            if offset[0] == turn:
                block = partner[2] * 4 + partner[3]
                sender.start(outgoing.at[block], grad_rows.at[expert], partner)
    kept = [pltpu.make_async_copy(outgoing.at[expert], grad_rows.at[expert], local.at[10])]
    kept[0].start()
    def grads_of(index, left, right):
        for part in range(2):
            total = by_rows(left[:, part * 512 : part * 512 + 512], right[...])
            expert_grads[index, :, part] = total.astype(BF16).reshape(4, TOK, FF)

    grads_of(0, chosen, by_gate)
    for k, partner in enumerate(along_x):
        sender.start(expert_grads.at[0, partner[1]], gate_x.at[k], partner)
    for index, turn in enumerate(turns):
        first = (z + turn) % 4 * 4
        result = by_columns(active[pl.ds(index * 288, 288), :], down_w)
        for j in range(4):
            returned[first + j] = result[j * CAP : j * CAP + CAP].astype(BF16)
    kept.append(pltpu.make_async_copy(returned, returned_out, local.at[11]))
    kept[-1].start()
    grads_of(1, chosen, by_up)
    for part in range(2):
        total = 0.0
        for index, turn in enumerate(turns):
            start = pl.multiple_of((z + turn) % 4 * 288, 288)
            total += by_rows(
                back[pl.ds(start, 288), pl.ds(part * 512, 512)],
                active[pl.ds(index * 288, 288), :],
            )
        expert_grads[2, :, part] = total.astype(BF16).reshape(4, TOK, FF)
    kept.append(pltpu.make_async_copy(expert_grads, expert_grads_out, local.at[12]))
    kept[-1].start()
    for copy in kept:
        copy.wait()
    arrived(sender.copies)
    sender.finish()


def shards(
    layer_in, norm_one, w_query, key_weight, value_weight, w_output, norm_two,
    w_gate, w_up, w_down, routes, route_gates, cotangent,
):
    key_value_resident = KEY_VALUE_HEADS // 4
    group_width = QUERY_HEADS // KEY_VALUE_HEADS
    head_width = key_value_resident * group_width * HEAD_SIZE
    kv_width = key_value_resident * HEAD_SIZE

    gains = jnp.pad(jnp.stack([norm_one, norm_two], axis=1), ((0, 0), (0, 126)))
    named = (routes[:, :, None] == jnp.arange(EXPERTS, dtype=jnp.int32)).astype(F32)
    gates_sent = jnp.sum(named * route_gates[:, :, None], axis=1).T
    gates_sent = jnp.broadcast_to(gates_sent[:, None, :], (EXPERTS, 8, TOK))

    heads_w, branch_w, tokens_all, weights_here, gates_all = remote_call(
        gather_kernel,
        (
            w_query, key_weight, value_weight, w_output, gains, layer_in,
            w_gate.reshape(512, FF), w_up.reshape(512, FF), w_down.reshape(512, FF), gates_sent,
        ),
        (
            (2, 4, 4, 32, 640),
            (2, 2, 4, 4, 32, 512),
            (2, 2, TOK, MODEL_WIDTH),
            (3, 2, 4, 32, FF),
            jax.ShapeDtypeStruct((EXPERTS, 8, TOK), F32),
        ),
        [
            pltpu.VMEM((32, 640), BF16),
            pltpu.VMEM((3, 512, FF), BF16),
            pltpu.VMEM((4, 3, 32, FF), BF16),
        ],
        37,
        12,
        1,
        "gather_all",
    )
    heads_w = heads_w.reshape(MODEL_WIDTH, 640)
    branch_w = branch_w.reshape(2, MODEL_WIDTH, 512)
    weights_here = weights_here.reshape(3, 2, TOK, FF)

    cosine, sine = jnp.asarray(COSINE), jnp.asarray(SINE)
    hbm, vmem = pl.BlockSpec(memory_space=pltpu.HBM), pl.BlockSpec(memory_space=pltpu.VMEM)
    block = (TOK, MODEL_WIDTH)

    def arrays(*entries):
        return tuple(jax.ShapeDtypeStruct(shape, kind) for shape, kind in entries)

    def buffers(*entries):
        return [pltpu.VMEM(shape, kind) for shape, kind in entries]

    kept_arrays = (
        ((SEQ_LEN, MODEL_WIDTH), BF16),
        ((SEQ_LEN, head_width), BF16),
        ((SEQ_LEN, kv_width), BF16),
        ((SEQ_LEN, kv_width), BF16),
        ((SEQ_LEN, head_width), BF16),
        ((SEQ_LEN, TOK), F32),
        (block, F32),
        ((EXPERTS, CAP, TOK), BF16),
        ((SLOTS, MODEL_WIDTH), BF16),
        ((EXPERTS, TOK, CAP), BF16),
        ((EXPERTS, TOK, CAP), BF16),
    )
    table = ((SEQ_LEN, TOK), F32)
    heads_array = ((MODEL_WIDTH, 640), BF16)
    (
        normed_all, query_all, key_all, value_all, attended, sums, middle, picks, grad_back,
        hits, shares, rows_all, weights_all, gains,
    ) = pl.pallas_call(
        forward_kernel,
        out_shape=arrays(
            *kept_arrays,
            ((4, 2, 2) + block, BF16),
            ((3, 2, 4, TOK, FF), BF16),
            ((8, MODEL_WIDTH), F32),
        ),
        in_specs=[hbm] * 8 + [vmem],
        out_specs=(hbm,) * 13 + (vmem,),
        scratch_shapes=buffers(
            ((4,) + block, BF16),
            heads_array,
            ((2, MODEL_WIDTH, 512), BF16),
            table,
            table,
            ((EXPERTS, 8, TOK), F32),
            ((4, 2, 2) + block, BF16),
            *kept_arrays,
            ((4, TOK, head_width), BF16),
            (block, BF16),
        )
        + [
            pltpu.SemaphoreType.DMA((42,)),
            pltpu.SemaphoreType.DMA((42,)),
            pltpu.SemaphoreType.DMA((7,)),
            pltpu.SemaphoreType.DMA((12,)),
        ],
        compiler_params=pltpu.CompilerParams(
            collective_id=7, has_side_effects=True, vmem_limit_bytes=60 * 2**20
        ),
        name="forward",
    )(
        tokens_all.reshape((4,) + block),
        heads_w,
        branch_w,
        cosine,
        sine,
        gates_all,
        cotangent,
        weights_here,
        gates_sent,
    )
    returned_array = ((EXPERTS, CAP, MODEL_WIDTH), BF16)
    grads_array = ((3, 4, 2, TOK, FF), BF16)
    gate_array = ((3, 2, TOK, FF), BF16)
    grad_rows, returned, expert_grads, gate_x = pl.pallas_call(
        expert_kernel,
        out_shape=arrays(returned_array, returned_array, grads_array, gate_array),
        in_specs=[hbm] * 5,
        out_specs=(hbm,) * 4,
        scratch_shapes=buffers(
            ((EXPERTS, CAP, TOK), BF16), ((SLOTS, MODEL_WIDTH), BF16), returned_array, grads_array
        )
        + [
            pltpu.VMEM((4, 4) + block, BF16),
            pltpu.VMEM((3, 2, 4, TOK, FF), BF16),
            pltpu.VMEM((EXPERTS, CAP, MODEL_WIDTH), BF16),
            pltpu.VMEM((SLOTS, MODEL_WIDTH), BF16),
            pltpu.VMEM((SLOTS, FF), BF16),
            pltpu.VMEM((SLOTS, FF), BF16),
            pltpu.VMEM((SLOTS, FF), BF16),
            pltpu.SemaphoreType.DMA((18,)),
            pltpu.SemaphoreType.DMA((18,)),
            pltpu.SemaphoreType.DMA((13,)),
        ],
        compiler_params=pltpu.CompilerParams(
            collective_id=5, has_side_effects=True, vmem_limit_bytes=60 * 2**20
        ),
        name="experts",
    )(rows_all.reshape((4, 4) + block), picks, grad_back, weights_here, weights_all)
    layer_out, grad_input, pair_dots, heads_four, branch_four, expert_four = pl.pallas_call(
        backward_kernel,
        out_shape=arrays(
            (block, BF16),
            (block, BF16),
            ((TOK, TOK), F32),
            ((2, 2, 32, 640), BF16),
            ((4, 16, 512), BF16),
            ((2, 2, 4, 32, 3 * FF), BF16),
        ),
        in_specs=[hbm] * 19 + [vmem],
        out_specs=(vmem,) * 3 + (hbm,) * 3,
        scratch_shapes=buffers(
            ((SEQ_LEN, head_width), BF16),
            ((SEQ_LEN, head_width), BF16),
            ((SEQ_LEN, kv_width), BF16),
            ((SEQ_LEN, kv_width), BF16),
            table,
            ((SEQ_LEN, MODEL_WIDTH), BF16),
            heads_array,
            table,
            table,
            gate_array,
            returned_array,
            ((EXPERTS, TOK, CAP), BF16),
            ((EXPERTS, TOK, CAP), BF16),
            (block, F32),
            (block, BF16),
            (block, BF16),
            returned_array,
            (block, BF16),
            (block, F32),
            ((3, 2, TOK, FF), BF16),
            ((3, 2, 2, TOK, FF), BF16),
        )
        + [
            pltpu.VMEM((2, 256, 512), BF16),
            pltpu.VMEM((2, 2) + block, BF16),
            pltpu.VMEM((8, 2, 16, MODEL_WIDTH), BF16),
            pltpu.VMEM((2, 2) + block, BF16),
            pltpu.VMEM((2,) + block, BF16),
            pltpu.VMEM(block, F32),
            pltpu.VMEM(block, BF16),
            pltpu.VMEM(block, BF16),
            pltpu.VMEM((3, 8, 16, 512), BF16),
            pltpu.VMEM((8, 16, 512), BF16),
            pltpu.VMEM((7, 16, 512), BF16),
        ]
        + buffers(
            ((2, 4, 4, 32, 512), BF16),
            ((3, 2, 4, 16, 512), BF16),
            ((3, 2, 4, 16, 512), BF16),
            ((2, 4, 16, 512), BF16),
            ((2, 4, 16, 512), BF16),
            ((7, 16, 512), BF16),
            ((7, 16, 512), BF16),
            ((2, 4, 4, 32, TOK), BF16),
            ((3, 2, 4, 32, TOK), BF16),
            ((2, 4, 32, TOK), BF16),
            ((7, 32, TOK), BF16),
            ((2, 4, 32, 3 * FF), BF16),
            ((2, 4, 32, 3 * FF), BF16),
            ((32, 640), BF16),
            ((16, 512), BF16),
            ((4, 32, 3 * FF), BF16),
        )
        + [
            pltpu.SemaphoreType.DMA((77,)),
            pltpu.SemaphoreType.DMA((77,)),
            pltpu.SemaphoreType.DMA((21,)),
            pltpu.SemaphoreType.DMA((4,)),
            pltpu.SemaphoreType.DMA((4,)),
        ],
        compiler_params=pltpu.CompilerParams(
            collective_id=6, has_side_effects=True, vmem_limit_bytes=60 * 2**20
        ),
        name="backward",
    )(
        returned,
        branch_w,
        attended,
        query_all,
        key_all,
        value_all,
        sums,
        normed_all,
        heads_w,
        cosine,
        sine,
        expert_grads,
        gate_x,
        grad_rows,
        hits,
        shares,
        middle,
        cotangent,
        layer_in,
        gains,
    )
    grad_gates = jnp.sum(named * pair_dots[:, None, :EXPERTS], axis=-1)
    gain_sums = jnp.sum(heads_four[:, :, :, 512:514].astype(F32), axis=(0, 1))
    projections = pl.pallas_call(
        unpack_kernel,
        out_shape=tuple(
            jax.ShapeDtypeStruct(shape, F32)
            for shape in ((32, 1024), (32, 512), (32, 512), (32, 1024)) + ((32, EXPERTS, FF),) * 3
        ),
        in_specs=[vmem] * 3,
        out_specs=(vmem,) * 7,
        compiler_params=pltpu.CompilerParams(vmem_limit_bytes=16 * 2**20),
        name="unpack",
    )(heads_four, branch_four, expert_four)
    experts_out = projections[4:]
    return (
        layer_out,
        grad_input,
        gain_sums[:, 0],
        projections[0],
        projections[1],
        projections[2],
        projections[3],
        gain_sums[:, 1],
        experts_out[0],
        experts_out[1],
        experts_out[2],
        grad_gates,
    )


def solution(mesh):
    dp = ("yh", "x", "z")
    cut = Mesh(mesh.devices.reshape(2, 4, 4, 4), AXES)
    tokens, rows, gain, experts = P(AXES, None), P(dp, None), P(dp), P(dp, None, None)
    return jax.shard_map(
        shards,
        mesh=cut,
        in_specs=(
            tokens, gain, rows, rows, rows, rows, gain, experts, experts, experts,
            tokens, tokens, tokens,
        ),
        out_specs=(
            tokens, tokens, gain, rows, rows, rows, rows, gain, experts, experts, experts, tokens,
        ),
        check_vma=False,
    )
```

```python
import jax
import jax.numpy as jnp
import numpy as np
from jax import lax
from jax.experimental import pallas as pl
from jax.experimental.pallas import tpu as pltpu
from jax.sharding import Mesh
from jax.sharding import PartitionSpec as P

MODEL_WIDTH = 1024
QUERY_HEADS = 16
KEY_VALUE_HEADS = 8
HEAD_SIZE = 64
TOP = 8
EXPERTS = 16
CAP = 72
SLOTS = EXPERTS * CAP
TOK = 128
SEQ_LEN = 512
FF = 512
EPSILON = 1e-05
RESIDUAL = 0.22
ROPE_BASE = 10000.0
MASK_VALUE = -1e30

PLACES = np.arange(SEQ_LEN, dtype=np.float32)
FREQUENCIES = (ROPE_BASE ** (-np.arange(0, HEAD_SIZE, 2) / HEAD_SIZE)).astype(np.float32)
TURNS = PLACES[:, None] * np.tile(FREQUENCIES, 4)[None, :]
COSINE = np.cos(TURNS).astype(np.float32)
SINE = np.where(np.arange(TOK) % HEAD_SIZE < 32, -np.sin(TURNS), np.sin(TURNS)).astype(np.float32)

BF16 = jnp.bfloat16
F32 = jnp.float32
AXES = ("yh", "x", "z", "seq")
BY_ID = pl.DeviceIdType.MESH


def place():
    return tuple(lax.axis_index(axis) for axis in AXES)


class Sender:
    def __init__(self, send, recv):
        self.send, self.recv, self.used, self.copies = send, recv, 0, []

    def start(self, source, target, device):
        copy = pltpu.make_async_remote_copy(
            src_ref=source,
            dst_ref=target,
            send_sem=self.send.at[self.used],
            recv_sem=self.recv.at[self.used],
            device_id=device,
            device_id_type=BY_ID,
        )
        copy.start()
        self.used += 1
        self.copies.append(copy)
        return copy

    def finish(self):
        for copy in self.copies:
            copy.wait_send()


def arrived(copies):
    for copy in copies:
        copy.wait_recv()


def greet(partners):
    barrier = pltpu.get_barrier_semaphore()
    for partner in partners:
        pl.semaphore_signal(barrier, inc=1, device_id=partner, device_id_type=BY_ID)
    pl.semaphore_wait(barrier, len(partners))


def remote_call(kernel, inputs, outputs, scratch, copies, local_copies, collective_id, name):
    return pl.pallas_call(
        kernel,
        out_shape=tuple(
            shape if isinstance(shape, jax.ShapeDtypeStruct) else jax.ShapeDtypeStruct(shape, BF16)
            for shape in outputs
        ),
        in_specs=[pl.BlockSpec(memory_space=pltpu.HBM)] * len(inputs),
        out_specs=tuple(pl.BlockSpec(memory_space=pltpu.HBM) for _ in outputs),
        scratch_shapes=scratch
        + [
            pltpu.SemaphoreType.DMA((copies,)),
            pltpu.SemaphoreType.DMA((copies,)),
            pltpu.SemaphoreType.DMA((local_copies,)),
        ],
        compiler_params=pltpu.CompilerParams(collective_id=collective_id, has_side_effects=True),
        name=name,
    )(*inputs)


def local_starts(pairs, sems):
    copies = []
    for index, (source, target) in enumerate(pairs):
        copy = pltpu.make_async_copy(source, target, sems.at[index])
        copy.start()
        copies.append(copy)
    return copies


def group_of(x, z, seq, yh):
    yl, core = seq // 2, seq % 2
    return [
        (yh, x, (z + k // 4) % 4, (yl + (k // 2) % 2) % 2 * 2 + (core + k % 2) % 2)
        for k in range(1, 16)
    ]


class Blocks:
    def __init__(self, sender, block, blocks_all):
        yh, x, z, seq = place()
        self.yl, self.core = seq // 2, seq % 2
        self.sender, self.z, self.blocks = sender, z, blocks_all
        self.near = (yh, x, z, (1 - self.yl) * 2 + self.core)
        self.sibling = (yh, x, z, self.yl * 2 + 1 - self.core)
        self.along_z = [(yh, x, (z + k) % 4, seq) for k in (1, 2, 3)]
        own = blocks_all.at[z, self.yl, self.core]
        first, second = pl.ds(0, 64), pl.ds(64, 64)
        self.halves = (first, second)
        self.near_first = sender.start(block.at[first], own.at[first], self.near)
        self.z_second = [
            sender.start(block.at[second], own.at[second], partner) for partner in self.along_z
        ]
        self.near_second = sender.start(block.at[second], own.at[second], self.near)
        self.z_first = [
            sender.start(block.at[first], own.at[first], partner) for partner in self.along_z
        ]
        self.to_sibling = [sender.start(block, own, self.sibling)]

    def again(self, ref, partner):
        return self.sender.start(ref, ref, partner)

    def forward(self):
        arrived([self.near_first])
        beside = self.blocks.at[self.z, 1 - self.yl, self.core]
        self.passed = [
            self.again(beside.at[self.halves[0]], partner) for partner in self.along_z
        ]
        others = [self.blocks.at[(self.z + 3 - k) % 4, self.yl, self.core] for k in range(3)]
        for k in range(3):
            arrived([self.z_second[k]])
            self.passed.append(self.again(others[k].at[self.halves[1]], self.near))
        arrived([self.near_second])
        self.to_sibling.append(self.again(beside, self.sibling))
        for k in range(3):
            arrived([self.z_first[k]])
            self.to_sibling.append(self.again(others[k], self.sibling))

    def finish(self):
        for k in range(3):
            arrived([self.passed[k], self.passed[k + 3]])
            block = self.blocks.at[(self.z + 3 - k) % 4, 1 - self.yl, self.core]
            self.to_sibling.append(self.again(block, self.sibling))
        arrived(self.to_sibling)


class Ring:
    def __init__(self, sender, here, left, right, own, block_at, half_at):
        self.sender, self.here, self.left, self.right = sender, here, left, right
        self.half_at = half_at
        self.from_left = sender.start(own, block_at(here), right)
        self.from_right = sender.start(own, block_at(here), left)

    def forward(self):
        arrived([self.from_left])
        half = self.half_at(0, (self.here + 3) % 4)
        self.passed = [self.sender.start(half, half, self.right)]
        arrived([self.from_right])
        half = self.half_at(1, (self.here + 1) % 4)
        self.passed.append(self.sender.start(half, half, self.left))

    def finish(self):
        arrived(self.passed)


class Local:
    def __init__(self, sems):
        self.sems, self.used = sems, 0

    def start(self, source, target):
        copy = pltpu.make_async_copy(source, target, self.sems.at[self.used])
        copy.start()
        self.used += 1
        return copy


def finished(copies):
    for copy in copies:
        copy.wait()


def by_rows(left, right):
    return lax.dot_general(left, right, (((0,), (0,)), ((), ())), preferred_element_type=F32)


def by_columns(left, right):
    return lax.dot_general(left, right, (((1,), (1,)), ((), ())), preferred_element_type=F32)


def half_turn(values):
    lane = lax.broadcasted_iota(jnp.int32, values.shape, 1)
    return jnp.where(lane % 64 < 32, pltpu.roll(values, 96, 1), pltpu.roll(values, 32, 1))


def causal_scores(query, key):
    row = lax.broadcasted_iota(jnp.int32, (SEQ_LEN, SEQ_LEN), 0)
    column = lax.broadcasted_iota(jnp.int32, (SEQ_LEN, SEQ_LEN), 1)
    return jnp.where(row >= column, by_columns(query, key) * (1.0 / HEAD_SIZE), MASK_VALUE)


def forward_kernel(
    w_query, key_weight, value_weight, w_output, gain_columns, tokens, w_gate, w_up, w_down,
    cosine_in, sine_in, out_in, own_gates,
    normed_out, query_out, key_out, value_out, attended_out, sums_out, middle_out, picks_out,
    back_out, hits_out, shares_out, rows_all, weights_plane, weights_all, heads_out, branch_out,
    gains,
    heads_piece, weights_raw, experts, heads_all, branch_all, tokens_all, cosine, sine, gates,
    out_here,
    normed, query, key, value, attended, sums, middle, picks, back, hits, shares,
    traded, rows, send, recv, local_sems,
):
    yh, x, z, seq = place()
    yl, core = seq // 2, seq % 2
    expert = z * 4 + seq
    along_y = (1 - yh, x, z, seq)
    along_x = [(yh, (x + k) % 4, z, seq) for k in (1, 2, 3)]
    along_z = [(yh, x, (z + k) % 4, seq) for k in (1, 2, 3)]
    beside = [(yh, x, z, (seq + k) % 4) for k in (1, 2, 3)]
    near = (yh, x, z, (1 - yl) * 2 + core)
    sibling = (yh, x, z, yl * 2 + 1 - core)
    group = [
        (yh, x, (z + k // 4) % 4, (yl + (k // 2) % 2) % 2 * 2 + (core + k % 2) % 2)
        for k in range(1, 16)
    ]
    local = Local(local_sems)
    wide = pl.ds(pl.multiple_of(seq * 256, 256), 256)
    narrow = pl.ds(pl.multiple_of(seq * 128, 128), 128)
    branch_piece = w_output.at[:, pl.ds(pl.multiple_of(core * 512, 512), 512)]
    built = [
        local.start(w_query.at[:, wide], heads_piece.at[:, pl.ds(0, 256)]),
        local.start(key_weight.at[:, narrow], heads_piece.at[:, pl.ds(256, 128)]),
        local.start(value_weight.at[:, narrow], heads_piece.at[:, pl.ds(384, 128)]),
        local.start(gain_columns, heads_piece.at[:, pl.ds(512, 128)]),
    ]
    raw = [
        local.start(source, weights_raw.at[k]) for k, source in enumerate((w_gate, w_up, w_down))
    ]
    greet([along_y] + along_x + group)
    sender = Sender(send, recv)
    finished(built)
    first = [
        sender.start(heads_piece, heads_all.at[yh, x, z], along_y),
        sender.start(branch_piece, branch_all.at[core, yh, x, z], along_y),
    ]
    token_copies = [
        sender.start(tokens, tokens_all.at[yl, core], near),
        sender.start(tokens, tokens_all.at[yl, core], sibling),
    ]
    own_pieces = [
        local.start(heads_piece, heads_all.at[yh, x, z]),
        local.start(branch_piece, branch_all.at[core, yh, x, z]),
    ]
    own_rest = [
        local.start(tokens, tokens_all.at[yl, core]),
        local.start(cosine_in, cosine),
        local.start(sine_in, sine),
    ]
    own_late = [
        local.start(own_gates.at[expert], gates.at[expert]),
        local.start(out_in, out_here.at[z, yl, core]),
    ]
    finished(raw)
    row = lax.broadcasted_iota(jnp.int32, (TOK, 512), 0)
    column = lax.broadcasted_iota(jnp.int32, (TOK, 512), 1)
    same = jnp.logical_and(column // 16 == row % 32, column % 16 == row // 32 * 4 + seq)
    picker = jnp.where(same, 1.0, 0.0).astype(BF16)
    for k in range(3):
        picked = jnp.dot(picker, weights_raw[k], preferred_element_type=F32).astype(BF16)
        experts[:, k] = picked.reshape(4, 32, FF)
    expert_first = [
        sender.start(experts.at[partner[2]], weights_plane.at[:, yh, z], partner)
        for partner in along_z
    ]
    own_experts = local.start(experts.at[z], weights_plane.at[:, yh, z])
    finished(own_pieces)
    arrived(first)
    heads_second, branch_second = [], []
    for k in range(3):
        source = heads_all.at[:, x, z]
        heads_second.append(sender.start(source, source, along_z[k]))
        source = branch_all.at[core, :, x, z]
        branch_second.append(sender.start(source, source, along_x[k]))
    own_experts.wait()
    arrived(expert_first)
    mine = weights_plane.at[:, yh]
    expert_second = sender.start(mine, mine, along_y)
    arrived(heads_second)
    heads_ring = Ring(
        sender, x, along_x[2], along_x[0], heads_all.at[:, x],
        lambda i: heads_all.at[:, i], lambda h, i: heads_all.at[h, i],
    )
    arrived(branch_second)
    source = branch_all.at[core, :, :, z]
    branch_third = [sender.start(source, source, partner) for partner in along_z]
    out_blocks = Blocks(sender, out_in, out_here)
    gate_copies = [
        sender.start(own_gates.at[partner[2] * 4 + partner[3]], gates.at[expert], partner)
        for partner in group
    ]
    arrived(token_copies)
    far = tokens_all.at[1 - yl, core]
    far_tokens = sender.start(far, far, sibling)
    heads_ring.forward()
    arrived([expert_second])
    weights_ring = Ring(
        sender, x, along_x[2], along_x[0], weights_plane,
        lambda i: weights_all.at[:, :, i], lambda h, i: weights_all.at[:, h, i],
    )
    finished(own_rest)
    arrived([far_tokens])
    sequence = tokens_all[...].reshape(SEQ_LEN, MODEL_WIDTH).astype(F32)
    factor = lax.rsqrt(jnp.mean(sequence * sequence, axis=-1, keepdims=True) + EPSILON)
    heads_ring.finish()
    heads_w = heads_all[...].reshape(MODEL_WIDTH, 640)
    gains[...] = heads_w[:, 512:640].astype(F32).T[0:8]
    normed[...] = (sequence * factor * gains[0:1]).astype(BF16)
    projected = jnp.dot(normed[...], heads_w[:, 0:512], preferred_element_type=F32)
    for k in range(2):
        part = projected[:, k * 128 : k * 128 + 128]
        query[:, k * 128 : k * 128 + 128] = (
            part * cosine[...] + half_turn(part) * sine[...]
        ).astype(BF16)
    part = projected[:, 256:384]
    key[...] = (part * cosine[...] + half_turn(part) * sine[...]).astype(BF16)
    value[...] = projected[:, 384:512].astype(BF16)
    lane = lax.broadcasted_iota(jnp.int32, (SEQ_LEN, TOK), 1)
    all_sums = jnp.zeros((SEQ_LEN, TOK), F32)
    for k in range(2):
        results = []
        key_head, value_head = key[:, k * 64 : k * 64 + 64], value[:, k * 64 : k * 64 + 64]
        for g in range(2):
            head = k * 2 + g
            scores = causal_scores(query[:, head * 64 : head * 64 + 64], key_head)
            top = jnp.max(scores, axis=-1, keepdims=True)
            exponent = jnp.exp(scores - top)
            total = jnp.sum(exponent, axis=-1, keepdims=True)
            probs = (exponent / total).astype(BF16)
            all_sums = jnp.where(lane == head, top + jnp.log(total), all_sums)
            results.append(jnp.dot(probs, value_head, preferred_element_type=F32))
        attended[:, k * 128 : k * 128 + 128] = jnp.concatenate(results, axis=1).astype(BF16)
    sums[...] = all_sums

    arrived(branch_third)
    half = branch_all.at[core]
    branch_half = sender.start(half, half, sibling)
    trades = []
    for partner in beside:
        start = pl.multiple_of(partner[3] * TOK, TOK)
        trades.append(sender.start(attended.at[pl.ds(start, TOK)], traded.at[seq], partner))
    traded[seq] = attended[pl.ds(pl.multiple_of(seq * TOK, TOK), TOK), :]
    out_blocks.forward()
    kept = [
        local.start(source, target)
        for source, target in (
            (normed, normed_out), (query, query_out), (key, key_out), (value, value_out),
            (attended, attended_out), (sums, sums_out), (heads_all, heads_out),
        )
    ]
    arrived([branch_half])
    kept.append(local.start(branch_all, branch_out))
    arrived(trades)
    here = jnp.concatenate([traded[k] for k in range(4)], axis=1)
    branch = jnp.concatenate(
        [
            jnp.dot(
                here, branch_all[k].reshape(MODEL_WIDTH, 512), preferred_element_type=F32
            )
            for k in range(2)
        ],
        axis=1,
    )
    mid = tokens_all[yl, core].astype(F32) + RESIDUAL * branch
    middle[...] = mid
    factor = lax.rsqrt(jnp.mean(mid * mid, axis=-1, keepdims=True) + EPSILON)
    rows[...] = (mid * factor * gains[1:2]).astype(BF16)

    blocks = Blocks(sender, rows, rows_all)
    weights_ring.forward()
    kept.append(local.start(rows, rows_all.at[z, yl, core]))
    kept.append(local.start(middle, middle_out))
    finished(own_late)
    arrived(gate_copies)
    out_blocks.finish()
    row = lax.broadcasted_iota(jnp.int32, (TOK, TOK), 0)
    column = lax.broadcasted_iota(jnp.int32, (TOK, TOK), 1)
    earlier = jnp.where(row < column, 1.0, 0.0).astype(BF16)
    slot = lax.broadcasted_iota(jnp.int32, (CAP, TOK), 0).astype(F32)

    def two(index, carry):
        parts = []
        for j in range(2):
            gate = gates[index * 2 + j]
            named = jnp.where(gate > 0.0, 1.0, 0.0)
            ranks = jnp.dot(named.astype(BF16), earlier, preferred_element_type=F32)
            place_in = jnp.where(named > 0.5, ranks, -1.0)[0:1]
            hit = jnp.where(slot == place_in, 1.0, 0.0)
            pick = hit.astype(BF16)
            picks[index * 2 + j] = pick
            weight = jnp.sum(hit * gate[0:1], axis=1, keepdims=True)
            chosen = jnp.dot(
                pick, out_here[index // 2, index % 2, j], preferred_element_type=F32
            )
            parts.append(chosen * (RESIDUAL * weight))
        start = pl.multiple_of(index * (2 * CAP), 2 * CAP)
        back[pl.ds(start, 2 * CAP), :] = jnp.concatenate(parts, axis=0).astype(BF16)
        return carry

    lax.fori_loop(0, 4, two, 0)
    blocks.forward()
    lax.fori_loop(4, 8, two, 0)
    gate = own_gates[:, 0, :]
    named = jnp.where(gate > 0.0, 1.0, 0.0)
    ranks = jnp.dot(named.astype(BF16), earlier, preferred_element_type=F32)
    places = jnp.where(named > 0.5, ranks, -1.0).T
    gate_columns = gate.T * RESIDUAL
    lane = lax.broadcasted_iota(jnp.int32, (TOK, CAP), 1).astype(F32)
    for e in range(EXPERTS):
        hit = jnp.where(lane == places[:, e : e + 1], 1.0, 0.0)
        hits[e] = hit.astype(BF16)
        shares[e] = (hit * gate_columns[:, e : e + 1]).astype(BF16)
    for source, target in (
        (picks, picks_out), (back, back_out), (hits, hits_out), (shares, shares_out)
    ):
        kept.append(local.start(source, target))
    blocks.finish()
    for copy in kept:
        copy.wait()
    weights_ring.finish()
    sender.finish()


def backward_kernel(
    returned, branch_w,
    attended_in, query_in, key_in, value_in, sums_in, normed_in, heads_in, cosine_in, sine_in,
    experts_in, gate_in, rows_in, hits_in, shares_in, middle_in, out_in, tokens_in, gain_rows,
    layer_out, grad_input, pair_dots, heads_four, branch_four, experts_four,
    attended, query, key, value, sums, normed, heads_w, cosine, sine,
    gate_x, rows, hits, shares, middle, out_tokens, own_tokens, returned_all, block, grad_middle,
    experts_own, experts_x, branch_here, blocks_all, output_term, parts,
    arriving, paired, outgoing, incoming, branch_z, branch_out, branch_plane,
    heads, upper_in, lower_in, upper_out, lower_out, upper_plane, lower_plane,
    gains, gains_in, gains_out, gains_plane,
    experts, experts_plane, heads_sum, branch_sum, experts_sum,
    send, recv, local, branch_sends, branch_recvs,
):
    yh, x, z, seq = place()
    yl, core = seq // 2, seq % 2
    dp = yh * 16 + x * 4 + z
    expert = z * 4 + seq
    near = (yh, x, z, (1 - yl) * 2 + core)
    sibling = (yh, x, z, yl * 2 + 1 - core)
    along_x = [(yh, (x + k) % 4, z, seq) for k in (1, 2, 3)]
    along_z = [(yh, x, (z + k) % 4, seq) for k in (1, 2, 3)]
    plane = [((yh + k // 4) % 2, (x + k % 4) % 4, z, seq) for k in range(1, 8)]
    plane_z = [((yh + k // 4) % 2, x, (z + k % 4) % 4, seq) for k in range(1, 8)]
    group = [
        (yh, x, (z + k // 4) % 4, (yl + (k // 2) % 2) % 2 * 2 + (core + k % 2) % 2)
        for k in range(1, 16)
    ]
    owner = seq * 8 + dp // 4
    source_seq = dp // 8
    slot = dp % 4
    here = owner == dp
    span = pl.ds(pl.multiple_of(seq * 256, 256), 256)
    fetched = local_starts(
        [
            (rows_in, rows), (hits_in, hits), (middle_in, middle), (out_in, out_tokens),
            (branch_w.at[:, span], branch_here),
            (attended_in, attended), (query_in, query), (key_in, key), (value_in, value),
            (sums_in, sums), (normed_in, normed), (heads_in, heads_w),
            (cosine_in, cosine), (sine_in, sine),
            (returned.at[expert], returned_all.at[expert]),
            (experts_in.at[:, x], experts_own), (gate_in, gate_x), (shares_in, shares),
            (tokens_in, own_tokens),
        ],
        local,
    )
    barrier = pltpu.get_barrier_semaphore()
    for partner in group + plane + plane_z[4:]:
        pl.semaphore_signal(barrier, inc=1, device_id=partner, device_id_type=BY_ID)
    for k in range(4):
        maker = dp % 8 * 4 + k
        foreign = jnp.logical_or(maker != dp, source_seq != seq)

        @pl.when(foreign)
        def _():
            pl.semaphore_signal(
                barrier,
                inc=1,
                device_id=(maker // 16, maker // 4 % 4, maker % 4, source_seq),
                device_id_type=BY_ID,
            )

    pl.semaphore_wait(barrier, 29 - here.astype(jnp.int32))
    sender = Sender(send, recv)
    circling = [
        sender.start(experts_in.at[pl.ds(1, 2), partner[1]], experts_x.at[k], partner)
        for k, partner in enumerate(along_x)
    ]
    def send_rows(partner):
        block_index = partner[2] * 4 + partner[3]
        return sender.start(returned.at[block_index], returned_all.at[expert], partner)

    row_copies = [send_rows(group[k - 1]) for k in range(1, 16) if (k // 2) % 2 == 0]
    for copy in fetched[:4]:
        copy.wait()
    grad_normed_two = jnp.zeros((TOK, MODEL_WIDTH), F32)
    for e in range(EXPERTS):
        grad_normed_two += jnp.dot(hits[e], rows[e], preferred_element_type=F32)
    gain_first, gain_second = gain_rows[0:1], gain_rows[1:2]
    mid = middle[...]
    factor = lax.rsqrt(jnp.mean(mid * mid, axis=-1, keepdims=True) + EPSILON)
    gain_two = jnp.sum(grad_normed_two * mid * factor, axis=0, keepdims=True)
    scaled = grad_normed_two * gain_second
    mean_term = jnp.mean(scaled * mid, axis=-1, keepdims=True)
    grad_middle[...] = (
        out_tokens[...].astype(F32) + factor * scaled - mid * factor * factor * factor * mean_term
    )
    block[...] = (RESIDUAL * grad_middle[...]).astype(BF16)
    first = [
        sender.start(block, blocks_all.at[yl, core], near),
        sender.start(block, blocks_all.at[yl, core], sibling),
    ]
    row_copies += [send_rows(group[k - 1]) for k in range(1, 16) if (k // 2) % 2 == 1]
    blocks_all[yl, core] = block[...]
    arrived(first[:1])
    far = blocks_all.at[1 - yl, core]
    last = sender.start(far, far, sibling)
    for copy in fetched[4:14]:
        copy.wait()
    arrived(first[1:])
    arrived([last])
    branch_all = blocks_all[...].reshape(SEQ_LEN, MODEL_WIDTH)
    output_term[...] = by_rows(attended[...], branch_all).astype(BF16).reshape(8, 2, 16, MODEL_WIDTH)

    def branch_block(place_z):
        left = pl.multiple_of(place_z % 2 * 512, 512)
        return output_term.at[:, place_z // 2, :, pl.ds(left, 512)]

    around = [
        sender.start(branch_block(partner[2]), branch_z.at[k], partner)
        for k, partner in enumerate(along_z)
    ]
    grad_heads = (
        by_columns(branch_all[:, :512], branch_here[0])
        + by_columns(branch_all[:, 512:], branch_here[1])
    ).astype(BF16)
    lane = lax.broadcasted_iota(jnp.int32, (SEQ_LEN, TOK), 1)
    grad_queries, grad_keys, grad_values = [], [], []
    for k in range(2):
        key_head, value_head = key[:, k * 64 : k * 64 + 64], value[:, k * 64 : k * 64 + 64]
        grad_key, grad_value = 0.0, 0.0
        for g in range(2):
            head = k * 2 + g
            query_head = query[:, head * 64 : head * 64 + 64]
            grad_head = grad_heads[:, head * 64 : head * 64 + 64]
            log_sum = jnp.sum(jnp.where(lane == head, sums[...], 0.0), axis=-1, keepdims=True)
            probs = jnp.exp(causal_scores(query_head, key_head) - log_sum)
            grad_probs = by_columns(grad_head, value_head)
            inner = jnp.sum(probs * grad_probs, axis=-1, keepdims=True)
            grad_scores = (probs * (grad_probs - inner)).astype(BF16)
            grad_value += by_rows(probs.astype(BF16), grad_head)
            grad_key += by_rows(grad_scores, query_head)
            grad_queries.append(
                jnp.dot(grad_scores, key_head, preferred_element_type=F32) * (1.0 / HEAD_SIZE)
            )
        grad_keys.append(grad_key * (1.0 / HEAD_SIZE))
        grad_values.append(grad_value)

    def unturn(pair):
        values = jnp.concatenate(pair, axis=1).astype(BF16).astype(F32)
        return (values * cosine[...] - half_turn(values) * sine[...]).astype(BF16)

    projected = jnp.concatenate(
        [
            unturn(grad_queries[:2]),
            unturn(grad_queries[2:]),
            unturn(grad_keys),
            jnp.concatenate(grad_values, axis=1).astype(BF16),
        ],
        axis=1,
    )
    parts[...] = by_columns(projected, heads_w[:, 0:512]).astype(BF16).reshape(2, 2, TOK, MODEL_WIDTH)
    second = [
        sender.start(parts.at[1 - yl, 1 - core], arriving.at[0], sibling),
        sender.start(parts.at[yl, 1 - core], arriving.at[1], sibling),
    ]
    arrived(second[:1])
    outgoing[...] = gather_sums([parts[1 - yl, core], arriving[0]]).astype(BF16)
    third = sender.start(outgoing, incoming, near)
    term = by_rows(normed[...], projected).astype(BF16)
    heads[...] = term.reshape(2, 4, 4, 32, 512)
    upper, lower = pl.ds(0, 16), pl.ds(16, 16)
    heads_first = []
    for k in range(3):
        partner = along_x[k]
        source = heads.at[:, partner[1], :, upper]
        heads_first.append(sender.start(source, upper_in.at[k], partner))
        partner = along_z[k]
        source = heads.at[:, :, partner[2], lower]
        heads_first.append(sender.start(source, lower_in.at[k], partner))
    for copy in fetched[15:17]:
        copy.wait()
    arrived(circling)
    for y in range(2):
        for k in range(3):
            if k == 0:
                pieces = [gate_x[j, y] for j in range(3)]
            else:
                pieces = [experts_x[j, k - 1, y] for j in range(3)]
            total = gather_sums([experts_own[k, y]] + pieces).astype(BF16)
            experts[y, :, :, k * 512 : k * 512 + 512] = total.reshape(4, 32, FF)
    experts_second = [
        sender.start(experts.at[partner[0], partner[2]], experts_plane.at[yh, z], partner)
        for partner in plane_z
    ]
    arrived(around)
    mine = branch_block(z)[...]
    branch_out[...] = gather_sums([mine] + [branch_z[k] for k in range(3)]).astype(BF16)
    across = [
        sender.start(branch_out.at[partner[0] * 4 + partner[1]], branch_plane.at[k], partner)
        for k, partner in enumerate(plane)
    ]
    arrived(second[1:])
    paired[...] = gather_sums([parts[yl, core], arriving[1]])
    arrived([third])
    total = paired[...] + incoming[...].astype(F32)
    fetched[18].wait()
    values = own_tokens[...].astype(F32)
    factor = lax.rsqrt(jnp.mean(values * values, axis=-1, keepdims=True) + EPSILON)
    gain_one = jnp.sum(total * values * factor, axis=0, keepdims=True)
    scaled = total * gain_first
    mean_term = jnp.mean(scaled * values, axis=-1, keepdims=True)
    grad_input[...] = (
        grad_middle[...] + factor * scaled - values * factor * factor * factor * mean_term
    ).astype(BF16)
    gain_terms = jnp.concatenate(
        [gain_one, gain_two, jnp.zeros((TOK - 2, MODEL_WIDTH), F32)], axis=0
    )
    gains[...] = gain_terms.T.astype(BF16).reshape(2, 4, 4, 32, TOK)
    gains_first = [
        sender.start(gains.at[:, partner[1]], gains_in.at[k], partner)
        for k, partner in enumerate(along_x)
    ]
    arrived(heads_first)
    for y in range(2):
        for j in range(4):
            upper_out[y, j] = gather_sums(
                [heads[y, x, j, 0:16]] + [upper_in[k, y, j] for k in range(3)]
            ).astype(BF16)
            lower_out[y, j] = gather_sums(
                [heads[y, j, z, 16:32]] + [lower_in[k, y, j] for k in range(3)]
            ).astype(BF16)
    heads_second = []
    for k in range(7):
        partner = plane_z[k]
        source = upper_out.at[partner[0], partner[2]]
        heads_second.append(sender.start(source, upper_plane.at[k], partner))
        partner = plane[k]
        source = lower_out.at[partner[0], partner[1]]
        heads_second.append(sender.start(source, lower_plane.at[k], partner))
    arrived(gains_first)
    for y in range(2):
        for j in range(4):
            gains_out[y, j] = gather_sums(
                [gains[y, x, j]] + [gains_in[k, y, j] for k in range(3)]
            ).astype(BF16)
    gains_second = [
        sender.start(gains_out.at[partner[0], partner[2]], gains_plane.at[k], partner)
        for k, partner in enumerate(plane_z)
    ]
    arrived(across)
    branch_sum[...] = gather_sums(
        [branch_out[yh * 4 + x]] + [branch_plane[k] for k in range(7)]
    ).astype(BF16)
    place_of = branch_four.at[slot]

    def branch_copy(k):
        return pltpu.make_async_remote_copy(
            src_ref=branch_sum,
            dst_ref=place_of,
            send_sem=branch_sends.at[k],
            recv_sem=branch_recvs.at[slot],
            device_id=(owner // 16, owner // 4 % 4, owner % 4, k),
            device_id_type=BY_ID,
        )

    for k in range(4):
        self_copy = jnp.logical_and(here, seq == k)

        @pl.when(jnp.logical_not(self_copy))
        def _():
            branch_copy(k).start()

        @pl.when(self_copy)
        def _():
            pltpu.make_async_copy(branch_sum, place_of, branch_recvs.at[slot]).start()

    arrived(experts_second)
    for j in range(4):

        @pl.when(z == j)
        def _():
            experts_sum[j] = gather_sums([experts[yh, j], experts_plane[1 - yh, j]]).astype(BF16)

        @pl.when(z != j)
        def _():
            experts_sum[j] = gather_sums([experts_plane[0, j], experts_plane[1, j]]).astype(BF16)

    experts_shared = [
        sender.start(experts_sum, experts_four.at[yl, core], partner) for partner in (near, sibling)
    ]
    kept = [pltpu.make_async_copy(experts_sum, experts_four.at[yl, core], local.at[20])]
    kept[0].start()
    arrived(heads_second)
    heads_sum[0:16, 0:512] = gather_sums(
        [upper_out[yh, z]] + [upper_plane[k] for k in range(7)]
    ).astype(BF16)
    heads_sum[16:32, 0:512] = gather_sums(
        [lower_out[yh, x]] + [lower_plane[k] for k in range(7)]
    ).astype(BF16)
    arrived(gains_second)
    heads_sum[:, 512:640] = gather_sums(
        [gains_out[yh, z]] + [gains_plane[k] for k in range(7)]
    ).astype(BF16)
    heads_shared = [
        sender.start(heads_sum, heads_four.at[yl, core], partner) for partner in (near, sibling)
    ]
    kept.append(pltpu.make_async_copy(heads_sum, heads_four.at[yl, core], local.at[19]))
    kept[-1].start()
    fetched[14].wait()
    fetched[17].wait()
    arrived(row_copies)
    mixed = middle[...]
    dots = jnp.zeros((TOK, TOK), F32)
    lane = lax.broadcasted_iota(jnp.int32, (TOK, TOK), 1)
    for e in range(EXPERTS):
        mixed += jnp.dot(shares[e], returned_all[e], preferred_element_type=F32)
        found = by_columns(out_tokens[...], returned_all[e]) * hits[e].astype(F32)
        dots = jnp.where(lane == e, jnp.sum(found, axis=-1, keepdims=True), dots)
    layer_out[...] = mixed.astype(BF16)
    pair_dots[...] = dots * RESIDUAL
    arrived(heads_shared[:1])
    far = heads_four.at[1 - yl, core]
    ending = [sender.start(far, far, sibling)]
    arrived(experts_shared[:1])
    far = experts_four.at[1 - yl, core]
    ending.append(sender.start(far, far, sibling))
    arrived(heads_shared[1:])
    arrived(experts_shared[1:])
    for copy in kept:
        copy.wait()
    arrived(ending)
    for k in range(4):
        pltpu.make_async_copy(branch_sum, branch_four.at[k], branch_recvs.at[k]).wait()
        self_copy = jnp.logical_and(here, seq == k)

        @pl.when(jnp.logical_not(self_copy))
        def _():
            branch_copy(k).wait_send()

    sender.finish()


def gather_sums(parts):
    total = parts[0].astype(F32)
    for part in parts[1:]:
        total = total + part.astype(F32)
    return total


def unpack_kernel(
    heads_in, branch_in, experts_in, layer_in, grad_in, dots_in, routes,
    query, key, value, output, gate, up, down, layer_out, grad_input, gates, gain_one, gain_two,
    heads, branch, experts, dots, local,
):
    copies = local_starts(
        [
            (heads_in, heads), (branch_in, branch), (dots_in, dots),
            (layer_in, layer_out), (grad_in, grad_input),
        ]
        + [(experts_in.at[s // 2, s % 2], experts.at[s]) for s in range(4)],
        local,
    )
    for copy in copies[:3]:
        copy.wait()
    gains = jnp.zeros((32, TOK), F32)
    for s in range(4):
        block = heads[s // 2, s % 2].astype(F32)
        query[:, s * 256 : s * 256 + 256] = block[:, :256]
        key[:, s * 128 : s * 128 + 128] = block[:, 256:384]
        value[:, s * 128 : s * 128 + 128] = block[:, 384:512]
        gains += block[:, 512:640]
        rows, columns = s // 2 * 16, s % 2 * 512
        output[rows : rows + 16, columns : columns + 512] = branch[s].astype(F32)
    gains = gains.T
    gain_one[...] = gains[0:1]
    gain_two[...] = gains[1:2]
    by_expert = dots[...].T[0:EXPERTS]
    index = lax.broadcasted_iota(jnp.int32, (EXPERTS, TOK), 0)
    for k in range(TOP):
        picked = jnp.where(index == routes[k : k + 1, :], by_expert, 0.0)
        gates[k : k + 1, :] = jnp.sum(picked, axis=0, keepdims=True)
    for s in range(4):
        copies[5 + s].wait()
        for j in range(4):
            block = experts[s, j].astype(F32)
            for index, result in enumerate((gate, up, down)):
                result[:, j * 4 + s, :] = block[:, index * 512 : index * 512 + 512]
    for copy in copies[3:5]:
        copy.wait()


def expert_kernel(
    rows_all, picks_in, back_in, own_w, weights_all,
    grad_rows, returned_out, expert_grads_out, gate_x,
    picks, back, returned, expert_grads,
    rows_here, weights, outgoing, chosen, active, by_gate, by_up, send, recv, local,
):
    yh, x, z, seq = place()
    expert = z * 4 + seq
    turns = (2, 1, 3, 0)
    offsets = [(turn, k) for turn in turns for k in range(4) if turn + k > 0]
    partners = [(yh, x, (z + turn) % 4, (seq + k) % 4) for turn, k in offsets]
    fetches = local_starts(
        [
            (weights_all.at[:, :, (x + k) % 4], weights.at[:, :, (x + k) % 4])
            for k in (1, 2, 3)
        ]
        + [(own_w, weights.at[:, :, x])]
        + [(rows_all.at[(z + turn) % 4], rows_here.at[turn]) for turn in turns]
        + [(picks_in, picks), (back_in, back)],
        local,
    )
    along_x = [(yh, (x + k) % 4, z, seq) for k in (1, 2, 3)]
    greet(partners + along_x)
    sender = Sender(send, recv)
    for copy in fetches[:4] + fetches[8:]:
        copy.wait()
    gate_w, up_w, down_w = (weights[k].reshape(MODEL_WIDTH, FF) for k in range(3))
    for index, turn in enumerate(turns):
        fetches[4 + index].wait()
        first = (z + turn) % 4 * 4
        rows = jnp.concatenate(
            [
                jnp.dot(picks[first + j], rows_here[turn, j], preferred_element_type=F32)
                for j in range(4)
            ],
            axis=0,
        ).astype(BF16)
        span = pl.ds(index * 288, 288)
        chosen[span, :] = rows
        gate_pre = jnp.dot(rows, gate_w, preferred_element_type=F32)
        up_pre = jnp.dot(rows, up_w, preferred_element_type=F32)
        back_rows = back[pl.ds(pl.multiple_of(first * CAP, 288), 288), :]
        grad_active = jnp.dot(back_rows, down_w, preferred_element_type=F32)
        sigmoid_gate = jax.nn.sigmoid(gate_pre)
        silu = gate_pre * sigmoid_gate
        slope = sigmoid_gate * (1.0 + gate_pre * (1.0 - sigmoid_gate))
        grad_gate = (grad_active * up_pre * slope).astype(BF16)
        grad_up = (grad_active * silu).astype(BF16)
        by_gate[span, :] = grad_gate
        by_up[span, :] = grad_up
        active[span, :] = (silu * up_pre).astype(BF16)
        result = by_columns(grad_gate, gate_w) + by_columns(grad_up, up_w)
        for j in range(4):
            outgoing[first + j] = result[j * CAP : j * CAP + CAP].astype(BF16)
        for partner, offset in zip(partners, offsets):
            if offset[0] == turn:
                block = partner[2] * 4 + partner[3]
                sender.start(outgoing.at[block], grad_rows.at[expert], partner)
    kept = [pltpu.make_async_copy(outgoing.at[expert], grad_rows.at[expert], local.at[10])]
    kept[0].start()
    def grads_of(index, left, right):
        for part in range(2):
            total = by_rows(left[:, part * 512 : part * 512 + 512], right[...])
            expert_grads[index, :, part] = total.astype(BF16).reshape(4, TOK, FF)

    grads_of(0, chosen, by_gate)
    for k, partner in enumerate(along_x):
        sender.start(expert_grads.at[0, partner[1]], gate_x.at[k], partner)
    for index, turn in enumerate(turns):
        first = (z + turn) % 4 * 4
        result = by_columns(active[pl.ds(index * 288, 288), :], down_w)
        for j in range(4):
            returned[first + j] = result[j * CAP : j * CAP + CAP].astype(BF16)
    kept.append(pltpu.make_async_copy(returned, returned_out, local.at[11]))
    kept[-1].start()
    grads_of(1, chosen, by_up)
    for part in range(2):
        total = 0.0
        for index, turn in enumerate(turns):
            start = pl.multiple_of((z + turn) % 4 * 288, 288)
            total += by_rows(
                back[pl.ds(start, 288), pl.ds(part * 512, 512)],
                active[pl.ds(index * 288, 288), :],
            )
        expert_grads[2, :, part] = total.astype(BF16).reshape(4, TOK, FF)
    kept.append(pltpu.make_async_copy(expert_grads, expert_grads_out, local.at[12]))
    kept[-1].start()
    for copy in kept:
        copy.wait()
    arrived(sender.copies)
    sender.finish()


def shards(
    layer_in, norm_one, w_query, key_weight, value_weight, w_output, norm_two,
    w_gate, w_up, w_down, routes, route_gates, cotangent,
):
    key_value_resident = KEY_VALUE_HEADS // 4
    group_width = QUERY_HEADS // KEY_VALUE_HEADS
    head_width = key_value_resident * group_width * HEAD_SIZE
    kv_width = key_value_resident * HEAD_SIZE

    gains = jnp.pad(jnp.stack([norm_one, norm_two], axis=1), ((0, 0), (0, 126)))
    named = (routes[:, :, None] == jnp.arange(EXPERTS, dtype=jnp.int32)).astype(F32)
    gates_sent = jnp.sum(named * route_gates[:, :, None], axis=1).T
    gates_sent = jnp.broadcast_to(gates_sent[:, None, :], (EXPERTS, 8, TOK))

    cosine, sine = jnp.asarray(COSINE), jnp.asarray(SINE)
    hbm, vmem = pl.BlockSpec(memory_space=pltpu.HBM), pl.BlockSpec(memory_space=pltpu.VMEM)
    block = (TOK, MODEL_WIDTH)

    def arrays(*entries):
        return tuple(jax.ShapeDtypeStruct(shape, kind) for shape, kind in entries)

    def buffers(*entries):
        return [pltpu.VMEM(shape, kind) for shape, kind in entries]

    kept_arrays = (
        ((SEQ_LEN, MODEL_WIDTH), BF16),
        ((SEQ_LEN, head_width), BF16),
        ((SEQ_LEN, kv_width), BF16),
        ((SEQ_LEN, kv_width), BF16),
        ((SEQ_LEN, head_width), BF16),
        ((SEQ_LEN, TOK), F32),
        (block, F32),
        ((EXPERTS, CAP, TOK), BF16),
        ((SLOTS, MODEL_WIDTH), BF16),
        ((EXPERTS, TOK, CAP), BF16),
        ((EXPERTS, TOK, CAP), BF16),
    )
    table = ((SEQ_LEN, TOK), F32)
    heads_array = ((MODEL_WIDTH, 640), BF16)
    (
        normed_all, query_all, key_all, value_all, attended, sums, middle, picks, grad_back,
        hits, shares, rows_all, weights_here, weights_all, heads_w, branch_w, gains,
    ) = pl.pallas_call(
        forward_kernel,
        out_shape=arrays(
            *kept_arrays,
            ((4, 2, 2) + block, BF16),
            ((3, 2, 4, 32, FF), BF16),
            ((3, 2, 4, 4, 32, FF), BF16),
            ((2, 4, 4, 32, 640), BF16),
            ((2, 2, 4, 4, 32, 512), BF16),
            ((8, MODEL_WIDTH), F32),
        ),
        in_specs=[hbm] * 12 + [vmem],
        out_specs=(hbm,) * 16 + (vmem,),
        scratch_shapes=buffers(
            ((32, 640), BF16),
            ((3, 512, FF), BF16),
            ((4, 3, 32, FF), BF16),
            ((2, 4, 4, 32, 640), BF16),
            ((2, 2, 4, 4, 32, 512), BF16),
            ((2, 2) + block, BF16),
            table,
            table,
            ((EXPERTS, 8, TOK), F32),
            ((4, 2, 2) + block, BF16),
            *kept_arrays,
            ((4, TOK, head_width), BF16),
            (block, BF16),
        )
        + [
            pltpu.SemaphoreType.DMA((89,)),
            pltpu.SemaphoreType.DMA((89,)),
            pltpu.SemaphoreType.DMA((29,)),
        ],
        compiler_params=pltpu.CompilerParams(
            collective_id=7, has_side_effects=True, vmem_limit_bytes=60 * 2**20
        ),
        name="forward",
    )(
        w_query,
        key_weight,
        value_weight,
        w_output,
        gains,
        layer_in,
        w_gate.reshape(512, FF),
        w_up.reshape(512, FF),
        w_down.reshape(512, FF),
        cosine,
        sine,
        cotangent,
        gates_sent,
    )
    heads_w = heads_w.reshape(MODEL_WIDTH, 640)
    branch_w = branch_w.reshape(2, MODEL_WIDTH, 512)
    weights_here = weights_here.reshape(3, 2, TOK, FF)
    weights_all = weights_all.reshape(3, 2, 4, TOK, FF)

    returned_array = ((EXPERTS, CAP, MODEL_WIDTH), BF16)
    grads_array = ((3, 4, 2, TOK, FF), BF16)
    gate_array = ((3, 2, TOK, FF), BF16)
    grad_rows, returned, expert_grads, gate_x = pl.pallas_call(
        expert_kernel,
        out_shape=arrays(returned_array, returned_array, grads_array, gate_array),
        in_specs=[hbm] * 5,
        out_specs=(hbm,) * 4,
        scratch_shapes=buffers(
            ((EXPERTS, CAP, TOK), BF16), ((SLOTS, MODEL_WIDTH), BF16), returned_array, grads_array
        )
        + [
            pltpu.VMEM((4, 4) + block, BF16),
            pltpu.VMEM((3, 2, 4, TOK, FF), BF16),
            pltpu.VMEM((EXPERTS, CAP, MODEL_WIDTH), BF16),
            pltpu.VMEM((SLOTS, MODEL_WIDTH), BF16),
            pltpu.VMEM((SLOTS, FF), BF16),
            pltpu.VMEM((SLOTS, FF), BF16),
            pltpu.VMEM((SLOTS, FF), BF16),
            pltpu.SemaphoreType.DMA((18,)),
            pltpu.SemaphoreType.DMA((18,)),
            pltpu.SemaphoreType.DMA((13,)),
        ],
        compiler_params=pltpu.CompilerParams(
            collective_id=5, has_side_effects=True, vmem_limit_bytes=60 * 2**20
        ),
        name="experts",
    )(rows_all.reshape((4, 4) + block), picks, grad_back, weights_here, weights_all)
    layer_out, grad_input, pair_dots, heads_four, branch_four, expert_four = pl.pallas_call(
        backward_kernel,
        out_shape=arrays(
            (block, BF16),
            (block, BF16),
            ((TOK, TOK), F32),
            ((2, 2, 32, 640), BF16),
            ((4, 16, 512), BF16),
            ((2, 2, 4, 32, 3 * FF), BF16),
        ),
        in_specs=[hbm] * 19 + [vmem],
        out_specs=(vmem,) * 3 + (hbm,) * 3,
        scratch_shapes=buffers(
            ((SEQ_LEN, head_width), BF16),
            ((SEQ_LEN, head_width), BF16),
            ((SEQ_LEN, kv_width), BF16),
            ((SEQ_LEN, kv_width), BF16),
            table,
            ((SEQ_LEN, MODEL_WIDTH), BF16),
            heads_array,
            table,
            table,
            gate_array,
            returned_array,
            ((EXPERTS, TOK, CAP), BF16),
            ((EXPERTS, TOK, CAP), BF16),
            (block, F32),
            (block, BF16),
            (block, BF16),
            returned_array,
            (block, BF16),
            (block, F32),
            ((3, 2, TOK, FF), BF16),
            ((3, 2, 2, TOK, FF), BF16),
        )
        + [
            pltpu.VMEM((2, 256, 512), BF16),
            pltpu.VMEM((2, 2) + block, BF16),
            pltpu.VMEM((8, 2, 16, MODEL_WIDTH), BF16),
            pltpu.VMEM((2, 2) + block, BF16),
            pltpu.VMEM((2,) + block, BF16),
            pltpu.VMEM(block, F32),
            pltpu.VMEM(block, BF16),
            pltpu.VMEM(block, BF16),
            pltpu.VMEM((3, 8, 16, 512), BF16),
            pltpu.VMEM((8, 16, 512), BF16),
            pltpu.VMEM((7, 16, 512), BF16),
        ]
        + buffers(
            ((2, 4, 4, 32, 512), BF16),
            ((3, 2, 4, 16, 512), BF16),
            ((3, 2, 4, 16, 512), BF16),
            ((2, 4, 16, 512), BF16),
            ((2, 4, 16, 512), BF16),
            ((7, 16, 512), BF16),
            ((7, 16, 512), BF16),
            ((2, 4, 4, 32, TOK), BF16),
            ((3, 2, 4, 32, TOK), BF16),
            ((2, 4, 32, TOK), BF16),
            ((7, 32, TOK), BF16),
            ((2, 4, 32, 3 * FF), BF16),
            ((2, 4, 32, 3 * FF), BF16),
            ((32, 640), BF16),
            ((16, 512), BF16),
            ((4, 32, 3 * FF), BF16),
        )
        + [
            pltpu.SemaphoreType.DMA((77,)),
            pltpu.SemaphoreType.DMA((77,)),
            pltpu.SemaphoreType.DMA((21,)),
            pltpu.SemaphoreType.DMA((4,)),
            pltpu.SemaphoreType.DMA((4,)),
        ],
        compiler_params=pltpu.CompilerParams(
            collective_id=6, has_side_effects=True, vmem_limit_bytes=60 * 2**20
        ),
        name="backward",
    )(
        returned,
        branch_w,
        attended,
        query_all,
        key_all,
        value_all,
        sums,
        normed_all,
        heads_w,
        cosine,
        sine,
        expert_grads,
        gate_x,
        grad_rows,
        hits,
        shares,
        middle,
        cotangent,
        layer_in,
        gains,
    )
    (
        grad_query_proj, grad_key_proj, grad_value_proj, grad_output_proj,
        grad_gate_proj, grad_up_proj, grad_down_proj, layer_out, grad_input,
        grad_gates, grad_norm_one, grad_norm_two,
    ) = pl.pallas_call(
        unpack_kernel,
        out_shape=arrays(
            ((32, 1024), F32),
            ((32, 512), F32),
            ((32, 512), F32),
            ((32, 1024), F32),
            ((32, EXPERTS, FF), F32),
            ((32, EXPERTS, FF), F32),
            ((32, EXPERTS, FF), F32),
            (block, BF16),
            (block, BF16),
            ((TOP, TOK), F32),
            ((1, 32), F32),
            ((1, 32), F32),
        ),
        in_specs=[hbm] * 6 + [vmem],
        out_specs=(vmem,) * 12,
        scratch_shapes=buffers(
            ((2, 2, 32, 640), BF16),
            ((4, 16, 512), BF16),
            ((4, 4, 32, 3 * FF), BF16),
            ((TOK, TOK), F32),
        )
        + [pltpu.SemaphoreType.DMA((9,))],
        compiler_params=pltpu.CompilerParams(vmem_limit_bytes=60 * 2**20),
        name="unpack",
    )(heads_four, branch_four, expert_four, layer_out, grad_input, pair_dots, routes.T)
    return (
        layer_out,
        grad_input,
        grad_norm_one.reshape(32),
        grad_query_proj,
        grad_key_proj,
        grad_value_proj,
        grad_output_proj,
        grad_norm_two.reshape(32),
        grad_gate_proj,
        grad_up_proj,
        grad_down_proj,
        grad_gates.T,
    )


def solution(mesh):
    dp = ("yh", "x", "z")
    cut = Mesh(mesh.devices.reshape(2, 4, 4, 4), AXES)
    tokens, rows, gain, experts = P(AXES, None), P(dp, None), P(dp), P(dp, None, None)
    return jax.shard_map(
        shards,
        mesh=cut,
        in_specs=(
            tokens, gain, rows, rows, rows, rows, gain, experts, experts, experts,
            tokens, tokens, tokens,
        ),
        out_specs=(
            tokens, tokens, gain, rows, rows, rows, rows, gain, experts, experts, experts, tokens,
        ),
        check_vma=False,
    )
```

```python
import jax
import jax.numpy as jnp
import numpy as np
from jax import lax
from jax.experimental import pallas as pl
from jax.experimental.pallas import tpu as pltpu
from jax.sharding import Mesh
from jax.sharding import PartitionSpec as P

MODEL_WIDTH = 1024
QUERY_HEADS = 16
KEY_VALUE_HEADS = 8
HEAD_SIZE = 64
TOP = 8
EXPERTS = 16
CAP = 72
SLOTS = EXPERTS * CAP
TOK = 128
SEQ_LEN = 512
FF = 512
EPSILON = 1e-05
RESIDUAL = 0.22
ROPE_BASE = 10000.0
MASK_VALUE = -1e30

PLACES = np.arange(SEQ_LEN, dtype=np.float32)
FREQUENCIES = (ROPE_BASE ** (-np.arange(0, HEAD_SIZE, 2) / HEAD_SIZE)).astype(np.float32)
TURNS = PLACES[:, None] * np.tile(FREQUENCIES, 4)[None, :]
COSINE = np.cos(TURNS).astype(np.float32)
SINE = np.where(np.arange(TOK) % HEAD_SIZE < 32, -np.sin(TURNS), np.sin(TURNS)).astype(np.float32)

BF16 = jnp.bfloat16
F32 = jnp.float32
AXES = ("yh", "x", "z", "seq")
BY_ID = pl.DeviceIdType.MESH


def place():
    return tuple(lax.axis_index(axis) for axis in AXES)


class Sender:
    def __init__(self, send, recv):
        self.send, self.recv, self.used, self.copies = send, recv, 0, []

    def start(self, source, target, device):
        copy = pltpu.make_async_remote_copy(
            src_ref=source,
            dst_ref=target,
            send_sem=self.send.at[self.used],
            recv_sem=self.recv.at[self.used],
            device_id=device,
            device_id_type=BY_ID,
        )
        copy.start()
        self.used += 1
        self.copies.append(copy)
        return copy

    def finish(self):
        for copy in self.copies:
            copy.wait_send()


def arrived(copies):
    for copy in copies:
        copy.wait_recv()


def greet(partners):
    barrier = pltpu.get_barrier_semaphore()
    for partner in partners:
        pl.semaphore_signal(barrier, inc=1, device_id=partner, device_id_type=BY_ID)
    pl.semaphore_wait(barrier, len(partners))


def remote_call(kernel, inputs, outputs, scratch, copies, local_copies, collective_id, name):
    return pl.pallas_call(
        kernel,
        out_shape=tuple(
            shape if isinstance(shape, jax.ShapeDtypeStruct) else jax.ShapeDtypeStruct(shape, BF16)
            for shape in outputs
        ),
        in_specs=[pl.BlockSpec(memory_space=pltpu.HBM)] * len(inputs),
        out_specs=tuple(pl.BlockSpec(memory_space=pltpu.HBM) for _ in outputs),
        scratch_shapes=scratch
        + [
            pltpu.SemaphoreType.DMA((copies,)),
            pltpu.SemaphoreType.DMA((copies,)),
            pltpu.SemaphoreType.DMA((local_copies,)),
        ],
        compiler_params=pltpu.CompilerParams(collective_id=collective_id, has_side_effects=True),
        name=name,
    )(*inputs)


def local_starts(pairs, sems):
    copies = []
    for index, (source, target) in enumerate(pairs):
        copy = pltpu.make_async_copy(source, target, sems.at[index])
        copy.start()
        copies.append(copy)
    return copies


def group_of(x, z, seq, yh):
    yl, core = seq // 2, seq % 2
    return [
        (yh, x, (z + k // 4) % 4, (yl + (k // 2) % 2) % 2 * 2 + (core + k % 2) % 2)
        for k in range(1, 16)
    ]


class Blocks:
    def __init__(self, sender, block, blocks_all):
        yh, x, z, seq = place()
        self.yl, self.core = seq // 2, seq % 2
        self.sender, self.z, self.blocks = sender, z, blocks_all
        self.near = (yh, x, z, (1 - self.yl) * 2 + self.core)
        self.sibling = (yh, x, z, self.yl * 2 + 1 - self.core)
        self.along_z = [(yh, x, (z + k) % 4, seq) for k in (1, 2, 3)]
        own = blocks_all.at[z, self.yl, self.core]
        first, second = pl.ds(0, 64), pl.ds(64, 64)
        self.halves = (first, second)
        self.near_first = sender.start(block.at[first], own.at[first], self.near)
        self.z_second = [
            sender.start(block.at[second], own.at[second], partner) for partner in self.along_z
        ]
        self.near_second = sender.start(block.at[second], own.at[second], self.near)
        self.z_first = [
            sender.start(block.at[first], own.at[first], partner) for partner in self.along_z
        ]
        self.to_sibling = [sender.start(block, own, self.sibling)]

    def again(self, ref, partner):
        return self.sender.start(ref, ref, partner)

    def forward(self):
        arrived([self.near_first])
        beside = self.blocks.at[self.z, 1 - self.yl, self.core]
        self.passed = [
            self.again(beside.at[self.halves[0]], partner) for partner in self.along_z
        ]
        others = [self.blocks.at[(self.z + 3 - k) % 4, self.yl, self.core] for k in range(3)]
        for k in range(3):
            arrived([self.z_second[k]])
            self.passed.append(self.again(others[k].at[self.halves[1]], self.near))
        arrived([self.near_second])
        self.to_sibling.append(self.again(beside, self.sibling))
        for k in range(3):
            arrived([self.z_first[k]])
            self.to_sibling.append(self.again(others[k], self.sibling))

    def finish(self):
        for k in range(3):
            arrived([self.passed[k], self.passed[k + 3]])
            block = self.blocks.at[(self.z + 3 - k) % 4, 1 - self.yl, self.core]
            self.to_sibling.append(self.again(block, self.sibling))
        arrived(self.to_sibling)


class Ring:
    def __init__(self, sender, here, left, right, own, block_at, half_at):
        self.sender, self.here, self.left, self.right = sender, here, left, right
        self.half_at = half_at
        self.from_left = sender.start(own, block_at(here), right)
        self.from_right = sender.start(own, block_at(here), left)

    def forward(self):
        arrived([self.from_left])
        half = self.half_at(0, (self.here + 3) % 4)
        self.passed = [self.sender.start(half, half, self.right)]
        arrived([self.from_right])
        half = self.half_at(1, (self.here + 1) % 4)
        self.passed.append(self.sender.start(half, half, self.left))

    def finish(self):
        arrived(self.passed)


class Local:
    def __init__(self, sems):
        self.sems, self.used = sems, 0

    def start(self, source, target):
        copy = pltpu.make_async_copy(source, target, self.sems.at[self.used])
        copy.start()
        self.used += 1
        return copy


def finished(copies):
    for copy in copies:
        copy.wait()


def by_rows(left, right):
    return lax.dot_general(left, right, (((0,), (0,)), ((), ())), preferred_element_type=F32)


def by_columns(left, right):
    return lax.dot_general(left, right, (((1,), (1,)), ((), ())), preferred_element_type=F32)


def half_turn(values):
    lane = lax.broadcasted_iota(jnp.int32, values.shape, 1)
    return jnp.where(lane % 64 < 32, pltpu.roll(values, 96, 1), pltpu.roll(values, 32, 1))


def causal_scores(query, key, first):
    shape = (query.shape[0], key.shape[0])
    row = lax.broadcasted_iota(jnp.int32, shape, 0) + first
    column = lax.broadcasted_iota(jnp.int32, shape, 1)
    return jnp.where(row >= column, by_columns(query, key) * (1.0 / HEAD_SIZE), MASK_VALUE)


def forward_kernel(
    w_query, key_weight, value_weight, w_output, tokens, w_gate, w_up, w_down,
    cosine_in, sine_in, out_in, norm_one, norm_two, routes, route_gates,
    normed_out, query_out, key_out, value_out, attended_out, sums_out, middle_out, picks_out,
    back_out, hits_out, shares_out, rows_all, weights_plane, weights_all, heads_out, branch_out,
    gains,
    own_gates, heads_piece, weights_raw, experts, heads_all, branch_all, tokens_all, cosine, sine, gates,
    out_here,
    normed, query, key, value, attended, sums, middle, picks, back, hits, shares,
    traded, rows, send, recv, local_sems,
):
    yh, x, z, seq = place()
    yl, core = seq // 2, seq % 2
    expert = z * 4 + seq
    along_y = (1 - yh, x, z, seq)
    along_x = [(yh, (x + k) % 4, z, seq) for k in (1, 2, 3)]
    along_z = [(yh, x, (z + k) % 4, seq) for k in (1, 2, 3)]
    beside = [(yh, x, z, (seq + k) % 4) for k in (1, 2, 3)]
    near = (yh, x, z, (1 - yl) * 2 + core)
    sibling = (yh, x, z, yl * 2 + 1 - core)
    group = [
        (yh, x, (z + k // 4) % 4, (yl + (k // 2) % 2) % 2 * 2 + (core + k % 2) % 2)
        for k in range(1, 16)
    ]
    local = Local(local_sems)
    wide = pl.ds(pl.multiple_of(seq * 256, 256), 256)
    narrow = pl.ds(pl.multiple_of(seq * 128, 128), 128)
    branch_piece = w_output.at[:, pl.ds(pl.multiple_of(core * 512, 512), 512)]
    built = [
        local.start(w_query.at[:, wide], heads_piece.at[:, pl.ds(0, 256)]),
        local.start(key_weight.at[:, narrow], heads_piece.at[:, pl.ds(256, 128)]),
        local.start(value_weight.at[:, narrow], heads_piece.at[:, pl.ds(384, 128)]),
    ]
    raw = [
        local.start(source, weights_raw.at[k]) for k, source in enumerate((w_gate, w_up, w_down))
    ]
    gain_rows = jnp.concatenate(
        [
            norm_one[...].astype(F32),
            norm_two[...].astype(F32),
            jnp.zeros((TOK - 2, 32), F32),
        ],
        axis=0,
    )
    heads_piece[:, 512:640] = gain_rows.T.astype(BF16)
    for e in range(EXPERTS):
        gate = jnp.where(routes[...] == e, route_gates[...], 0.0)
        own_gates[e] = jnp.broadcast_to(jnp.sum(gate, axis=0, keepdims=True), (8, TOK))
    greet([along_y] + along_x + group)
    sender = Sender(send, recv)
    finished(built)
    first = [
        sender.start(heads_piece, heads_all.at[yh, x, z], along_y),
        sender.start(branch_piece, branch_all.at[core, yh, x, z], along_y),
    ]
    token_copies = [
        sender.start(tokens, tokens_all.at[yl, core], near),
        sender.start(tokens, tokens_all.at[yl, core], sibling),
    ]
    own_pieces = [
        local.start(heads_piece, heads_all.at[yh, x, z]),
        local.start(branch_piece, branch_all.at[core, yh, x, z]),
    ]
    own_rest = [
        local.start(tokens, tokens_all.at[yl, core]),
        local.start(cosine_in, cosine),
        local.start(sine_in, sine),
    ]
    own_late = [
        local.start(own_gates.at[expert], gates.at[expert]),
        local.start(out_in, out_here.at[z, yl, core]),
    ]
    finished(raw)
    row = lax.broadcasted_iota(jnp.int32, (TOK, 512), 0)
    column = lax.broadcasted_iota(jnp.int32, (TOK, 512), 1)
    same = jnp.logical_and(column // 16 == row % 32, column % 16 == row // 32 * 4 + seq)
    picker = jnp.where(same, 1.0, 0.0).astype(BF16)
    for k in range(3):
        picked = jnp.dot(picker, weights_raw[k], preferred_element_type=F32).astype(BF16)
        experts[:, k] = picked.reshape(4, 32, FF)
    expert_first = [
        sender.start(experts.at[partner[2]], weights_plane.at[:, yh, z], partner)
        for partner in along_z
    ]
    own_experts = local.start(experts.at[z], weights_plane.at[:, yh, z])
    finished(own_pieces)
    arrived(first)
    heads_second, branch_second = [], []
    for k in range(3):
        source = heads_all.at[:, x, z]
        heads_second.append(sender.start(source, source, along_z[k]))
        source = branch_all.at[core, :, x, z]
        branch_second.append(sender.start(source, source, along_x[k]))
    own_experts.wait()
    arrived(expert_first)
    mine = weights_plane.at[:, yh]
    expert_second = sender.start(mine, mine, along_y)
    arrived(heads_second)
    heads_ring = Ring(
        sender, x, along_x[2], along_x[0], heads_all.at[:, x],
        lambda i: heads_all.at[:, i], lambda h, i: heads_all.at[h, i],
    )
    arrived(branch_second)
    source = branch_all.at[core, :, :, z]
    branch_third = [sender.start(source, source, partner) for partner in along_z]
    out_blocks = Blocks(sender, out_in, out_here)
    gate_copies = [
        sender.start(own_gates.at[partner[2] * 4 + partner[3]], gates.at[expert], partner)
        for partner in group
    ]
    arrived(token_copies)
    far = tokens_all.at[1 - yl, core]
    far_tokens = sender.start(far, far, sibling)
    heads_ring.forward()
    arrived([expert_second])
    weights_ring = Ring(
        sender, x, along_x[2], along_x[0], weights_plane,
        lambda i: weights_all.at[:, :, i], lambda h, i: weights_all.at[:, h, i],
    )
    finished(own_rest)
    arrived([far_tokens])
    sequence = tokens_all[...].reshape(SEQ_LEN, MODEL_WIDTH).astype(F32)
    factor = lax.rsqrt(jnp.mean(sequence * sequence, axis=-1, keepdims=True) + EPSILON)
    heads_ring.finish()
    heads_w = heads_all[...].reshape(MODEL_WIDTH, 640)
    gains[...] = heads_w[:, 512:640].astype(F32).T[0:8]
    normed[...] = (sequence * factor * gains[0:1]).astype(BF16)
    projected = jnp.dot(normed[...], heads_w[:, 0:512], preferred_element_type=F32)
    for k in range(2):
        part = projected[:, k * 128 : k * 128 + 128]
        query[:, k * 128 : k * 128 + 128] = (
            part * cosine[...] + half_turn(part) * sine[...]
        ).astype(BF16)
    part = projected[:, 256:384]
    key[...] = (part * cosine[...] + half_turn(part) * sine[...]).astype(BF16)
    value[...] = projected[:, 384:512].astype(BF16)
    lane = lax.broadcasted_iota(jnp.int32, (SEQ_LEN, TOK), 1)
    all_sums = jnp.zeros((SEQ_LEN, TOK), F32)
    for k in range(2):
        results = []
        key_head, value_head = key[:, k * 64 : k * 64 + 64], value[:, k * 64 : k * 64 + 64]
        for g in range(2):
            head = k * 2 + g
            columns = slice(head * 64, head * 64 + 64)
            halves, half_sums = [], []
            for part in range(2):
                start, keys = part * 256, part * 256 + 256
                scores = causal_scores(
                    query[start : start + 256, columns], key_head[:keys], start
                )
                top = jnp.max(scores, axis=-1, keepdims=True)
                exponent = jnp.exp(scores - top)
                total = jnp.sum(exponent, axis=-1, keepdims=True)
                probs = (exponent / total).astype(BF16)
                half_sums.append(top + jnp.log(total))
                halves.append(jnp.dot(probs, value_head[:keys], preferred_element_type=F32))
            all_sums = jnp.where(lane == head, jnp.concatenate(half_sums, axis=0), all_sums)
            results.append(jnp.concatenate(halves, axis=0))
        attended[:, k * 128 : k * 128 + 128] = jnp.concatenate(results, axis=1).astype(BF16)
    sums[...] = all_sums

    arrived(branch_third)
    half = branch_all.at[core]
    branch_half = sender.start(half, half, sibling)
    trades = []
    for partner in beside:
        start = pl.multiple_of(partner[3] * TOK, TOK)
        trades.append(sender.start(attended.at[pl.ds(start, TOK)], traded.at[seq], partner))
    traded[seq] = attended[pl.ds(pl.multiple_of(seq * TOK, TOK), TOK), :]
    out_blocks.forward()
    kept = [
        local.start(source, target)
        for source, target in (
            (normed, normed_out), (query, query_out), (key, key_out), (value, value_out),
            (attended, attended_out), (sums, sums_out), (heads_all, heads_out),
        )
    ]
    arrived([branch_half])
    kept.append(local.start(branch_all, branch_out))
    arrived(trades)
    here = jnp.concatenate([traded[k] for k in range(4)], axis=1)
    branch = jnp.concatenate(
        [
            jnp.dot(
                here, branch_all[k].reshape(MODEL_WIDTH, 512), preferred_element_type=F32
            )
            for k in range(2)
        ],
        axis=1,
    )
    mid = tokens_all[yl, core].astype(F32) + RESIDUAL * branch
    middle[...] = mid
    factor = lax.rsqrt(jnp.mean(mid * mid, axis=-1, keepdims=True) + EPSILON)
    rows[...] = (mid * factor * gains[1:2]).astype(BF16)

    blocks = Blocks(sender, rows, rows_all)
    weights_ring.forward()
    kept.append(local.start(rows, rows_all.at[z, yl, core]))
    kept.append(local.start(middle, middle_out))
    finished(own_late)
    arrived(gate_copies)
    out_blocks.finish()
    row = lax.broadcasted_iota(jnp.int32, (TOK, TOK), 0)
    column = lax.broadcasted_iota(jnp.int32, (TOK, TOK), 1)
    earlier = jnp.where(row < column, 1.0, 0.0).astype(BF16)
    slot = lax.broadcasted_iota(jnp.int32, (CAP, TOK), 0).astype(F32)

    def two(index, carry):
        parts = []
        for j in range(2):
            gate = gates[index * 2 + j]
            named = jnp.where(gate > 0.0, 1.0, 0.0)
            ranks = jnp.dot(named.astype(BF16), earlier, preferred_element_type=F32)
            place_in = jnp.where(named > 0.5, ranks, -1.0)[0:1]
            hit = jnp.where(slot == place_in, 1.0, 0.0)
            pick = hit.astype(BF16)
            picks[index * 2 + j] = pick
            weight = jnp.sum(hit * gate[0:1], axis=1, keepdims=True)
            chosen = jnp.dot(
                pick, out_here[index // 2, index % 2, j], preferred_element_type=F32
            )
            parts.append(chosen * (RESIDUAL * weight))
        start = pl.multiple_of(index * (2 * CAP), 2 * CAP)
        back[pl.ds(start, 2 * CAP), :] = jnp.concatenate(parts, axis=0).astype(BF16)
        return carry

    lax.fori_loop(0, 4, two, 0)
    blocks.forward()
    lax.fori_loop(4, 8, two, 0)
    gate = own_gates[:, 0, :]
    named = jnp.where(gate > 0.0, 1.0, 0.0)
    ranks = jnp.dot(named.astype(BF16), earlier, preferred_element_type=F32)
    places = jnp.where(named > 0.5, ranks, -1.0).T
    gate_columns = gate.T * RESIDUAL
    lane = lax.broadcasted_iota(jnp.int32, (TOK, CAP), 1).astype(F32)
    for e in range(EXPERTS):
        hit = jnp.where(lane == places[:, e : e + 1], 1.0, 0.0)
        hits[e] = hit.astype(BF16)
        shares[e] = (hit * gate_columns[:, e : e + 1]).astype(BF16)
    for source, target in (
        (picks, picks_out), (back, back_out), (hits, hits_out), (shares, shares_out)
    ):
        kept.append(local.start(source, target))
    blocks.finish()
    for copy in kept:
        copy.wait()
    weights_ring.finish()
    sender.finish()


def backward_kernel(
    returned, branch_w,
    attended_in, query_in, key_in, value_in, sums_in, normed_in, heads_in, cosine_in, sine_in,
    experts_in, gate_in, rows_in, hits_in, shares_in, middle_in, out_in, tokens_in, gain_rows,
    layer_out, grad_input, pair_dots, heads_four, branch_four, experts_four,
    attended, query, key, value, sums, normed, heads_w, cosine, sine,
    gate_x, rows, hits, shares, middle, out_tokens, own_tokens, returned_all, block, grad_middle,
    experts_own, experts_x, branch_here, blocks_all, output_term, parts,
    arriving, paired, outgoing, incoming, branch_z, branch_out, branch_plane,
    heads, upper_in, lower_in, upper_out, lower_out, upper_plane, lower_plane,
    gains, gains_in, gains_out, gains_plane,
    experts, experts_plane, heads_sum, branch_sum, experts_sum,
    send, recv, local, branch_sends, branch_recvs,
):
    yh, x, z, seq = place()
    yl, core = seq // 2, seq % 2
    dp = yh * 16 + x * 4 + z
    expert = z * 4 + seq
    near = (yh, x, z, (1 - yl) * 2 + core)
    sibling = (yh, x, z, yl * 2 + 1 - core)
    along_x = [(yh, (x + k) % 4, z, seq) for k in (1, 2, 3)]
    along_z = [(yh, x, (z + k) % 4, seq) for k in (1, 2, 3)]
    plane = [((yh + k // 4) % 2, (x + k % 4) % 4, z, seq) for k in range(1, 8)]
    plane_z = [((yh + k // 4) % 2, x, (z + k % 4) % 4, seq) for k in range(1, 8)]
    group = [
        (yh, x, (z + k // 4) % 4, (yl + (k // 2) % 2) % 2 * 2 + (core + k % 2) % 2)
        for k in range(1, 16)
    ]
    owner = seq * 8 + dp // 4
    source_seq = dp // 8
    slot = dp % 4
    here = owner == dp
    span = pl.ds(pl.multiple_of(seq * 256, 256), 256)
    fetched = local_starts(
        [
            (rows_in, rows), (hits_in, hits), (middle_in, middle), (out_in, out_tokens),
            (branch_w.at[:, span], branch_here),
            (attended_in, attended), (query_in, query), (key_in, key), (value_in, value),
            (sums_in, sums), (normed_in, normed), (heads_in, heads_w),
            (cosine_in, cosine), (sine_in, sine),
            (returned.at[expert], returned_all.at[expert]),
            (experts_in.at[:, x], experts_own), (gate_in, gate_x), (shares_in, shares),
            (tokens_in, own_tokens),
        ],
        local,
    )
    barrier = pltpu.get_barrier_semaphore()
    for partner in group + plane + plane_z[4:]:
        pl.semaphore_signal(barrier, inc=1, device_id=partner, device_id_type=BY_ID)
    for k in range(4):
        maker = dp % 8 * 4 + k
        foreign = jnp.logical_or(maker != dp, source_seq != seq)

        @pl.when(foreign)
        def _():
            pl.semaphore_signal(
                barrier,
                inc=1,
                device_id=(maker // 16, maker // 4 % 4, maker % 4, source_seq),
                device_id_type=BY_ID,
            )

    pl.semaphore_wait(barrier, 29 - here.astype(jnp.int32))
    sender = Sender(send, recv)
    circling = [
        sender.start(experts_in.at[pl.ds(1, 2), partner[1]], experts_x.at[k], partner)
        for k, partner in enumerate(along_x)
    ]
    def send_rows(partner):
        block_index = partner[2] * 4 + partner[3]
        return sender.start(returned.at[block_index], returned_all.at[expert], partner)

    row_copies = [send_rows(group[k - 1]) for k in range(1, 16) if (k // 2) % 2 == 0]
    for copy in fetched[:4]:
        copy.wait()
    grad_normed_two = jnp.zeros((TOK, MODEL_WIDTH), F32)
    for e in range(EXPERTS):
        grad_normed_two += jnp.dot(hits[e], rows[e], preferred_element_type=F32)
    gain_first, gain_second = gain_rows[0:1], gain_rows[1:2]
    mid = middle[...]
    factor = lax.rsqrt(jnp.mean(mid * mid, axis=-1, keepdims=True) + EPSILON)
    gain_two = jnp.sum(grad_normed_two * mid * factor, axis=0, keepdims=True)
    scaled = grad_normed_two * gain_second
    mean_term = jnp.mean(scaled * mid, axis=-1, keepdims=True)
    grad_middle[...] = (
        out_tokens[...].astype(F32) + factor * scaled - mid * factor * factor * factor * mean_term
    )
    block[...] = (RESIDUAL * grad_middle[...]).astype(BF16)
    first = [
        sender.start(block, blocks_all.at[yl, core], near),
        sender.start(block, blocks_all.at[yl, core], sibling),
    ]
    row_copies += [send_rows(group[k - 1]) for k in range(1, 16) if (k // 2) % 2 == 1]
    blocks_all[yl, core] = block[...]
    arrived(first[:1])
    far = blocks_all.at[1 - yl, core]
    last = sender.start(far, far, sibling)
    for copy in fetched[4:14]:
        copy.wait()
    arrived(first[1:])
    arrived([last])
    branch_all = blocks_all[...].reshape(SEQ_LEN, MODEL_WIDTH)
    output_term[...] = by_rows(attended[...], branch_all).astype(BF16).reshape(8, 2, 16, MODEL_WIDTH)

    def branch_block(place_z):
        left = pl.multiple_of(place_z % 2 * 512, 512)
        return output_term.at[:, place_z // 2, :, pl.ds(left, 512)]

    around = [
        sender.start(branch_block(partner[2]), branch_z.at[k], partner)
        for k, partner in enumerate(along_z)
    ]
    grad_heads = (
        by_columns(branch_all[:, :512], branch_here[0])
        + by_columns(branch_all[:, 512:], branch_here[1])
    ).astype(BF16)
    lane = lax.broadcasted_iota(jnp.int32, (SEQ_LEN, TOK), 1)
    grad_queries, grad_keys, grad_values = [], [], []
    for k in range(2):
        key_head, value_head = key[:, k * 64 : k * 64 + 64], value[:, k * 64 : k * 64 + 64]
        key_terms, value_terms = ([], []), ([], [])
        for g in range(2):
            head = k * 2 + g
            query_head = query[:, head * 64 : head * 64 + 64]
            grad_head = grad_heads[:, head * 64 : head * 64 + 64]
            log_sum = jnp.sum(jnp.where(lane == head, sums[...], 0.0), axis=-1, keepdims=True)
            halves = []
            for part in range(2):
                start, keys = part * 256, part * 256 + 256
                query_part = query_head[start : start + 256]
                grad_part = grad_head[start : start + 256]
                scores = causal_scores(query_part, key_head[:keys], start)
                probs = jnp.exp(scores - log_sum[start : start + 256])
                grad_probs = by_columns(grad_part, value_head[:keys])
                inner = jnp.sum(probs * grad_probs, axis=-1, keepdims=True)
                grad_scores = (probs * (grad_probs - inner)).astype(BF16)
                value_terms[part].append(by_rows(probs.astype(BF16), grad_part))
                key_terms[part].append(by_rows(grad_scores, query_part))
                halves.append(
                    jnp.dot(grad_scores, key_head[:keys], preferred_element_type=F32)
                )
            grad_queries.append(jnp.concatenate(halves, axis=0) * (1.0 / HEAD_SIZE))
        grad_key, grad_value = (
            jnp.concatenate(
                [
                    terms[0][0] + terms[0][1] + terms[1][0][:256] + terms[1][1][:256],
                    terms[1][0][256:] + terms[1][1][256:],
                ],
                axis=0,
            )
            for terms in (key_terms, value_terms)
        )
        grad_keys.append(grad_key * (1.0 / HEAD_SIZE))
        grad_values.append(grad_value)

    def unturn(pair):
        values = jnp.concatenate(pair, axis=1).astype(BF16).astype(F32)
        return (values * cosine[...] - half_turn(values) * sine[...]).astype(BF16)

    projected = jnp.concatenate(
        [
            unturn(grad_queries[:2]),
            unturn(grad_queries[2:]),
            unturn(grad_keys),
            jnp.concatenate(grad_values, axis=1).astype(BF16),
        ],
        axis=1,
    )
    parts[...] = by_columns(projected, heads_w[:, 0:512]).astype(BF16).reshape(2, 2, TOK, MODEL_WIDTH)
    second = [
        sender.start(parts.at[1 - yl, 1 - core], arriving.at[0], sibling),
        sender.start(parts.at[yl, 1 - core], arriving.at[1], sibling),
    ]
    arrived(second[:1])
    outgoing[...] = gather_sums([parts[1 - yl, core], arriving[0]]).astype(BF16)
    third = sender.start(outgoing, incoming, near)
    term = by_rows(normed[...], projected).astype(BF16)
    heads[...] = term.reshape(2, 4, 4, 32, 512)
    upper, lower = pl.ds(0, 16), pl.ds(16, 16)
    heads_first = []
    for k in range(3):
        partner = along_x[k]
        source = heads.at[:, partner[1], :, upper]
        heads_first.append(sender.start(source, upper_in.at[k], partner))
        partner = along_z[k]
        source = heads.at[:, :, partner[2], lower]
        heads_first.append(sender.start(source, lower_in.at[k], partner))
    for copy in fetched[15:17]:
        copy.wait()
    arrived(circling)
    for y in range(2):
        for k in range(3):
            if k == 0:
                pieces = [gate_x[j, y] for j in range(3)]
            else:
                pieces = [experts_x[j, k - 1, y] for j in range(3)]
            total = gather_sums([experts_own[k, y]] + pieces).astype(BF16)
            experts[y, :, :, k * 512 : k * 512 + 512] = total.reshape(4, 32, FF)
    experts_second = [
        sender.start(experts.at[partner[0], partner[2]], experts_plane.at[yh, z], partner)
        for partner in plane_z
    ]
    arrived(around)
    mine = branch_block(z)[...]
    branch_out[...] = gather_sums([mine] + [branch_z[k] for k in range(3)]).astype(BF16)
    across = [
        sender.start(branch_out.at[partner[0] * 4 + partner[1]], branch_plane.at[k], partner)
        for k, partner in enumerate(plane)
    ]
    arrived(second[1:])
    paired[...] = gather_sums([parts[yl, core], arriving[1]])
    arrived([third])
    total = paired[...] + incoming[...].astype(F32)
    fetched[18].wait()
    values = own_tokens[...].astype(F32)
    factor = lax.rsqrt(jnp.mean(values * values, axis=-1, keepdims=True) + EPSILON)
    gain_one = jnp.sum(total * values * factor, axis=0, keepdims=True)
    scaled = total * gain_first
    mean_term = jnp.mean(scaled * values, axis=-1, keepdims=True)
    grad_input[...] = (
        grad_middle[...] + factor * scaled - values * factor * factor * factor * mean_term
    ).astype(BF16)
    gain_terms = jnp.concatenate(
        [gain_one, gain_two, jnp.zeros((TOK - 2, MODEL_WIDTH), F32)], axis=0
    )
    gains[...] = gain_terms.T.astype(BF16).reshape(2, 4, 4, 32, TOK)
    gains_first = [
        sender.start(gains.at[:, partner[1]], gains_in.at[k], partner)
        for k, partner in enumerate(along_x)
    ]
    arrived(heads_first)
    for y in range(2):
        for j in range(4):
            upper_out[y, j] = gather_sums(
                [heads[y, x, j, 0:16]] + [upper_in[k, y, j] for k in range(3)]
            ).astype(BF16)
            lower_out[y, j] = gather_sums(
                [heads[y, j, z, 16:32]] + [lower_in[k, y, j] for k in range(3)]
            ).astype(BF16)
    heads_second = []
    for k in range(7):
        partner = plane_z[k]
        source = upper_out.at[partner[0], partner[2]]
        heads_second.append(sender.start(source, upper_plane.at[k], partner))
        partner = plane[k]
        source = lower_out.at[partner[0], partner[1]]
        heads_second.append(sender.start(source, lower_plane.at[k], partner))
    arrived(gains_first)
    for y in range(2):
        for j in range(4):
            gains_out[y, j] = gather_sums(
                [gains[y, x, j]] + [gains_in[k, y, j] for k in range(3)]
            ).astype(BF16)
    gains_second = [
        sender.start(gains_out.at[partner[0], partner[2]], gains_plane.at[k], partner)
        for k, partner in enumerate(plane_z)
    ]
    arrived(across)
    branch_sum[...] = gather_sums(
        [branch_out[yh * 4 + x]] + [branch_plane[k] for k in range(7)]
    ).astype(BF16)
    place_of = branch_four.at[slot]

    def branch_copy(k):
        return pltpu.make_async_remote_copy(
            src_ref=branch_sum,
            dst_ref=place_of,
            send_sem=branch_sends.at[k],
            recv_sem=branch_recvs.at[slot],
            device_id=(owner // 16, owner // 4 % 4, owner % 4, k),
            device_id_type=BY_ID,
        )

    for k in range(4):
        self_copy = jnp.logical_and(here, seq == k)

        @pl.when(jnp.logical_not(self_copy))
        def _():
            branch_copy(k).start()

        @pl.when(self_copy)
        def _():
            pltpu.make_async_copy(branch_sum, place_of, branch_recvs.at[slot]).start()

    arrived(experts_second)
    for j in range(4):

        @pl.when(z == j)
        def _():
            experts_sum[j] = gather_sums([experts[yh, j], experts_plane[1 - yh, j]]).astype(BF16)

        @pl.when(z != j)
        def _():
            experts_sum[j] = gather_sums([experts_plane[0, j], experts_plane[1, j]]).astype(BF16)

    experts_shared = [
        sender.start(experts_sum, experts_four.at[yl, core], partner) for partner in (near, sibling)
    ]
    kept = [pltpu.make_async_copy(experts_sum, experts_four.at[yl, core], local.at[20])]
    kept[0].start()
    arrived(heads_second)
    heads_sum[0:16, 0:512] = gather_sums(
        [upper_out[yh, z]] + [upper_plane[k] for k in range(7)]
    ).astype(BF16)
    heads_sum[16:32, 0:512] = gather_sums(
        [lower_out[yh, x]] + [lower_plane[k] for k in range(7)]
    ).astype(BF16)
    arrived(gains_second)
    heads_sum[:, 512:640] = gather_sums(
        [gains_out[yh, z]] + [gains_plane[k] for k in range(7)]
    ).astype(BF16)
    heads_shared = [
        sender.start(heads_sum, heads_four.at[yl, core], partner) for partner in (near, sibling)
    ]
    kept.append(pltpu.make_async_copy(heads_sum, heads_four.at[yl, core], local.at[19]))
    kept[-1].start()
    fetched[14].wait()
    fetched[17].wait()
    arrived(row_copies)
    mixed = middle[...]
    dots = jnp.zeros((TOK, TOK), F32)
    lane = lax.broadcasted_iota(jnp.int32, (TOK, TOK), 1)
    for e in range(EXPERTS):
        mixed += jnp.dot(shares[e], returned_all[e], preferred_element_type=F32)
        found = by_columns(out_tokens[...], returned_all[e]) * hits[e].astype(F32)
        dots = jnp.where(lane == e, jnp.sum(found, axis=-1, keepdims=True), dots)
    layer_out[...] = mixed.astype(BF16)
    pair_dots[...] = dots * RESIDUAL
    arrived(heads_shared[:1])
    far = heads_four.at[1 - yl, core]
    ending = [sender.start(far, far, sibling)]
    arrived(experts_shared[:1])
    far = experts_four.at[1 - yl, core]
    ending.append(sender.start(far, far, sibling))
    arrived(heads_shared[1:])
    arrived(experts_shared[1:])
    for copy in kept:
        copy.wait()
    arrived(ending)
    for k in range(4):
        pltpu.make_async_copy(branch_sum, branch_four.at[k], branch_recvs.at[k]).wait()
        self_copy = jnp.logical_and(here, seq == k)

        @pl.when(jnp.logical_not(self_copy))
        def _():
            branch_copy(k).wait_send()

    sender.finish()


def gather_sums(parts):
    total = parts[0].astype(F32)
    for part in parts[1:]:
        total = total + part.astype(F32)
    return total


def unpack_kernel(
    heads_in, branch_in, experts_in, layer_in, grad_in, dots_in, routes,
    query, key, value, output, gate, up, down, layer_out, grad_input, gates, gain_one, gain_two,
    heads, branch, experts, dots, local,
):
    copies = local_starts(
        [
            (heads_in, heads), (branch_in, branch), (dots_in, dots),
            (layer_in, layer_out), (grad_in, grad_input),
        ]
        + [(experts_in.at[s // 2, s % 2], experts.at[s]) for s in range(4)],
        local,
    )
    for copy in copies[:3]:
        copy.wait()
    gains = jnp.zeros((32, TOK), F32)
    for s in range(4):
        block = heads[s // 2, s % 2].astype(F32)
        query[:, s * 256 : s * 256 + 256] = block[:, :256]
        key[:, s * 128 : s * 128 + 128] = block[:, 256:384]
        value[:, s * 128 : s * 128 + 128] = block[:, 384:512]
        gains += block[:, 512:640]
        rows, columns = s // 2 * 16, s % 2 * 512
        output[rows : rows + 16, columns : columns + 512] = branch[s].astype(F32)
    gains = gains.T
    gain_one[...] = gains[0:1]
    gain_two[...] = gains[1:2]
    by_expert = dots[...].T[0:EXPERTS]
    index = lax.broadcasted_iota(jnp.int32, (EXPERTS, TOK), 0)
    for k in range(TOP):
        picked = jnp.where(index == routes[k : k + 1, :], by_expert, 0.0)
        gates[k : k + 1, :] = jnp.sum(picked, axis=0, keepdims=True)
    for s in range(4):
        copies[5 + s].wait()
        for j in range(4):
            block = experts[s, j].astype(F32)
            for index, result in enumerate((gate, up, down)):
                result[:, j * 4 + s, :] = block[:, index * 512 : index * 512 + 512]
    for copy in copies[3:5]:
        copy.wait()


def expert_kernel(
    rows_all, picks_in, back_in, own_w, weights_all,
    grad_rows, returned_out, expert_grads_out, gate_x,
    picks, back, returned, expert_grads,
    rows_here, weights, outgoing, chosen, active, by_gate, by_up, send, recv, local,
):
    yh, x, z, seq = place()
    expert = z * 4 + seq
    turns = (2, 1, 3, 0)
    offsets = [(turn, k) for turn in turns for k in range(4) if turn + k > 0]
    partners = [(yh, x, (z + turn) % 4, (seq + k) % 4) for turn, k in offsets]
    fetches = local_starts(
        [
            (weights_all.at[:, :, (x + k) % 4], weights.at[:, :, (x + k) % 4])
            for k in (1, 2, 3)
        ]
        + [(own_w, weights.at[:, :, x])]
        + [(rows_all.at[(z + turn) % 4], rows_here.at[turn]) for turn in turns]
        + [(picks_in, picks), (back_in, back)],
        local,
    )
    along_x = [(yh, (x + k) % 4, z, seq) for k in (1, 2, 3)]
    greet(partners + along_x)
    sender = Sender(send, recv)
    for copy in fetches[:4] + fetches[8:]:
        copy.wait()
    gate_w, up_w, down_w = (weights[k].reshape(MODEL_WIDTH, FF) for k in range(3))
    for index, turn in enumerate(turns):
        fetches[4 + index].wait()
        first = (z + turn) % 4 * 4
        rows = jnp.concatenate(
            [
                jnp.dot(picks[first + j], rows_here[turn, j], preferred_element_type=F32)
                for j in range(4)
            ],
            axis=0,
        ).astype(BF16)
        span = pl.ds(index * 288, 288)
        chosen[span, :] = rows
        gate_pre = jnp.dot(rows, gate_w, preferred_element_type=F32)
        up_pre = jnp.dot(rows, up_w, preferred_element_type=F32)
        back_rows = back[pl.ds(pl.multiple_of(first * CAP, 288), 288), :]
        grad_active = jnp.dot(back_rows, down_w, preferred_element_type=F32)
        sigmoid_gate = jax.nn.sigmoid(gate_pre)
        silu = gate_pre * sigmoid_gate
        slope = sigmoid_gate * (1.0 + gate_pre * (1.0 - sigmoid_gate))
        grad_gate = (grad_active * up_pre * slope).astype(BF16)
        grad_up = (grad_active * silu).astype(BF16)
        by_gate[span, :] = grad_gate
        by_up[span, :] = grad_up
        active[span, :] = (silu * up_pre).astype(BF16)
        result = by_columns(grad_gate, gate_w) + by_columns(grad_up, up_w)
        for j in range(4):
            outgoing[first + j] = result[j * CAP : j * CAP + CAP].astype(BF16)
        for partner, offset in zip(partners, offsets):
            if offset[0] == turn:
                block = partner[2] * 4 + partner[3]
                sender.start(outgoing.at[block], grad_rows.at[expert], partner)
    kept = [pltpu.make_async_copy(outgoing.at[expert], grad_rows.at[expert], local.at[10])]
    kept[0].start()
    def grads_of(index, left, right):
        for part in range(2):
            total = by_rows(left[:, part * 512 : part * 512 + 512], right[...])
            expert_grads[index, :, part] = total.astype(BF16).reshape(4, TOK, FF)

    grads_of(0, chosen, by_gate)
    for k, partner in enumerate(along_x):
        sender.start(expert_grads.at[0, partner[1]], gate_x.at[k], partner)
    for index, turn in enumerate(turns):
        first = (z + turn) % 4 * 4
        result = by_columns(active[pl.ds(index * 288, 288), :], down_w)
        for j in range(4):
            returned[first + j] = result[j * CAP : j * CAP + CAP].astype(BF16)
    kept.append(pltpu.make_async_copy(returned, returned_out, local.at[11]))
    kept[-1].start()
    grads_of(1, chosen, by_up)
    for part in range(2):
        total = 0.0
        for index, turn in enumerate(turns):
            start = pl.multiple_of((z + turn) % 4 * 288, 288)
            total += by_rows(
                back[pl.ds(start, 288), pl.ds(part * 512, 512)],
                active[pl.ds(index * 288, 288), :],
            )
        expert_grads[2, :, part] = total.astype(BF16).reshape(4, TOK, FF)
    kept.append(pltpu.make_async_copy(expert_grads, expert_grads_out, local.at[12]))
    kept[-1].start()
    for copy in kept:
        copy.wait()
    arrived(sender.copies)
    sender.finish()


def shards(
    layer_in, norm_one, w_query, key_weight, value_weight, w_output, norm_two,
    w_gate, w_up, w_down, routes, route_gates, cotangent,
):
    key_value_resident = KEY_VALUE_HEADS // 4
    group_width = QUERY_HEADS // KEY_VALUE_HEADS
    head_width = key_value_resident * group_width * HEAD_SIZE
    kv_width = key_value_resident * HEAD_SIZE

    cosine, sine = jnp.asarray(COSINE), jnp.asarray(SINE)
    hbm, vmem = pl.BlockSpec(memory_space=pltpu.HBM), pl.BlockSpec(memory_space=pltpu.VMEM)
    block = (TOK, MODEL_WIDTH)

    def arrays(*entries):
        return tuple(jax.ShapeDtypeStruct(shape, kind) for shape, kind in entries)

    def buffers(*entries):
        return [pltpu.VMEM(shape, kind) for shape, kind in entries]

    kept_arrays = (
        ((SEQ_LEN, MODEL_WIDTH), BF16),
        ((SEQ_LEN, head_width), BF16),
        ((SEQ_LEN, kv_width), BF16),
        ((SEQ_LEN, kv_width), BF16),
        ((SEQ_LEN, head_width), BF16),
        ((SEQ_LEN, TOK), F32),
        (block, F32),
        ((EXPERTS, CAP, TOK), BF16),
        ((SLOTS, MODEL_WIDTH), BF16),
        ((EXPERTS, TOK, CAP), BF16),
        ((EXPERTS, TOK, CAP), BF16),
    )
    table = ((SEQ_LEN, TOK), F32)
    heads_array = ((MODEL_WIDTH, 640), BF16)
    (
        normed_all, query_all, key_all, value_all, attended, sums, middle, picks, grad_back,
        hits, shares, rows_all, weights_here, weights_all, heads_w, branch_w, gains,
    ) = pl.pallas_call(
        forward_kernel,
        out_shape=arrays(
            *kept_arrays,
            ((4, 2, 2) + block, BF16),
            ((3, 2, 4, 32, FF), BF16),
            ((3, 2, 4, 4, 32, FF), BF16),
            ((2, 4, 4, 32, 640), BF16),
            ((2, 2, 4, 4, 32, 512), BF16),
            ((8, MODEL_WIDTH), F32),
        ),
        in_specs=[hbm] * 11 + [vmem] * 4,
        out_specs=(hbm,) * 16 + (vmem,),
        scratch_shapes=buffers(
            ((EXPERTS, 8, TOK), F32),
            ((32, 640), BF16),
            ((3, 512, FF), BF16),
            ((4, 3, 32, FF), BF16),
            ((2, 4, 4, 32, 640), BF16),
            ((2, 2, 4, 4, 32, 512), BF16),
            ((2, 2) + block, BF16),
            table,
            table,
            ((EXPERTS, 8, TOK), F32),
            ((4, 2, 2) + block, BF16),
            *kept_arrays,
            ((4, TOK, head_width), BF16),
            (block, BF16),
        )
        + [
            pltpu.SemaphoreType.DMA((89,)),
            pltpu.SemaphoreType.DMA((89,)),
            pltpu.SemaphoreType.DMA((28,)),
        ],
        compiler_params=pltpu.CompilerParams(
            collective_id=7, has_side_effects=True, vmem_limit_bytes=60 * 2**20
        ),
        name="forward",
    )(
        w_query,
        key_weight,
        value_weight,
        w_output,
        layer_in,
        w_gate.reshape(512, FF),
        w_up.reshape(512, FF),
        w_down.reshape(512, FF),
        cosine,
        sine,
        cotangent,
        norm_one.reshape(1, 32),
        norm_two.reshape(1, 32),
        routes.T,
        route_gates.T,
    )
    heads_w = heads_w.reshape(MODEL_WIDTH, 640)
    branch_w = branch_w.reshape(2, MODEL_WIDTH, 512)
    weights_here = weights_here.reshape(3, 2, TOK, FF)
    weights_all = weights_all.reshape(3, 2, 4, TOK, FF)

    returned_array = ((EXPERTS, CAP, MODEL_WIDTH), BF16)
    grads_array = ((3, 4, 2, TOK, FF), BF16)
    gate_array = ((3, 2, TOK, FF), BF16)
    grad_rows, returned, expert_grads, gate_x = pl.pallas_call(
        expert_kernel,
        out_shape=arrays(returned_array, returned_array, grads_array, gate_array),
        in_specs=[hbm] * 5,
        out_specs=(hbm,) * 4,
        scratch_shapes=buffers(
            ((EXPERTS, CAP, TOK), BF16), ((SLOTS, MODEL_WIDTH), BF16), returned_array, grads_array
        )
        + [
            pltpu.VMEM((4, 4) + block, BF16),
            pltpu.VMEM((3, 2, 4, TOK, FF), BF16),
            pltpu.VMEM((EXPERTS, CAP, MODEL_WIDTH), BF16),
            pltpu.VMEM((SLOTS, MODEL_WIDTH), BF16),
            pltpu.VMEM((SLOTS, FF), BF16),
            pltpu.VMEM((SLOTS, FF), BF16),
            pltpu.VMEM((SLOTS, FF), BF16),
            pltpu.SemaphoreType.DMA((18,)),
            pltpu.SemaphoreType.DMA((18,)),
            pltpu.SemaphoreType.DMA((13,)),
        ],
        compiler_params=pltpu.CompilerParams(
            collective_id=5, has_side_effects=True, vmem_limit_bytes=60 * 2**20
        ),
        name="experts",
    )(rows_all.reshape((4, 4) + block), picks, grad_back, weights_here, weights_all)
    layer_out, grad_input, pair_dots, heads_four, branch_four, expert_four = pl.pallas_call(
        backward_kernel,
        out_shape=arrays(
            (block, BF16),
            (block, BF16),
            ((TOK, TOK), F32),
            ((2, 2, 32, 640), BF16),
            ((4, 16, 512), BF16),
            ((2, 2, 4, 32, 3 * FF), BF16),
        ),
        in_specs=[hbm] * 19 + [vmem],
        out_specs=(vmem,) * 3 + (hbm,) * 3,
        scratch_shapes=buffers(
            ((SEQ_LEN, head_width), BF16),
            ((SEQ_LEN, head_width), BF16),
            ((SEQ_LEN, kv_width), BF16),
            ((SEQ_LEN, kv_width), BF16),
            table,
            ((SEQ_LEN, MODEL_WIDTH), BF16),
            heads_array,
            table,
            table,
            gate_array,
            returned_array,
            ((EXPERTS, TOK, CAP), BF16),
            ((EXPERTS, TOK, CAP), BF16),
            (block, F32),
            (block, BF16),
            (block, BF16),
            returned_array,
            (block, BF16),
            (block, F32),
            ((3, 2, TOK, FF), BF16),
            ((3, 2, 2, TOK, FF), BF16),
        )
        + [
            pltpu.VMEM((2, 256, 512), BF16),
            pltpu.VMEM((2, 2) + block, BF16),
            pltpu.VMEM((8, 2, 16, MODEL_WIDTH), BF16),
            pltpu.VMEM((2, 2) + block, BF16),
            pltpu.VMEM((2,) + block, BF16),
            pltpu.VMEM(block, F32),
            pltpu.VMEM(block, BF16),
            pltpu.VMEM(block, BF16),
            pltpu.VMEM((3, 8, 16, 512), BF16),
            pltpu.VMEM((8, 16, 512), BF16),
            pltpu.VMEM((7, 16, 512), BF16),
        ]
        + buffers(
            ((2, 4, 4, 32, 512), BF16),
            ((3, 2, 4, 16, 512), BF16),
            ((3, 2, 4, 16, 512), BF16),
            ((2, 4, 16, 512), BF16),
            ((2, 4, 16, 512), BF16),
            ((7, 16, 512), BF16),
            ((7, 16, 512), BF16),
            ((2, 4, 4, 32, TOK), BF16),
            ((3, 2, 4, 32, TOK), BF16),
            ((2, 4, 32, TOK), BF16),
            ((7, 32, TOK), BF16),
            ((2, 4, 32, 3 * FF), BF16),
            ((2, 4, 32, 3 * FF), BF16),
            ((32, 640), BF16),
            ((16, 512), BF16),
            ((4, 32, 3 * FF), BF16),
        )
        + [
            pltpu.SemaphoreType.DMA((77,)),
            pltpu.SemaphoreType.DMA((77,)),
            pltpu.SemaphoreType.DMA((21,)),
            pltpu.SemaphoreType.DMA((4,)),
            pltpu.SemaphoreType.DMA((4,)),
        ],
        compiler_params=pltpu.CompilerParams(
            collective_id=6, has_side_effects=True, vmem_limit_bytes=60 * 2**20
        ),
        name="backward",
    )(
        returned,
        branch_w,
        attended,
        query_all,
        key_all,
        value_all,
        sums,
        normed_all,
        heads_w,
        cosine,
        sine,
        expert_grads,
        gate_x,
        grad_rows,
        hits,
        shares,
        middle,
        cotangent,
        layer_in,
        gains,
    )
    (
        grad_query_proj, grad_key_proj, grad_value_proj, grad_output_proj,
        grad_gate_proj, grad_up_proj, grad_down_proj, layer_out, grad_input,
        grad_gates, grad_norm_one, grad_norm_two,
    ) = pl.pallas_call(
        unpack_kernel,
        out_shape=arrays(
            ((32, 1024), F32),
            ((32, 512), F32),
            ((32, 512), F32),
            ((32, 1024), F32),
            ((32, EXPERTS, FF), F32),
            ((32, EXPERTS, FF), F32),
            ((32, EXPERTS, FF), F32),
            (block, BF16),
            (block, BF16),
            ((TOP, TOK), F32),
            ((1, 32), F32),
            ((1, 32), F32),
        ),
        in_specs=[hbm] * 6 + [vmem],
        out_specs=(vmem,) * 12,
        scratch_shapes=buffers(
            ((2, 2, 32, 640), BF16),
            ((4, 16, 512), BF16),
            ((4, 4, 32, 3 * FF), BF16),
            ((TOK, TOK), F32),
        )
        + [pltpu.SemaphoreType.DMA((9,))],
        compiler_params=pltpu.CompilerParams(vmem_limit_bytes=60 * 2**20),
        name="unpack",
    )(heads_four, branch_four, expert_four, layer_out, grad_input, pair_dots, routes.T)
    return (
        layer_out,
        grad_input,
        grad_norm_one.reshape(32),
        grad_query_proj,
        grad_key_proj,
        grad_value_proj,
        grad_output_proj,
        grad_norm_two.reshape(32),
        grad_gate_proj,
        grad_up_proj,
        grad_down_proj,
        grad_gates.T,
    )


def solution(mesh):
    dp = ("yh", "x", "z")
    cut = Mesh(mesh.devices.reshape(2, 4, 4, 4), AXES)
    tokens, rows, gain, experts = P(AXES, None), P(dp, None), P(dp), P(dp, None, None)
    return jax.shard_map(
        shards,
        mesh=cut,
        in_specs=(
            tokens, gain, rows, rows, rows, rows, gain, experts, experts, experts,
            tokens, tokens, tokens,
        ),
        out_specs=(
            tokens, tokens, gain, rows, rows, rows, rows, gain, experts, experts, experts, tokens,
        ),
        check_vma=False,
    )
```
